32 devices in a mesh: wide: 8 (over z, x), seq: 4 (over y, core).
Axes of the slice: x: 2, y: 2, z: 4, core: 2. Of those that a mesh axis runs over, the one named last changes fastest.
Arguments:
- tokens: bfloat16 [16, 1024, 768], P('wide', 'seq'), may hold values from -6 to 6
- condition: float32 [16, 128], P('wide'), may hold values from -6 to 6
- cotangent: bfloat16 [16, 1024, 768], P('wide', 'seq'), may hold values from -6 to 6
- adaptive: bfloat16 [128, 4608], replicated, may hold values from -0.5 to 0.5
- shifts: float32 [4608], replicated, may hold values from -3 to 3
- prenorm: float32 [768], replicated, may hold values from 0.5 to 1.5
- mixer: bfloat16 [768, 2304], replicated, may hold values from -0.21875 to 0.21875
- projection: bfloat16 [768, 768], replicated, may hold values from -1.25 to 1.25
- postnorm: float32 [768], replicated, may hold values from 0.5 to 1.5
- expand: bfloat16 [768, 3072], replicated, may hold values from -0.21875 to 0.21875
- offsets: float32 [3072], replicated, may hold values from -3 to 3
- contract: bfloat16 [3072, 768], replicated, may hold values from -0.109375 to 0.109375
- baseline: float32 [768], replicated, may hold values from -3 to 3
Outputs:
- layer_output: bfloat16 [16, 1024, 768], P('wide', 'seq')
- grad_tokens: bfloat16 [16, 1024, 768], P('wide', 'seq')
- grad_time: float32 [16, 128], P('wide')
- grad_adaptive: float32 [128, 4608], P('wide')
- grad_shifts: float32 [4608], P('wide')
- grad_prenorm: float32 [768], P('wide')
- grad_mixer: float32 [768, 2304], P('wide')
- grad_projection: float32 [768, 768], P('wide')
- grad_postnorm: float32 [768], P('wide')
- grad_expand: float32 [768, 3072], P('wide')
- grad_offsets: float32 [3072], P('wide')
- grad_contract: float32 [3072, 768], P('wide')
- grad_baseline: float32 [768], P('wide')
The draws below stay inside these ranges and needn't reach their ends.
All inputs are finite; a program needn't handle non-finite values.
Results may differ from the reference program's by a relative error of at most 0.014.
The reference program's roundings to bfloat16 on the way count: a program that leaves them out, or rounds other values in their place, can miss the bound.
Values may be sent and summed in bfloat16 or wider, within the bound.
A program may use at most 192 MiB of HBM per device.

```python
import math
import jax
import jax.numpy as jnp
from jax import lax

D = 768
HEADS = 12
HDIM = 64
FF = 3072
COND = 128
LENGTH = 1024
ROWS = 16


def steps_of(rng, extent, cuts, low, high):
    def one(dim, blocks):
        draws = jax.random.uniform(jax.random.fold_in(jax.random.fold_in(rng, 6), dim), (blocks,), jnp.float32, low / len(cuts), high / len(cuts))
        return jnp.repeat(jnp.exp(draws), extent[dim] // blocks).reshape((-1,) + (1,) * (len(extent) - dim - 1))

    level = one(*cuts[0])
    for cut in cuts[1:]:
        level = level * one(*cut)
    return level


def gaussian(key, dims, spread, most, cuts=(), kind=jnp.bfloat16):
    array = jax.random.normal(key, dims, jnp.float32) * spread
    if len(cuts) > 0:
        array = steps_of(key, dims, cuts, -0.22, 0.18) * array
    return jnp.clip(array, min=-most, max=most).astype(kind)


def setup_inputs(seed: int = 0) -> dict:
    key_of = jax.random.split(jax.random.key(seed), 14)
    return {
        "tokens": gaussian(key_of[0], (ROWS, LENGTH, D), 1.0, 6.0, ((0, 8), (1, 4))),
        "condition": gaussian(key_of[1], (ROWS, COND), 1.0, 6.0, ((0, 8),), jnp.float32),
        "cotangent": gaussian(key_of[2], (ROWS, LENGTH, D), 1.0, 6.0, ((0, 8), (1, 4))),
        "adaptive": gaussian(key_of[3], (COND, 6 * D), COND ** -0.5, 0.5),
        "shifts": gaussian(key_of[4], (6 * D,), 0.5, 3.0, (), jnp.float32),
        "prenorm": jnp.clip(1.0 + 0.1 * jax.random.normal(key_of[5], (D,), jnp.float32), 0.5, 1.5),
        "mixer": gaussian(key_of[6], (D, 3 * D), D ** -0.5, 0.21875),
        "projection": gaussian(key_of[7], (D, D), (D // 32) ** -0.5, 1.25),
        "postnorm": jnp.clip(1.0 + 0.1 * jax.random.normal(key_of[8], (D,), jnp.float32), 0.5, 1.5),
        "expand": gaussian(key_of[9], (D, FF), D ** -0.5, 0.21875),
        "offsets": gaussian(key_of[10], (FF,), 0.5, 3.0, (), jnp.float32),
        "contract": gaussian(key_of[11], (FF, D), FF ** -0.5, 0.109375),
        "baseline": gaussian(key_of[12], (D,), 0.5, 3.0, (), jnp.float32),
    }


@jax.custom_vjp
def low(v):
    return lax.optimization_barrier(v.astype(jnp.bfloat16)).astype(jnp.float32)

@jax.custom_vjp
def low_back(v):
    return v

def low_keep(v):
    return (low(v), None)

def low_pass(kept, grad):
    return (grad,)

def back_keep(v):
    return (v, None)

def back_low(kept, grad):
    return (low(grad),)
low.defvjp(low_keep, low_pass)
low_back.defvjp(back_keep, back_low)
epsilon = 1e-06

def layer_norm(values):
    center = values - lax.optimization_barrier(jnp.mean(values, axis=-1, keepdims=True))
    return center * lax.rsqrt(lax.optimization_barrier(jnp.mean(center * center, axis=-1, keepdims=True)) + epsilon)

def rotary_tables(positions):
    half_dim = HDIM // 2
    frequency = jnp.exp(jnp.arange(half_dim, dtype=jnp.float32) * (-2.0 * math.log(10000.0) / HDIM))
    angles = positions.astype(jnp.float32)[:, None] * frequency[None, :]
    cosines = jnp.concatenate([jnp.cos(angles), jnp.cos(angles)], axis=-1)
    sines = jnp.concatenate([jnp.sin(angles), jnp.sin(angles)], axis=-1)
    return (cosines, sines)

def rotate(values, cosines, sines):
    shaped = values.reshape(values.shape[:-1] + (HEADS, HDIM))
    half_dim = HDIM // 2
    turned = jnp.concatenate([-shaped[..., half_dim:], shaped[..., :half_dim]], axis=-1)
    result = shaped * cosines[..., None, :] + turned * sines[..., None, :]
    return result.reshape(values.shape)

def layer_row(inputs, cond, weight_set):
    adaptive, shifts, prenorm, mixer, projection, postnorm, expand, offsets, contract, baseline = weight_set
    highest = lax.Precision.HIGHEST
    modulation = jnp.dot(jax.nn.silu(cond)[None, :], adaptive, precision=highest)[0] + shifts
    shift_attend, scale_attend, gate_attend, shift_feed, scale_feed, gate_feed = jnp.split(modulation, 6)
    hidden_attend = low(layer_norm(inputs) * prenorm * (1.0 + scale_attend) + shift_attend)
    mixed = low_back(jnp.dot(hidden_attend, mixer, precision=highest))
    cosines, sines = rotary_tables(jnp.arange(LENGTH, dtype=jnp.int32))
    queries = low(rotate(mixed[:, :D], cosines, sines)).reshape(LENGTH, HEADS, HDIM)
    key_rows = low(rotate(mixed[:, D:2 * D], cosines, sines)).reshape(LENGTH, HEADS, HDIM)
    value_rows = low(mixed[:, 2 * D:]).reshape(LENGTH, HEADS, HDIM)
    raw_scores = jnp.einsum('qhd,khd->hqk', queries, key_rows, precision=highest)
    scores = low_back(raw_scores * HDIM ** (-0.5))
    weights_low = low(jax.nn.softmax(scores, axis=-1))
    attended = jnp.einsum('hqk,khd->qhd', weights_low, value_rows, precision=highest)
    attended_low = low(low_back(attended)).reshape(LENGTH, D)
    branch = low_back(jnp.dot(attended_low, projection, precision=highest))
    middle = inputs + gate_attend * branch
    hidden_feed = low(layer_norm(middle) * postnorm * (1.0 + scale_feed) + shift_feed)
    widened = low_back(jnp.dot(hidden_feed, expand, precision=highest) + offsets)
    activated = low(jax.nn.gelu(widened, approximate=True))
    narrowed = low_back(jnp.dot(activated, contract, precision=highest) + baseline)
    return middle + gate_feed * narrowed

def reference(tokens, condition, cotangent, adaptive, shifts, prenorm, mixer, projection, postnorm, expand, offsets, contract, baseline):
    weight_set = tuple((element.astype(jnp.float32) for element in (adaptive, shifts, prenorm, mixer, projection, postnorm, expand, offsets, contract, baseline)))

    def whole(inputs, cond, weights_all):

        def per_row(row_pair):
            return jax.checkpoint(layer_row)(row_pair[0], row_pair[1], weights_all)
        return lax.map(per_row, (inputs, cond))
    output, pullback = jax.vjp(whole, tokens.astype(jnp.float32), condition.astype(jnp.float32), weight_set)
    grad_inputs, grad_cond, grad_weights = pullback(cotangent.astype(jnp.float32))
    return (output.astype(jnp.bfloat16), grad_inputs.astype(jnp.bfloat16), grad_cond, grad_weights[0], grad_weights[1], grad_weights[2], grad_weights[3], grad_weights[4], grad_weights[5], grad_weights[6], grad_weights[7], grad_weights[8], grad_weights[9])
```

```python
import functools
import math

import jax
import jax.numpy as jnp
import numpy as np
from jax import lax
from jax.experimental import pallas as pl
from jax.experimental.pallas import tpu as pltpu
from jax.sharding import PartitionSpec as P

F32 = jnp.float32
BF16 = jnp.bfloat16
MESH = pl.DeviceIdType.MESH
HDIM = 64
PAIR = 2 * HDIM
EPSILON = 1e-06
GELU_A = 0.7978845608
GELU_B = 0.044715

ROWS_BY_ROWS = (((1,), (1,)), ((), ()))
COLS_BY_COLS = (((0,), (0,)), ((), ()))


def dot(a, b, dims=None):
    if dims is None:
        return jnp.dot(a, b, preferred_element_type=F32)
    return lax.dot_general(a, b, dims, preferred_element_type=F32)


def normalize(values):
    center = values - jnp.mean(values, axis=-1, keepdims=True)
    scale = lax.rsqrt(jnp.mean(center * center, axis=-1, keepdims=True) + EPSILON)
    return center * scale, scale


def normalize_back(grad, normal, scale):
    first = jnp.mean(grad, axis=-1, keepdims=True)
    second = jnp.mean(grad * normal, axis=-1, keepdims=True)
    return scale * (grad - first - normal * second)


def turn(values):
    lane = lax.broadcasted_iota(jnp.int32, values.shape, 1)
    first = lax.rem(lane, HDIM) < HDIM // 2
    return jnp.where(
        first, pltpu.roll(values, PAIR - HDIM // 2, 1), pltpu.roll(values, HDIM // 2, 1)
    )


def column_sum(values):
    return jnp.sum(values, axis=0, keepdims=True)


def layer_kernel(
    tok_h, cot_h, adap_h, mix_h, proj_h, exp_h, con_h,
    cond, shifts, prenorm, postnorm, offsets, baseline, cosine, sine,
    out_h, gtok_h, ge_h, gc_h, gp_h, gm_h, vec_h, e_h,
    tok, cot, adap, mix, proj, exp, con, mod, hid_a, qm, kk, vv, v_t, k_t, est, inv_l, att_t, att_s, att,
    branch, middle, hid_f, gnar, gbr, act, gwid, nacc, hacc, nsend, nrecv, hsend, hrecv,
    dom, dsum, dv, dk, dq_t, gmx, ost, ge, gc, gp, gm, vec,
    lsem, esem, ssem, rsem,
):
    span = tok.shape[1]
    width = tok.shape[2]
    total = hid_a.shape[0]
    half = width // 2
    pairs = half // PAIR
    blocks = total // span
    ub = exp.shape[1] // 2
    w = lax.axis_index("wide")
    s = lax.axis_index("seq")
    y = lax.div(s, 2)
    c = lax.rem(s, 2)
    core_dev = (w, y * 2 + 1 - c)
    y_dev = (w, (1 - y) * 2 + c)

    def rows_of(p):
        return pl.ds(pl.multiple_of(p * span, span), span)

    def remote(src, dst, k, dev):
        return pltpu.make_async_remote_copy(
            src_ref=src, dst_ref=dst, send_sem=ssem.at[k], recv_sem=rsem.at[k],
            device_id=dev, device_id_type=MESH,
        )

    def local(src, dst, k):
        return pltpu.make_async_copy(src, dst, lsem.at[k])

    loads = [local(adap_h, adap, 0), local(tok_h.at[y], tok.at[y], 1), local(cot_h.at[y], cot.at[y], 2)]
    mix_loads = []
    for j in range(pairs):
        for b in range(3):
            mix_loads.append(local(
                mix_h.at[:, pl.ds(pl.multiple_of(b * width + c * half + j * PAIR, PAIR), PAIR)],
                mix.at[:, pl.ds((j * 3 + b) * PAIR, PAIR)],
                3 + j * 3 + b,
            ))
    k0 = 3 + 3 * pairs
    proj_load = local(proj_h, proj, k0)
    exp_load = local(exp_h.at[:, pl.ds(pl.multiple_of(c * 2 * ub, PAIR), 2 * ub)], exp, k0 + 1)
    con_load = local(con_h.at[pl.ds(pl.multiple_of(c * 2 * ub, PAIR), 2 * ub), :], con, k0 + 2)
    for item in loads + mix_loads + [proj_load, exp_load, con_load]:
        item.start()

    barrier = pltpu.get_barrier_semaphore()
    for dev in (core_dev, y_dev):
        pl.semaphore_signal(barrier, inc=1, device_id=dev, device_id_type=MESH)
    pl.semaphore_wait(barrier, 2)

    tok_swap = remote(tok_h.at[1 - y], tok.at[y], 0, y_dev)
    cot_swap = remote(cot_h.at[1 - y], cot.at[y], 1, y_dev)
    tok_swap.start()
    cot_swap.start()

    vec[...] = jnp.zeros_like(vec)

    loads[0].wait()
    crow = jnp.where(y == 0, cond[0:1, :], cond[1:2, :])
    crow = crow * (1.0 / (1.0 + jnp.exp(-crow)))
    extent = crow.shape[1]
    eye = lax.broadcasted_iota(jnp.int32, (extent, extent), 0) == lax.broadcasted_iota(
        jnp.int32, (extent, extent), 1
    )
    ccol = jnp.sum(jnp.where(eye, jnp.broadcast_to(crow, (extent, extent)), 0.0), axis=1, keepdims=True)
    for n in range(6):
        part = pl.ds(n * width, width)
        mod[n : n + 1, :] = column_sum(adap[:, part].astype(F32) * ccol) + shifts[:, part]

    def first_norm(j, t):
        normal, _ = normalize(tok[j].astype(F32))
        value = normal * (prenorm[...] * (1.0 + mod[1:2, :])) + mod[0:1, :]
        place = rows_of(2 * j + c)
        hid_a[place, :] = value.astype(BF16)
        push = remote(hid_a.at[place, :], hid_a.at[place, :], 2 + t, core_dev)
        push.start()

    def wait_hid_a(j, t):
        place = rows_of(2 * j + 1 - c)
        remote(hid_a.at[place, :], hid_a.at[place, :], 2 + t, core_dev).wait_recv()

    def project(p):
        place = rows_of(p)
        mixed = dot(hid_a[place, :], mix[...])
        cos_here = cosine[place, :]
        sin_here = sine[place, :]
        lane = lax.broadcasted_iota(jnp.int32, (span, PAIR), 1)
        for j in range(pairs):
            base = j * 3 * PAIR
            query = mixed[:, base : base + PAIR]
            query = (query * cos_here + turn(query) * sin_here).astype(BF16) * jnp.asarray(
                HDIM ** (-0.5), BF16
            )
            zero = jnp.zeros_like(query)
            qm[2 * j, place, :] = jnp.where(lane < HDIM, query, zero)
            qm[2 * j + 1, place, :] = jnp.where(lane < HDIM, zero, query)
            key = mixed[:, base + PAIR : base + 2 * PAIR]
            kk[j, place, :] = (key * cos_here + turn(key) * sin_here).astype(BF16)
            vv[j, place, :] = mixed[:, base + 2 * PAIR : base + 3 * PAIR].astype(BF16)

    loads[1].wait()
    first_norm(y, 0)
    for item in mix_loads:
        item.wait()
    project(2 * y + c)
    tok_swap.wait_recv()
    first_norm(1 - y, 1)
    wait_hid_a(y, 0)
    project(2 * y + 1 - c)
    project(2 * (1 - y) + c)
    wait_hid_a(1 - y, 1)
    project(2 * (1 - y) + 1 - c)
    for j in range(pairs):
        k_t[j * PAIR : (j + 1) * PAIR, :] = kk[j].T
        v_t[j * PAIR : (j + 1) * PAIR, :] = vv[j].T

    loads[2].wait()
    cot_swap.wait_recv()
    for j in range(2):
        place = rows_of(2 * j + c)
        low = (cot[j].astype(F32) * mod[5:6, :]).astype(BF16)
        gnar[place, :] = low
        vec[8:9, :] += column_sum(low.astype(F32))
        remote(gnar.at[place, :], gnar.at[place, :], 4 + j, core_dev).start()

    def e_copy(n, slot):
        return pltpu.make_async_copy(est.at[slot], e_h.at[n], esem.at[slot])

    def attend(j, carry):
        for hh in range(2):
            h = 2 * j + hh
            head = pl.ds(pl.multiple_of(h * HDIM, HDIM), HDIM)
            for qb in range(blocks):
                n = h * blocks + qb
                slot = qb % 2
                part = pl.ds(qb * span, span)
                score = dot(kk[j], qm[h, part, :], ROWS_BY_ROWS)
                top = jnp.max(score, axis=0, keepdims=True)
                value = jnp.exp(score - top)
                inverse = 1.0 / column_sum(value)
                low = value.astype(BF16)
                if hh == 0 and qb < 2:
                    @pl.when(j > 0)
                    def _():
                        e_copy(n, slot).wait()
                else:
                    e_copy(n, slot).wait()
                est[slot] = low
                e_copy(n, slot).start()
                inv_l[pl.ds(h, 1), part] = inverse
                att_t[head, part] = (dot(v_t[head, :], low) * inverse).astype(BF16)
        here = att_t[pl.ds(pl.multiple_of(j * PAIR, PAIR), PAIR), :].T
        att_s[j] = here
        lanes = pl.ds(pl.multiple_of(c * half + j * PAIR, PAIR), PAIR)
        for jj in range(2):
            att[jj, :, lanes] = att_s[j, rows_of(2 * jj + c), :]
            remote(
                att_s.at[j, rows_of(2 * jj + 1 - c), :], att.at[jj, :, lanes], 6 + 2 * j + jj, core_dev
            ).start()
        return carry

    lax.fori_loop(0, pairs, attend, 0)
    for slot in range(2):
        e_copy(0, slot).wait()
    k1 = 6 + 2 * pairs
    for j in range(pairs):
        lanes = pl.ds(pl.multiple_of((1 - c) * half + j * PAIR, PAIR), PAIR)
        for jj in range(2):
            remote(
                att_s.at[j, rows_of(2 * jj + 1 - c), :], att.at[jj, :, lanes], 6 + 2 * j + jj, core_dev
            ).wait_recv()

    proj_load.wait()
    for j in range(2):
        grown = dot(att[j], proj[...])
        branch[j] = grown
        value = tok[j].astype(F32) + mod[2:3, :] * grown
        middle[j] = value
        normal, _ = normalize(value)
        place = rows_of(2 * j + c)
        hid_f[place, :] = (
            normal * (postnorm[...] * (1.0 + mod[4:5, :])) + mod[3:4, :]
        ).astype(BF16)
        remote(hid_f.at[place, :], hid_f.at[place, :], k1 + j, core_dev).start()

    exp_load.wait()
    con_load.wait()
    for i in range(2):
        units = pl.ds(i * ub, ub)
        off_units = pl.ds(pl.multiple_of((2 * c + i) * ub, PAIR), ub)

        def feed(t, carry, i=i, units=units, off_units=off_units):
            late = lax.div(t, 2)
            j = lax.rem(t, 2)
            p = 2 * j + lax.rem(c + late + i, 2)
            place = rows_of(p)
            if i == 0:
                @pl.when(late == 1)
                def _():
                    remote(hid_f.at[place, :], hid_f.at[place, :], k1 + j, core_dev).wait_recv()
                    remote(gnar.at[place, :], gnar.at[place, :], 4 + j, core_dev).wait_recv()
            v = dot(hid_f[place, :], exp[:, units]) + offsets[:, off_units]
            square = v * v
            th = jnp.tanh(v * (GELU_A + (GELU_A * GELU_B) * square))
            up = 0.5 + 0.5 * th
            low = (v * up).astype(BF16)
            act[place, :] = low
            slope = up + (v * (0.5 - 0.5 * th * th)) * (GELU_A + (3.0 * GELU_A * GELU_B) * square)
            grad = (dot(gnar[place, :], con[units, :], ROWS_BY_ROWS) * slope).astype(BF16)
            gwid[place, :] = grad
            r = 9 + 2 * c + i
            vec[pl.ds(r, 1), :] += column_sum(grad.astype(F32))
            n_part = dot(low, con[units, :])
            h_part = dot(grad, exp[:, units], ROWS_BY_ROWS)
            if i == 0:
                nacc[place, :] = n_part
                hacc[place, :] = h_part
            else:
                n_part = nacc[place, :] + n_part
                h_part = hacc[place, :] + h_part
                nacc[place, :] = n_part
                hacc[place, :] = h_part

                @pl.when(late == 0)
                def _():
                    hsend[j] = hacc[place, :].astype(BF16)
                    remote(hsend.at[j], hrecv.at[j], k1 + 2 + j, core_dev).start()
                    nsend[j] = nacc[place, :].astype(BF16)
                    remote(nsend.at[j], nrecv.at[j], k1 + 4 + j, core_dev).start()
            return carry

        lax.fori_loop(0, 4, feed, 0)
        ge[:, units] = dot(hid_f[...], gwid[...], COLS_BY_COLS).astype(BF16)
        gc[units, :] = dot(act[...], gnar[...], COLS_BY_COLS).astype(BF16)

    for j in range(2):
        remote(hsend.at[j], hrecv.at[j], k1 + 2 + j, core_dev).wait_recv()
        place = rows_of(2 * j + c)
        got = hacc[place, :] + hrecv[j].astype(F32)
        normal, scale = normalize(middle[j])
        vec[3:4, :] += column_sum(got)
        both = column_sum(got * normal)
        vec[4:5, :] += both * postnorm[...]
        vec[7:8, :] += both * (1.0 + mod[4:5, :])
        g = cot[j].astype(F32)
        remote(nsend.at[j], nrecv.at[j], k1 + 4 + j, core_dev).wait_recv()
        narrowed = nacc[place, :] + nrecv[j].astype(F32) + baseline[...]
        ost[j] = (middle[j] + mod[5:6, :] * narrowed).astype(BF16)
        vec[5:6, :] += column_sum(g * narrowed)
        value = g + normalize_back(got * (postnorm[...] * (1.0 + mod[4:5, :])), normal, scale)
        middle[j] = value
        vec[2:3, :] += column_sum(value * branch[j])
        gbr[place, :] = (mod[2:3, :] * value).astype(BF16)
        remote(gbr.at[place, :], gbr.at[place, :], k1 + 6 + j, core_dev).start()

    out_local = local(ost.at[y], out_h.at[y], 0)
    out_push = remote(ost.at[1 - y], out_h.at[y], k1 + 8, y_dev)
    out_local.start()
    out_push.start()
    for j in range(2):
        place = rows_of(2 * j + 1 - c)
        remote(gbr.at[place, :], gbr.at[place, :], k1 + 6 + j, core_dev).wait_recv()

    def e_back(n, slot):
        return pltpu.make_async_copy(e_h.at[n], est.at[slot], esem.at[slot])

    e_back(0, 0).start()
    gp[...] = dot(att_t[...], gbr[...]).astype(BF16)

    def attend_back(j, carry):
        pair = pl.ds(pl.multiple_of(j * PAIR, PAIR), PAIR)
        own = proj[pl.ds(pl.multiple_of(c * half + j * PAIR, PAIR), PAIR), :]
        grown = dot(own, gbr[...], ROWS_BY_ROWS).astype(BF16).astype(F32)
        here = att_t[pair, :].astype(F32)
        scaled = []
        for hh in range(2):
            inverse = inv_l[pl.ds(2 * j + hh, 1), :]
            rows = slice(hh * HDIM, (hh + 1) * HDIM)
            dsum[hh : hh + 1, :] = column_sum(grown[rows] * here[rows]) * inverse
            scaled.append(grown[rows] * inverse)
        turned = jnp.concatenate(scaled, axis=0).astype(BF16).T
        lane = lax.broadcasted_iota(jnp.int32, turned.shape, 1)
        zero = jnp.zeros_like(turned)
        dom[0] = jnp.where(lane < HDIM, turned, zero)
        dom[1] = jnp.where(lane < HDIM, zero, turned)
        for hh in range(2):
            h = 2 * j + hh
            head = pl.ds(pl.multiple_of(h * HDIM, HDIM), HDIM)
            for qb in range(blocks):
                n = h * blocks + qb
                slot = qb % 2
                e_back(n, slot).wait()
                if hh == 1 and qb == blocks - 1:
                    @pl.when(j < pairs - 1)
                    def _():
                        e_back(n + 1, 1 - slot).start()
                else:
                    e_back(n + 1, 1 - slot).start()
                part = pl.ds(qb * span, span)
                low = est[slot]
                there = dom[hh, part, :]
                grad = dot(vv[j], there, ROWS_BY_ROWS)
                grad = (low.astype(F32) * (grad - dsum[hh : hh + 1, part])).astype(BF16)
                v_part = dot(low, there)
                k_part = dot(grad, qm[h, part, :])
                if hh == 0 and qb == 0:
                    dv[...] = v_part
                    dk[...] = k_part
                else:
                    dv[...] += v_part
                    dk[...] += k_part
                dq_t[hh * HDIM : (hh + 1) * HDIM, part] = dot(k_t[head, :], grad)
        gq = dq_t[...].T * HDIM ** (-0.5)
        gk = dk[...]
        gmx[:, :PAIR] = (gq * cosine[...] - turn(gq) * sine[...]).astype(BF16)
        gmx[:, PAIR : 2 * PAIR] = (gk * cosine[...] - turn(gk) * sine[...]).astype(BF16)
        gmx[:, 2 * PAIR :] = dv[...].astype(BF16)
        gm[j] = dot(hid_a[...], gmx[...], COLS_BY_COLS).astype(BF16)
        lanes = pl.ds(pl.multiple_of(j * 3 * PAIR, PAIR), 3 * PAIR)

        def back(p, inner):
            place = rows_of(p)
            part = dot(gmx[place, :], mix[:, lanes], ROWS_BY_ROWS)

            @pl.when(j == 0)
            def _():
                hacc[place, :] = part

            @pl.when(j > 0)
            def _():
                hacc[place, :] += part

            return inner

        lax.fori_loop(0, blocks, back, 0)
        return carry

    lax.fori_loop(0, pairs, attend_back, 0)
    for j in range(2):
        remote(hsend.at[j], hrecv.at[j], k1 + 2 + j, core_dev).wait_send()
        hsend[j] = hacc[rows_of(2 * j + 1 - c), :].astype(BF16)
        remote(hsend.at[j], hrecv.at[j], k1 + 9 + j, core_dev).start()

    out_local.wait()
    out_push.wait()
    for j in range(2):
        remote(hsend.at[j], hrecv.at[j], k1 + 9 + j, core_dev).wait_recv()
        got = hacc[rows_of(2 * j + c), :] + hrecv[j].astype(F32)
        normal, scale = normalize(tok[j].astype(F32))
        vec[0:1, :] += column_sum(got)
        both = column_sum(got * normal)
        vec[1:2, :] += both * prenorm[...]
        vec[6:7, :] += both * (1.0 + mod[1:2, :])
        ost[j] = (
            middle[j] + normalize_back(got * (prenorm[...] * (1.0 + mod[1:2, :])), normal, scale)
        ).astype(BF16)
    gtok_local = local(ost.at[y], gtok_h.at[y], 0)
    gtok_push = remote(ost.at[1 - y], gtok_h.at[y], k1 + 11, y_dev)
    gtok_local.start()
    gtok_push.start()
    stores = [local(ge, ge_h, 1), local(gc, gc_h, 2), local(gp, gp_h, 3), local(gm, gm_h, 4), local(vec, vec_h, 5)]
    for item in stores:
        item.start()
    for item in stores:
        item.wait()
    gtok_local.wait()
    gtok_push.wait()

    tok_swap.wait_send()
    cot_swap.wait_send()
    for j in range(2):
        place = rows_of(2 * j + c)
        for k in (2 + j, 4 + j, k1 + j, k1 + 6 + j):
            remote(hid_a.at[place, :], hid_a.at[place, :], k, core_dev).wait_send()
        for k in (k1 + 4 + j, k1 + 9 + j):
            remote(hsend.at[j], hrecv.at[j], k, core_dev).wait_send()
    for j in range(pairs):
        for jj in range(2):
            remote(
                att_s.at[j, rows_of(2 * jj), :], att.at[jj, :, pl.ds(0, PAIR)], 6 + 2 * j + jj, core_dev
            ).wait_send()


def rotary_constants(length):
    half_dim = HDIM // 2
    frequency = np.exp(np.arange(half_dim, dtype=np.float32) * np.float32(-2.0 * math.log(10000.0) / HDIM))
    angles = np.arange(length, dtype=np.float32)[:, None] * frequency[None, :].astype(np.float32)
    angles = angles.astype(np.float64)
    cosine = np.cos(angles).astype(np.float32)
    sine = np.sin(angles).astype(np.float32)
    cosine = np.concatenate([cosine] * 4, axis=-1)
    sine = np.concatenate([-sine, sine, -sine, sine], axis=-1)
    return cosine, sine


def local_part(wide_count, tokens, condition, cotangent, adaptive, shifts, prenorm, mixer, projection, postnorm,
               expand, offsets, contract, baseline):
    rows, span, width = tokens.shape
    total = 4 * span
    half = width // 2
    pairs = half // PAIR
    ff = expand.shape[1]
    uf = ff // 2
    ub = uf // 2
    cosine, sine = rotary_constants(total)
    hbm = pl.BlockSpec(memory_space=pl.ANY)
    vmem = pl.BlockSpec(memory_space=pltpu.VMEM)
    row_of = lambda v: v.reshape(1, -1)
    out_shape = (
        jax.ShapeDtypeStruct(tokens.shape, BF16),
        jax.ShapeDtypeStruct(tokens.shape, BF16),
        jax.ShapeDtypeStruct((width, uf), BF16),
        jax.ShapeDtypeStruct((uf, width), BF16),
        jax.ShapeDtypeStruct((half, width), BF16),
        jax.ShapeDtypeStruct((pairs, width, 3 * PAIR), BF16),
        jax.ShapeDtypeStruct((16, width), F32),
        jax.ShapeDtypeStruct((2 * pairs * 4, total, span), BF16),
    )
    V = pltpu.VMEM
    piece = (2, span, width)
    whole = (total, width)
    scratch = [
        V(piece, BF16), V(piece, BF16), V(adaptive.shape, BF16), V((width, 3 * half), BF16),
        V(projection.shape, BF16), V((width, uf), BF16), V((uf, width), BF16), V((8, width), F32),
        V(whole, BF16), V((2 * pairs, total, PAIR), BF16), V((pairs, total, PAIR), BF16),
        V((pairs, total, PAIR), BF16), V((half, total), BF16), V((half, total), BF16),
        V((2, total, span), BF16), V((8, total), F32), V((half, total), BF16), V((pairs, total, PAIR), BF16),
        V(piece, BF16),
        V(piece, F32), V(piece, F32), V(whole, BF16), V(whole, BF16), V(whole, BF16), V((total, ub), BF16),
        V((total, ub), BF16), V(whole, F32), V(whole, F32), V(piece, BF16), V(piece, BF16), V(piece, BF16),
        V(piece, BF16),
        V((2, total, PAIR), BF16), V((8, total), F32), V((total, PAIR), F32), V((total, PAIR), F32),
        V((PAIR, total), F32), V((total, 3 * PAIR), BF16), V(piece, BF16),
        V((width, uf), BF16), V((uf, width), BF16), V((half, width), BF16), V((pairs, width, 3 * PAIR), BF16),
        V((16, width), F32),
        pltpu.SemaphoreType.DMA((16,)), pltpu.SemaphoreType.DMA((2,)), pltpu.SemaphoreType.DMA((32,)),
        pltpu.SemaphoreType.DMA((32,)),
    ]
    outs = pl.pallas_call(
        layer_kernel,
        out_shape=out_shape,
        in_specs=[hbm] * 7 + [vmem] * 8,
        out_specs=(hbm,) * 8,
        scratch_shapes=scratch,
        compiler_params=pltpu.CompilerParams(
            collective_id=0, has_side_effects=True, vmem_limit_bytes=64 * 1024 * 1024 - 65536
        ),
        name="layer",
    )(
        tokens, cotangent, adaptive, mixer, projection, expand, contract,
        condition, row_of(shifts), row_of(prenorm), row_of(postnorm), row_of(offsets), row_of(baseline),
        jnp.asarray(cosine), jnp.asarray(sine),
    )
    layer_output, grad_tokens, ge, gc, gp, gm, vec, _ = outs
    core = lax.rem(lax.axis_index("seq"), 2)
    w = lax.axis_index("wide")

    def by_columns(part):
        out = lax.psum_scatter(part.astype(F32), "wide", scatter_dimension=0, tiled=True)
        out = lax.all_gather(out, "seq", axis=0)
        return out[0:2] + out[2:4]

    def by_rows(part):
        whole_part = jnp.zeros((2 * part.shape[0], part.shape[1]), F32)
        whole_part = lax.dynamic_update_slice(whole_part, part.astype(F32), (core * part.shape[0], 0))
        out = lax.psum_scatter(whole_part, "wide", scatter_dimension=0, tiled=True)
        return lax.psum(out, "seq")

    grad_expand = jnp.concatenate(list(by_columns(ge)), axis=-1)
    mixed = by_columns(gm.reshape(pairs, width, 3, PAIR).transpose(1, 2, 0, 3).reshape(width, 3 * half))
    mixed = mixed.reshape(2, -1, 3, half).transpose(1, 2, 0, 3)
    grad_mixer = mixed.reshape(mixed.shape[0], 3 * width)
    grad_contract = by_rows(gc)
    grad_projection = by_rows(gp)

    every = lax.all_gather(vec, ("wide", "seq"), axis=0)
    every = every.reshape(wide_count, 2, 2, 16, width)
    every = (every[:, :, 0] + every[:, :, 1]).reshape(2 * wide_count, 16, width)
    grad_mod = every[:, :6].reshape(2 * wide_count, 6 * width)
    sums = jnp.sum(every[:, 6:13], axis=0)
    conditions = lax.all_gather(condition, "wide", axis=0, tiled=True)
    silu_all = jax.nn.silu(conditions)
    own_rows = adaptive.shape[0] // wide_count
    highest = lax.Precision.HIGHEST
    grad_adaptive = jnp.dot(
        lax.dynamic_slice_in_dim(silu_all, w * own_rows, own_rows, axis=1).T, grad_mod, precision=highest
    )

    def own(vector):
        size = vector.shape[0] // wide_count
        return lax.dynamic_slice_in_dim(vector, w * size, size)

    here = lax.dynamic_slice_in_dim(grad_mod, w * rows, rows, axis=0)
    _, silu_back = jax.vjp(jax.nn.silu, condition)
    (grad_time,) = silu_back(jnp.dot(here, adaptive.astype(F32).T, precision=highest))
    return (
        layer_output, grad_tokens, grad_time, grad_adaptive, own(jnp.sum(grad_mod, axis=0)), own(sums[0]),
        grad_mixer, grad_projection, own(sums[1]), grad_expand, own(sums[3:7].reshape(-1)), grad_contract,
        own(sums[2]),
    )


def solution(mesh):
    rows = P("wide", "seq", None)
    by_wide = P("wide", None)
    in_specs = (rows, by_wide, rows) + (P(),) * 10
    out_specs = (
        rows, rows, by_wide, by_wide, P("wide"), P("wide"), by_wide, by_wide, P("wide"), by_wide, P("wide"),
        by_wide, P("wide"),
    )
    return jax.shard_map(
        functools.partial(local_part, mesh.shape["wide"]),
        mesh=mesh, in_specs=in_specs, out_specs=out_specs, check_vma=False,
    )
```

```python
import functools
import itertools
import math
import types

import jax
import jax.numpy as jnp
import numpy as np
from jax import lax
from jax.experimental import pallas as pl
from jax.experimental.pallas import tpu as pltpu
from jax.sharding import PartitionSpec as P

F32 = jnp.float32
BF16 = jnp.bfloat16
MESH = pl.DeviceIdType.MESH
HDIM = 64
PAIR = 2 * HDIM
EPSILON = 1e-06
GELU_A = 0.7978845608
GELU_B = 0.044715

ROWS_BY_ROWS = (((1,), (1,)), ((), ()))
COLS_BY_COLS = (((0,), (0,)), ((), ()))


def dot(a, b, dims=None):
    if dims is None:
        return jnp.dot(a, b, preferred_element_type=F32)
    return lax.dot_general(a, b, dims, preferred_element_type=F32)


def normalize(values):
    center = values - jnp.mean(values, axis=-1, keepdims=True)
    scale = lax.rsqrt(jnp.mean(center * center, axis=-1, keepdims=True) + EPSILON)
    return center * scale, scale


def normalize_back(grad, normal, scale):
    first = jnp.mean(grad, axis=-1, keepdims=True)
    second = jnp.mean(grad * normal, axis=-1, keepdims=True)
    return scale * (grad - first - normal * second)


def turn(values):
    lane = lax.broadcasted_iota(jnp.int32, values.shape, 1)
    first = lax.rem(lane, HDIM) < HDIM // 2
    return jnp.where(
        first, pltpu.roll(values, PAIR - HDIM // 2, 1), pltpu.roll(values, HDIM // 2, 1)
    )


def column_sum(values):
    return jnp.sum(values, axis=0, keepdims=True)


def kernel_buffers(span, width, extent, ff):
    total = 4 * span
    half = width // 2
    pairs = half // PAIR
    uf = ff // 2
    ub = uf // 2
    strip = width // 16
    block = ff // 16
    V = pltpu.VMEM
    piece = (2, span, width)
    whole = (total, width)
    two = lambda n: (2,) * n
    wide_strip = (strip, width)
    half_strip = (strip, half)
    tall = (block, half)
    return dict(
        tok=V(piece, BF16), cot=V(piece, BF16), adap=V((extent, 6 * width), BF16),
        mix=V((width, 3 * half), BF16), proj=V((width, width), BF16), exp=V((width, uf), BF16),
        con=V((uf, width), BF16), mod=V((8, width), F32),
        hid_a=V(whole, BF16), qq=V((pairs, total, PAIR), BF16), kk=V((pairs, total, PAIR), BF16),
        vv=V((pairs, total, PAIR), BF16), q_t=V((half, total), BF16),
        est=V((2, span, total), BF16), inv_l=V((total, PAIR), F32),
        att_s=V((pairs, total, PAIR), BF16), att=V(piece, BF16),
        branch=V(piece, BF16), middle=V(piece, F32), hid_f=V(whole, BF16), gnar=V(whole, BF16),
        gbr=V(whole, BF16), act=V((total, ub), BF16), gwid=V((total, ub), BF16),
        nacc=V(whole, F32), hacc=V(whole, F32), nsend=V(piece, BF16),
        hsend=V(piece, BF16), hrecv=V(piece, BF16),
        dom=V((total, PAIR), BF16), dom_t=V((PAIR, total), BF16), dsum=V((total, PAIR), F32),
        dv_t=V((PAIR, total), F32), dk_t=V((PAIR, total), F32), dq=V((total, PAIR), F32),
        ge=V((2,) + two(4) + wide_strip, BF16), gc=V(two(4) + tall, BF16), gcs=V(two(2) + tall, BF16),
        gp=V(two(4) + half_strip, BF16), gps=V(two(3) + half_strip, BF16),
        e1=V((2,) + two(3) + wide_strip, BF16), e2=V((2,) + two(2) + wide_strip, BF16),
        e3=V((2,) + two(1) + wide_strip, BF16), e4=V((2,) + wide_strip, BF16),
        c1=V(two(3) + tall, BF16), c2=V(two(2) + tall, BF16), c3=V(two(1) + tall, BF16), c4=V(tall, BF16),
        p1=V(two(3) + half_strip, BF16), p2=V(two(2) + half_strip, BF16), p3=V(two(1) + half_strip, BF16),
        p4=V(half_strip, BF16),
        m1=V((pairs, 8 * strip, half), BF16), m2=V((pairs, 4 * strip, half), BF16),
        m3=V((pairs, 2 * strip, half), BF16), m4=V((pairs,) + half_strip, BF16),
        ag_e=V(two(3) + wide_strip, BF16), ag_c=V(two(2) + tall, BF16),
        ag_m=V(two(2) + (pairs + 1,) + half_strip, BF16),
        va=V((2, 16, half), F32), vb=V((2, 8, half), F32), va_r=V((16, half), F32), vb_r=V((8, half), F32),
        all_a=V((2, 16, 16, half), F32), all_b=V((2, 16, 8, half), F32), st=V((extent, 16), F32),
        lsem=pltpu.SemaphoreType.DMA((64,)), esem=pltpu.SemaphoreType.DMA((2,)),
        ssem=pltpu.SemaphoreType.DMA((100,)), rsem=pltpu.SemaphoreType.DMA((100,)),
    )


INPUTS = (
    "tok_h", "cot_h", "adap_h", "mix_h", "proj_h", "exp_h", "con_h",
    "cond", "shifts", "prenorm", "postnorm", "offsets", "baseline", "cosine", "sine",
)
GRADS = ("out_h", "gtok_h", "oe_h", "oc_h", "op_h", "om_h", "e_h")
FINALS = ("time_o", "adaptive_o", "shifts_o", "prenorm_o", "postnorm_o", "offsets_o", "baseline_o")
PARTIALS = ("all_a_h", "all_b_h")


def layer_kernel(leftover, names, *refs):
    R = types.SimpleNamespace(**dict(zip(names, refs)))
    R.nrecv = R.att
    span = R.tok.shape[1]
    width = R.tok.shape[2]
    total = R.hid_a.shape[0]
    half = width // 2
    pairs = half // PAIR
    blocks = total // span
    ub = R.exp.shape[1] // 2
    strip = width // 16
    block = ub // 4
    w = lax.axis_index("wide")
    s = lax.axis_index("seq")
    y = lax.div(s, 2)
    c = lax.rem(s, 2)
    hi = lax.div(w, leftover)
    b0 = lax.rem(hi, 2)
    b1 = lax.rem(lax.div(hi, 2), 2)
    b2 = lax.div(hi, 4)
    core_dev = (w, y * 2 + 1 - c)
    y_dev = (w, (1 - y) * 2 + c)
    dev0 = (w + leftover * (1 - 2 * b0), s)
    dev1 = (w + 2 * leftover * (1 - 2 * b1), s)
    dev2 = (w + 4 * leftover * (1 - 2 * b2), s)
    remote_count = itertools.count()
    local_count = itertools.count()
    sent = []

    def rows_of(p):
        return pl.ds(pl.multiple_of(p * span, span), span)

    def remote(src, dst, k, dev):
        return pltpu.make_async_remote_copy(
            src_ref=src, dst_ref=dst, send_sem=R.ssem.at[k], recv_sem=R.rsem.at[k],
            device_id=dev, device_id_type=MESH,
        )

    class Link:
        def __init__(self, item):
            self.item, self.open = item, False
            sent.append(self)

        def start(self):
            self.item.start()
            self.open = True

        def wait_recv(self):
            self.item.wait_recv()

        def wait_send(self):
            self.item.wait_send()
            self.open = False

    def link(src, dst, dev):
        return Link(remote(src, dst, next(remote_count), dev))

    def local(src, dst):
        return pltpu.make_async_copy(src, dst, R.lsem.at[next(local_count)])

    own_place = [rows_of(2 * j + c) for j in range(2)]
    other_place = [rows_of(2 * j + 1 - c) for j in range(2)]

    adap_load = local(R.adap_h, R.adap)
    tok_load = local(R.tok_h.at[y], R.tok.at[y])
    cot_load = local(R.cot_h.at[y], R.cot.at[y])
    mix_loads = []
    for j in range(pairs):
        for b in range(3):
            mix_loads.append(local(
                R.mix_h.at[:, pl.ds(pl.multiple_of(b * width + c * half + j * PAIR, PAIR), PAIR)],
                R.mix.at[:, pl.ds((j * 3 + b) * PAIR, PAIR)],
            ))
    proj_load = local(R.proj_h, R.proj)
    exp_load = local(R.exp_h.at[:, pl.ds(pl.multiple_of(c * 2 * ub, PAIR), 2 * ub)], R.exp)
    con_load = local(R.con_h.at[pl.ds(pl.multiple_of(c * 2 * ub, PAIR), 2 * ub), :], R.con)
    for item in [adap_load, tok_load, cot_load] + mix_loads + [proj_load, exp_load, con_load]:
        item.start()

    barrier = pltpu.get_barrier_semaphore()
    for dev in (core_dev, y_dev, dev0, dev1, dev2):
        pl.semaphore_signal(barrier, inc=1, device_id=dev, device_id_type=MESH)
    pl.semaphore_wait(barrier, 5)

    tok_swap = link(R.tok_h.at[1 - y], R.tok.at[y], y_dev)
    cot_swap = link(R.cot_h.at[1 - y], R.cot.at[y], y_dev)
    hid_a_push = []
    for j in (y, 1 - y):
        place = rows_of(2 * j + c)
        hid_a_push.append(link(R.hid_a.at[place, :], R.hid_a.at[place, :], core_dev))
    gnar_base = next(remote_count)
    next(remote_count)
    gnar_push = [Link(remote(R.gnar.at[p, :], R.gnar.at[p, :], gnar_base + j, core_dev)) for j, p in enumerate(own_place)]
    hid_f_base = next(remote_count)
    next(remote_count)
    hid_f_push = [Link(remote(R.hid_f.at[p, :], R.hid_f.at[p, :], hid_f_base + j, core_dev)) for j, p in enumerate(own_place)]
    att_base = next(remote_count)
    for _ in range(2 * pairs - 1):
        next(remote_count)
    hsum_base = next(remote_count)
    next(remote_count)
    nsum_base = next(remote_count)
    next(remote_count)
    hsum_push = [Link(remote(R.hsend.at[j], R.hrecv.at[j], hsum_base + j, core_dev)) for j in range(2)]
    nsum_push = [Link(remote(R.nsend.at[j], R.nrecv.at[j], nsum_base + j, core_dev)) for j in range(2)]
    gbr_push = [link(R.gbr.at[p, :], R.gbr.at[p, :], core_dev) for p in own_place]
    asum_push = [link(R.hsend.at[j], R.hrecv.at[j], core_dev) for j in range(2)]
    def stage(n, j):
        return R.gwid.at[pl.ds(pl.multiple_of((2 * n + j) * span, span), span), :]

    out_push = link(stage(0, 1 - y), R.out_h.at[y], y_dev)
    gtok_push = link(stage(1, 1 - y), R.gtok_h.at[y], y_dev)

    class Halving:
        def __init__(self, acc, steps):
            self.acc = acc
            self.steps = []
            place = ()
            for bit, dev, recv in steps:
                self.steps.append((link(acc.at[place + (1 - bit,)], recv, dev), place + (bit,), recv))
                place = place + (bit,)

        def send(self, t):
            self.steps[t][0].start()

        def land(self, t, into=None):
            item, place, recv = self.steps[t]
            item.wait_recv()
            value = self.acc.at[place][...] + recv[...]
            if into is None:
                self.acc.at[place][...] = value
            else:
                into[...] = value

    class Strips:
        def __init__(self, ref, lanes):
            self.ref, self.lanes = ref, lanes

        @property
        def at(self):
            return self

        def __getitem__(self, bits):
            start = 0
            for n, bit in enumerate(bits):
                start = start + bit * (8 >> n)
            rows = (16 >> len(bits)) * strip
            return self.ref.at[pl.ds(pl.multiple_of(start * strip, strip), rows), self.lanes]

    x_step, z_step, y_step, q_step = (b0, dev0), (b1, dev1), (y, y_dev), (b2, dev2)
    sum_e = [
        Halving(R.ge.at[i], [z_step + (R.e1.at[i],), y_step + (R.e2.at[i],), x_step + (R.e3.at[i],), q_step + (R.e4.at[i],)])
        for i in range(2)
    ]
    sum_m = [
        Halving(Strips(R.exp, pl.ds(j * half, half)), [x_step + (R.m1.at[j],), z_step + (R.m2.at[j],), y_step + (R.m3.at[j],), q_step + (R.m4.at[j],)])
        for j in range(pairs)
    ]
    swap_p = link(R.gps, R.gp.at[:, :, :, c], core_dev)
    sum_p = Halving(R.gp, [y_step + (R.p1,), x_step + (R.p2,), z_step + (R.p3,), q_step + (R.p4,)])
    swap_c = [link(R.gcs, R.gc.at[:, :, i, c], core_dev) for i in range(2)]
    first_c = [link(R.gc.at[1 - b0, :, i], R.c1.at[i], dev0) for i in range(2)]
    second_c = [link(R.gc.at[b0, 1 - y, i], R.c2.at[i], y_dev) for i in range(2)]
    third_c = link(R.gc.at[b0, y, 1 - b1], R.c3, dev1)
    fourth_c = link(R.gc.at[b0, y, b1, 1 - b2], R.c4, dev2)

    def land_c1(i):
        first_c[i].wait_recv()
        R.gc[b0, :, i] = R.gc[b0, :, i] + R.c1[i]

    def land_c2(i):
        second_c[i].wait_recv()
        R.gc[b0, y, i] = R.gc[b0, y, i] + R.c2[i]

    def land_c3():
        third_c.wait_recv()
        R.gc[b0, y, b1] = R.gc[b0, y, b1] + R.c3[...]

    def land_c4():
        fourth_c.wait_recv()
        R.ag_c[c, y] = R.gc[b0, y, b1, b2] + R.c4[...]

    y_e, core_e = link(R.ag_e.at[c, y], R.ag_e.at[c, y], y_dev), link(R.ag_e.at[c], R.ag_e.at[c], core_dev)
    y_c, core_c = link(R.ag_c.at[c, y], R.ag_c.at[c, y], y_dev), link(R.ag_c.at[c], R.ag_c.at[c], core_dev)
    most, last = pl.ds(0, pairs), pl.ds(pairs, 1)
    y_m, core_m = [], []
    for part in (most, last):
        y_m.append(link(R.ag_m.at[c, y, part], R.ag_m.at[c, y, part], y_dev))
        core_m.append(link(R.ag_m.at[c, :, part], R.ag_m.at[c, :, part], core_dev))

    def add_row(ref, r, value):
        for n in range(2):
            ref[n, pl.ds(r, 1), :] += value[:, n * half : (n + 1) * half]

    chip = y * 8 + hi

    class Gather:
        def __init__(self, part, recv, every):
            self.part, self.recv, self.every = part, recv, every
            self.first = link(part.at[1 - c], recv, core_dev)
            self.steps = []
            for t, dev in enumerate((dev0, dev1, dev2, y_dev)):
                size = 2**t
                start = lax.div(chip, size) * size
                ref = every.at[c, pl.ds(start, size)]
                self.steps.append(link(ref, ref, dev))
            self.steps.append(link(every.at[c], every.at[c], core_dev))

        def start(self):
            self.first.start()

        def step(self, t):
            if t == 0:
                self.first.wait_recv()
                self.every[c, chip] = self.part[c] + self.recv[...]
            else:
                self.steps[t - 1].wait_recv()
            self.steps[t].start()

        def finish(self):
            self.steps[-1].wait_recv()

    gather_a = Gather(R.va, R.va_r, R.all_a)
    gather_b = Gather(R.vb, R.vb_r, R.all_b)

    tok_swap.start()
    cot_swap.start()
    R.va[...] = jnp.zeros_like(R.va)
    R.vb[...] = jnp.zeros_like(R.vb)

    adap_load.wait()
    crow = jnp.where(y == 0, R.cond[0:1, :], R.cond[1:2, :])
    crow = crow * (1.0 / (1.0 + jnp.exp(-crow)))
    extent = crow.shape[1]
    R.va[0, 10:11, :extent] = crow * (1 - c).astype(F32)
    eye = lax.broadcasted_iota(jnp.int32, (extent, extent), 0) == lax.broadcasted_iota(
        jnp.int32, (extent, extent), 1
    )
    ccol = jnp.sum(jnp.where(eye, jnp.broadcast_to(crow, (extent, extent)), 0.0), axis=1, keepdims=True)
    shifts = R.shifts[...].reshape(1, 6 * width)
    for n in range(6):
        part = pl.ds(n * width, width)
        R.mod[n : n + 1, :] = column_sum(R.adap[:, part].astype(F32) * ccol) + shifts[:, n * width : (n + 1) * width]
    pregain = R.prenorm[...].reshape(1, width)
    postgain = R.postnorm[...].reshape(1, width)

    def first_norm(j, t):
        normal, _ = normalize(R.tok[j].astype(F32))
        value = normal * (pregain * (1.0 + R.mod[1:2, :])) + R.mod[0:1, :]
        R.hid_a[rows_of(2 * j + c), :] = value.astype(BF16)
        hid_a_push[t].start()

    def project(p):
        place = rows_of(p)
        mixed = dot(R.hid_a[place, :], R.mix[...])
        cos_here = R.cosine[place, :]
        sin_here = R.sine[place, :]
        for j in range(pairs):
            base = j * 3 * PAIR
            query = mixed[:, base : base + PAIR]
            query = (query * cos_here + turn(query) * sin_here).astype(BF16) * jnp.asarray(
                HDIM ** (-0.5), BF16
            )
            R.qq[j, place, :] = query
            key = mixed[:, base + PAIR : base + 2 * PAIR]
            R.kk[j, place, :] = (key * cos_here + turn(key) * sin_here).astype(BF16)
            R.vv[j, place, :] = mixed[:, base + 2 * PAIR : base + 3 * PAIR].astype(BF16)

    tok_load.wait()
    first_norm(y, 0)
    for item in mix_loads:
        item.wait()
    project(2 * y + c)
    tok_swap.wait_recv()
    first_norm(1 - y, 1)
    hid_a_push[0].wait_recv()
    project(2 * y + 1 - c)
    project(2 * (1 - y) + c)
    hid_a_push[1].wait_recv()
    project(2 * (1 - y) + 1 - c)
    for j in range(pairs):
        R.q_t[j * PAIR : (j + 1) * PAIR, :] = R.qq[j].T

    cot_load.wait()
    cot_swap.wait_recv()
    for j in range(2):
        low = (R.cot[j].astype(F32) * R.mod[5:6, :]).astype(BF16)
        R.gnar[own_place[j], :] = low
        add_row(R.va, 5, column_sum(low.astype(F32)))
        gnar_push[j].start()

    def e_copy(n, slot):
        return pltpu.make_async_copy(R.est.at[slot], R.e_h.at[n], R.esem.at[slot])

    def att_push(j, jj):
        lanes = pl.ds(pl.multiple_of(c * half + j * PAIR, PAIR), PAIR)
        return remote(
            R.att_s.at[j, other_place[jj], :], R.att.at[jj, :, lanes], att_base + 2 * j + jj, core_dev
        )

    lane_pair = lax.broadcasted_iota(jnp.int32, (span, PAIR), 1)
    lane_long = lax.broadcasted_iota(jnp.int32, (total, PAIR), 1)

    def in_head(lane, hh):
        return lane < HDIM if hh == 0 else lane >= HDIM

    def attend(j, carry):
        def score_of(hh, qb):
            query = R.qq[j, qb * span : (qb + 1) * span, :]
            query = jnp.where(in_head(lane_pair, hh), query, jnp.zeros_like(query))
            return dot(query, R.kk[j], ROWS_BY_ROWS)

        values = []
        for hh in range(2):
            there = R.vv[j]
            values.append(jnp.where(in_head(lane_long, hh), there, jnp.ones_like(there)))
        steps = [(hh, qb) for hh in range(2) for qb in range(blocks)]
        score = score_of(*steps[0])
        for index, (hh, qb) in enumerate(steps):
            following = score_of(*steps[index + 1]) if index + 1 < len(steps) else None
            n = j * (2 * blocks) + index
            slot = index % 2
            place = slice(qb * span, (qb + 1) * span)
            top = jnp.max(score, axis=1, keepdims=True)
            low = jnp.exp(score - top).astype(BF16)
            if index < 2:
                @pl.when(j > 0)
                def _():
                    e_copy(n, slot).wait()
            else:
                e_copy(n, slot).wait()
            R.est[slot] = low
            e_copy(n, slot).start()
            grown = dot(low, values[hh])
            inverse = 1.0 / pltpu.roll(grown, HDIM, 1)
            grown = (grown * inverse).astype(BF16)
            head_lane = 0 if hh == 0 else HDIM
            R.inv_l[place, :] = jnp.where(
                lane_pair == 2 * j + hh, inverse[:, head_lane : head_lane + 1], R.inv_l[place, :]
            )
            if hh == 0:
                R.att_s[j, place, :] = grown
            else:
                R.att_s[j, place, :] = jnp.where(lane_pair < HDIM, R.att_s[j, place, :], grown)
            score = following
        lanes = pl.ds(pl.multiple_of(c * half + j * PAIR, PAIR), PAIR)
        for jj in range(2):
            att_push(j, jj).start()
            R.att[jj, :, lanes] = R.att_s[j, own_place[jj], :]
        return carry

    R.inv_l[...] = jnp.zeros_like(R.inv_l)
    lax.fori_loop(0, pairs, attend, 0)
    for slot in range(2):
        e_copy(0, slot).wait()
    for j in range(pairs):
        for jj in range(2):
            att_push(j, jj).wait_recv()

    proj_load.wait()
    for j in range(2):
        grown = dot(R.att[j], R.proj[...])
        R.branch[j] = grown.astype(BF16)
        value = R.tok[j].astype(F32) + R.mod[2:3, :] * grown
        R.middle[j] = value
        normal, _ = normalize(value)
        R.hid_f[own_place[j], :] = (normal * (postgain * (1.0 + R.mod[4:5, :])) + R.mod[3:4, :]).astype(BF16)
        hid_f_push[j].start()

    exp_load.wait()
    con_load.wait()
    offsets = R.offsets[...].reshape(1, 4 * ub)
    offsets = jnp.where(c == 0, offsets[:, : 2 * ub], offsets[:, 2 * ub :])
    for i in range(2):
        units = pl.ds(i * ub, ub)

        def feed(t, carry, i=i, units=units):
            late = lax.div(t, 2)
            j = lax.rem(t, 2)
            place = rows_of(2 * j + lax.rem(c + late + i, 2))
            if i == 0:
                @pl.when(late == 1)
                def _():
                    remote(R.hid_f.at[place, :], R.hid_f.at[place, :], hid_f_base + j, core_dev).wait_recv()
                    remote(R.gnar.at[place, :], R.gnar.at[place, :], gnar_base + j, core_dev).wait_recv()
            else:
                @pl.when(t == 1)
                def _():
                    swap_c[0].wait_recv()
                    first_c[0].start()
            v = dot(R.hid_f[place, :], R.exp[:, units]) + offsets[:, i * ub : (i + 1) * ub]
            square = v * v
            th = jnp.tanh(v * (GELU_A + (GELU_A * GELU_B) * square))
            up = 0.5 + 0.5 * th
            low = (v * up).astype(BF16)
            R.act[place, :] = low
            slope = up + (v * (0.5 - 0.5 * th * th)) * (GELU_A + (3.0 * GELU_A * GELU_B) * square)
            grad = (dot(R.gnar[place, :], R.con[units, :], ROWS_BY_ROWS) * slope).astype(BF16)
            R.gwid[place, :] = grad
            add_row(R.va, 6 + 2 * c + i, column_sum(grad.astype(F32)))
            n_part = dot(low, R.con[units, :])
            h_part = dot(grad, R.exp[:, units], ROWS_BY_ROWS)
            if i == 0:
                R.nacc[place, :] = n_part
                R.hacc[place, :] = h_part
            else:
                R.nacc[place, :] += n_part
                R.hacc[place, :] += h_part

                @pl.when(late == 0)
                def _():
                    R.hsend[j] = R.hacc[place, :].astype(BF16)
                    remote(R.hsend.at[j], R.hrecv.at[j], hsum_base + j, core_dev).start()
                    R.nsend[j] = R.nacc[place, :].astype(BF16)
                    remote(R.nsend.at[j], R.nrecv.at[j], nsum_base + j, core_dev).start()
            return carry

        lax.fori_loop(0, 4, feed, 0)
        if i == 1:
            for item in hsum_push + nsum_push:
                item.open = True
        value = dot(R.hid_f[...], R.gwid[...], COLS_BY_COLS).astype(BF16)
        for n in range(16):
            a2, a1, a0, ay = n // 8, n // 4 % 2, n // 2 % 2, n % 2
            R.ge[i, a1, ay, a0, a2] = value[n * strip : (n + 1) * strip]
        sum_e[i].send(0)
        value = dot(R.act[...], R.gnar[...], COLS_BY_COLS).astype(BF16)
        left, right = value[:, :half], value[:, half:]
        mine = jnp.where(c == 0, left, right)
        theirs = jnp.where(c == 0, right, left)
        if i == 1:
            swap_c[0].wait_send()
        for n in range(4):
            a0, ay = n // 2, n % 2
            R.gcs[a0, ay] = theirs[n * block : (n + 1) * block]
            R.gc[a0, ay, i, c] = mine[n * block : (n + 1) * block]
        swap_c[i].start()

    base_row = R.baseline[...].reshape(1, width)
    for j in range(2):
        place = own_place[j]
        hsum_push[j].wait_recv()
        got = R.hacc[place, :] + R.hrecv[j].astype(F32)
        normal, scale = normalize(R.middle[j])
        add_row(R.va, 1, column_sum(got))
        both = column_sum(got * normal)
        add_row(R.va, 2, both * postgain)
        add_row(R.va, 4, both * (1.0 + R.mod[4:5, :]))
        g = R.cot[j].astype(F32)
        nsum_push[j].wait_recv()
        narrowed = R.nacc[place, :] + R.nrecv[j].astype(F32) + base_row
        R.gwid[j * span : (j + 1) * span, :] = (R.middle[j] + R.mod[5:6, :] * narrowed).astype(BF16)
        add_row(R.va, 3, column_sum(g * narrowed))
        value = g + normalize_back(got * (postgain * (1.0 + R.mod[4:5, :])), normal, scale)
        R.middle[j] = value
        add_row(R.va, 0, column_sum(value * R.branch[j].astype(F32)))
        R.gbr[place, :] = (R.mod[2:3, :] * value).astype(BF16)
        gbr_push[j].start()
        if j == 0:
            swap_c[1].wait_recv()
            first_c[1].start()

    out_local = local(stage(0, y), R.out_h.at[y])
    out_local.start()
    out_push.start()
    gather_a.start()
    for j in range(2):
        gbr_push[j].wait_recv()

    def e_back(n, slot):
        return pltpu.make_async_copy(R.e_h.at[n], R.est.at[slot], R.esem.at[slot])

    e_back(0, 0).start()
    value = jnp.concatenate(
        [dot(R.att_s[j], R.gbr[...], COLS_BY_COLS).astype(BF16) for j in range(pairs)], axis=0
    )
    left, right = value[:, :half], value[:, half:]
    mine = jnp.where(c == 0, left, right)
    theirs = jnp.where(c == 0, right, left)
    for n in range(8):
        a1, a0, ay = n // 4, n // 2 % 2, n % 2
        R.gps[ay, a0, a1] = theirs[n * strip : (n + 1) * strip]
        R.gp[ay, a0, a1, c] = mine[n * strip : (n + 1) * strip]
    swap_p.start()
    sum_e[0].land(0)
    sum_e[0].send(1)

    def m_first(j):
        return lambda: sum_m[j].send(0)

    def forward(item, t, into=None):
        def run():
            item.land(t, into)
            if into is None:
                item.send(t + 1)
        return run

    def c_second(i):
        def run():
            land_c1(i)
            second_c[i].start()
        return run

    def c_third():
        land_c2(0)
        land_c2(1)
        third_c.start()

    def c_fourth():
        land_c3()
        fourth_c.start()

    def c_last():
        land_c4()
        y_c.start()

    def c_core():
        y_c.wait_recv()
        core_c.start()

    def e_y():
        y_e.start()

    def e_core():
        y_e.wait_recv()
        core_e.start()

    def p_first():
        swap_p.wait_recv()
        sum_p.send(0)

    final_e = [R.ag_e.at[c, y, i] for i in range(2)]
    final_m = [R.ag_m.at[c, y, 1 + j] for j in range(pairs)]
    final_p = R.ag_m.at[c, y, 0]
    schedule = {
        (0, 0): [p_first, lambda: gather_a.step(0)],
        (0, 1): [c_second(0), lambda: gather_a.step(1)],
        (0, 2): [m_first(0), forward(sum_e[0], 1)],
        (1, 0): [forward(sum_e[1], 0), lambda: gather_a.step(2)],
        (1, 1): [c_second(1), forward(sum_p, 0), lambda: gather_a.step(3)],
        (1, 2): [m_first(1), forward(sum_e[0], 2)],
        (2, 0): [forward(sum_e[1], 1), forward(sum_m[0], 0), forward(sum_p, 1), lambda: gather_a.step(4)],
        (2, 1): [c_third, forward(sum_e[0], 3, final_e[0]), forward(sum_p, 2)],
        (2, 2): [m_first(2), forward(sum_e[1], 2), forward(sum_m[0], 1), forward(sum_m[1], 0)],
    }

    def service(j, point):
        for k in range(pairs):
            tasks = schedule.get((k, point), [])
            if tasks:
                @pl.when(j == k)
                def _(tasks=tasks):
                    for task in tasks:
                        task()

    own_proj = R.proj[pl.ds(pl.multiple_of(c * half, PAIR), half), :]
    grown = dot(R.gbr[...], own_proj, ROWS_BY_ROWS).astype(BF16)
    for j in range(pairs):
        R.act[:, half + j * PAIR : half + (j + 1) * PAIR] = grown[:, j * PAIR : (j + 1) * PAIR]

    def attend_back(j, carry):
        grown = R.act[:, pl.ds(pl.multiple_of(half + j * PAIR, PAIR), PAIR)].astype(F32)
        product = grown * R.att_s[j].astype(F32)
        table = R.inv_l[...]
        inverse, inner = [], []
        for hh in range(2):
            inverse.append(jnp.sum(jnp.where(lane_long == 2 * j + hh, table, 0.0), axis=1, keepdims=True))
            inner.append(jnp.sum(jnp.where(in_head(lane_long, hh), product, 0.0), axis=1, keepdims=True))
        inverse = jnp.where(in_head(lane_long, 0), inverse[0], inverse[1])
        R.dsum[...] = jnp.where(in_head(lane_long, 0), inner[0], inner[1]) * inverse
        grown = (grown * inverse).astype(BF16)
        R.dom[...] = grown
        R.dom_t[...] = grown.T

        def grad_of(hh, qb):
            there = R.dom[qb * span : (qb + 1) * span, :]
            there = jnp.where(in_head(lane_pair, hh), there, jnp.zeros_like(there))
            return dot(there, R.vv[j], ROWS_BY_ROWS)

        steps = [(hh, qb) for hh in range(2) for qb in range(blocks)]
        grad = grad_of(*steps[0])
        for index, (hh, qb) in enumerate(steps):
            following = grad_of(*steps[index + 1]) if index + 1 < len(steps) else None
            n = j * (2 * blocks) + index
            slot = index % 2
            e_back(n, slot).wait()
            if index + 1 == len(steps):
                @pl.when(j < pairs - 1)
                def _():
                    e_back(n + 1, 1 - slot).start()
            else:
                e_back(n + 1, 1 - slot).start()
            place = slice(qb * span, (qb + 1) * span)
            rows = slice(hh * HDIM, (hh + 1) * HDIM)
            low = R.est[slot]
            grad = (low.astype(F32) * (grad - R.dsum[place, hh * HDIM : hh * HDIM + 1])).astype(BF16)
            q_part = dot(grad, R.kk[j])
            v_part = dot(R.dom_t[rows, place], low)
            k_part = dot(R.q_t[pl.ds(pl.multiple_of(j * PAIR + hh * HDIM, HDIM), HDIM), place], grad)
            if hh == 0:
                R.dq[place, :] = q_part
            else:
                R.dq[place, :] = jnp.where(lane_pair < HDIM, R.dq[place, :], q_part)
            if qb == 0:
                R.dv_t[rows, :] = v_part
                R.dk_t[rows, :] = k_part
            else:
                R.dv_t[rows, :] += v_part
                R.dk_t[rows, :] += k_part
            if qb == blocks - 1:
                service(j, hh)
            grad = following
        gq = R.dq[...] * HDIM ** (-0.5)
        gk = R.dk_t[...].T
        gmx = R.act.at[:, pl.ds(0, 3 * PAIR)]
        gmx[:, :PAIR] = (gq * R.cosine[...] - turn(gq) * R.sine[...]).astype(BF16)
        gmx[:, PAIR : 2 * PAIR] = (gk * R.cosine[...] - turn(gk) * R.sine[...]).astype(BF16)
        gmx[:, 2 * PAIR :] = R.dv_t[...].astype(BF16).T
        value = dot(R.hid_a[...], gmx[...], COLS_BY_COLS).astype(BF16)
        for n in range(16):
            a2, a1, a0, ay = n // 8, n // 4 % 2, n // 2 % 2, n % 2
            index = ((a0 * 2 + a1) * 2 + ay) * 2 + a2
            R.exp[index * strip : (index + 1) * strip, pl.ds(pl.multiple_of(j * half, PAIR), half)] = value[
                n * strip : (n + 1) * strip
            ]
        service(j, 2)
        lanes = pl.ds(pl.multiple_of(j * 3 * PAIR, PAIR), 3 * PAIR)

        def back(p, inner):
            place = rows_of(p)
            part = dot(gmx[place, :], R.mix[:, lanes], ROWS_BY_ROWS)

            @pl.when(j == 0)
            def _():
                R.hacc[place, :] = part

            @pl.when(j > 0)
            def _():
                R.hacc[place, :] += part

            return inner

        lax.fori_loop(0, blocks, back, 0)
        return carry

    lax.fori_loop(0, pairs, attend_back, 0)
    for j in range(2):
        hsum_push[j].wait_send()
        R.hsend[j] = R.hacc[other_place[j], :].astype(BF16)
        asum_push[j].start()

    forward(sum_p, 3, final_p)()
    c_fourth()
    gtok_local = local(stage(1, y), R.gtok_h.at[y])
    for j, item in ((1 - y, gtok_push), (y, gtok_local)):
        got = R.hacc[rows_of(2 * j + c), :] + 0.0
        if item is gtok_push:
            asum_push[0].wait_recv()
            asum_push[1].wait_recv()
        got = got + R.hrecv[j].astype(F32)
        normal, scale = normalize(R.tok[j].astype(F32))
        add_row(R.vb, 0, column_sum(got))
        both = column_sum(got * normal)
        add_row(R.vb, 1, both * pregain)
        add_row(R.vb, 2, both * (1.0 + R.mod[1:2, :]))
        stage(1, j)[...] = (
            R.middle[j] + normalize_back(got * (pregain * (1.0 + R.mod[1:2, :])), normal, scale)
        ).astype(BF16)
        item.start()
    gather_b.start()
    forward(sum_e[1], 3, final_e[1])()
    e_y()
    forward(sum_m[0], 2)()
    forward(sum_m[1], 1)()
    forward(sum_m[2], 0)()
    gather_b.step(0)
    c_last()
    forward(sum_m[0], 3, final_m[0])()
    forward(sum_m[1], 2)()
    forward(sum_m[2], 1)()
    gather_b.step(1)
    e_core()
    forward(sum_m[1], 3, final_m[1])()
    y_m[0].start()
    forward(sum_m[2], 2)()
    gather_b.step(2)
    c_core()
    forward(sum_m[2], 3, final_m[2])()
    y_m[1].start()
    gather_b.step(3)
    y_m[0].wait_recv()
    core_m[0].start()
    gather_b.step(4)
    y_m[1].wait_recv()
    core_m[1].start()

    stores = []

    def store(src, dst):
        item = local(src, dst)
        item.start()
        stores.append(item)

    core_e.wait_recv()
    for n in range(8):
        cc, yy, i = n // 4, n // 2 % 2, n % 2
        store(
            R.ag_e.at[cc, yy, i],
            R.oe_h.at[pl.ds(yy * strip, strip), pl.ds((2 * cc + i) * width, width)],
        )
    core_c.wait_recv()
    for n in range(4):
        cc, yy = n // 2, n % 2
        store(R.ag_c.at[cc, yy], R.oc_h.at[pl.ds(yy * block, block), pl.ds(cc * half, half)])
    gather_a.finish()
    gather_b.finish()
    if leftover == 1:
        finish_vectors(R, hi, width, half, extent)
    else:
        store(R.all_a, R.all_a_h)
        store(R.all_b, R.all_b_h)
    core_m[0].wait_recv()
    for n in range(4):
        cc, yy = n // 2, n % 2
        store(R.ag_m.at[cc, yy, 0], R.op_h.at[pl.ds(yy * strip, strip), pl.ds(cc * half, half)])
    core_m[1].wait_recv()
    for item in hid_f_push:
        item.open = True
        item.wait_send()
    for n in range(4):
        cc, yy = n // 2, n % 2
        for j in range(pairs):
            value = R.ag_m[cc, yy, 1 + j]
            for b in range(3):
                lane = cc * half + j * PAIR
                row = (2 * b + yy) * strip
                R.hid_f[row : row + strip, lane : lane + PAIR] = value[:, b * PAIR : (b + 1) * PAIR]
    for b in range(3):
        store(R.hid_f.at[pl.ds(2 * b * strip, 2 * strip), :], R.om_h.at[:, pl.ds(b * width, width)])
    for item in stores:
        item.wait()
    out_local.wait()
    out_push.wait_recv()
    gtok_local.wait()
    gtok_push.wait_recv()
    for j in range(pairs):
        for jj in range(2):
            att_push(j, jj).wait_send()
    for item in sent:
        if item.open:
            item.wait_send()


def finish_vectors(R, hi, width, half, extent):
    own = extent // 8
    highest = lax.Precision.HIGHEST
    R.st[...] = R.all_a[0, :, 10, :extent].T
    silu_own = R.st[pl.ds(pl.multiple_of(hi * own, own), own), :]
    sections = ((R.all_b, 0), (R.all_b, 1), (R.all_a, 0), (R.all_a, 1), (R.all_a, 2), (R.all_a, 3))
    sums = []
    back = [jnp.zeros((extent, 1), F32) for _ in range(2)]
    for n, (ref, r) in enumerate(sections):
        for h in range(2):
            grads = ref[h, :, r, :]
            lanes = pl.ds(n * width + h * half, half)
            R.adaptive_o[:, lanes] = jnp.dot(silu_own, grads, precision=highest, preferred_element_type=F32)
            sums.append(column_sum(grads))
            table = R.adap[:, lanes].astype(F32)
            for yy in range(2):
                mine = ref[h, pl.ds(yy * 8 + hi, 1), r, :]
                back[yy] = back[yy] + jnp.sum(table * mine, axis=1, keepdims=True)
    eye = lax.broadcasted_iota(jnp.int32, (extent, extent), 0) == lax.broadcasted_iota(
        jnp.int32, (extent, extent), 1
    )
    for yy in range(2):
        row = column_sum(jnp.where(eye, jnp.broadcast_to(back[yy], (extent, extent)), 0.0))
        cond = R.cond[yy : yy + 1, :]
        gate = 1.0 / (1.0 + jnp.exp(-cond))
        R.time_o[yy : yy + 1, :] = row * (gate * (1.0 + cond * (1.0 - gate)))

    def share(vector, out):
        size = vector.shape[1] // 8
        value = jnp.zeros((1, size), F32)
        for k in range(8):
            value = jnp.where(hi == k, vector[:, k * size : (k + 1) * size], value)
        out[...] = value.reshape(size)

    def total_of(ref, r):
        return jnp.concatenate([column_sum(ref[h, :, r, :]) for h in range(2)], axis=1)

    share(jnp.concatenate(sums, axis=1), R.shifts_o)
    share(total_of(R.all_b, 2), R.prenorm_o)
    share(total_of(R.all_a, 4), R.postnorm_o)
    share(jnp.concatenate([total_of(R.all_a, 6 + n) for n in range(4)], axis=1), R.offsets_o)
    share(total_of(R.all_a, 5), R.baseline_o)


def rotary_constants(length):
    half_dim = HDIM // 2
    frequency = np.exp(np.arange(half_dim, dtype=np.float32) * np.float32(-2.0 * math.log(10000.0) / HDIM))
    angles = np.arange(length, dtype=np.float32)[:, None] * frequency[None, :].astype(np.float32)
    angles = angles.astype(np.float64)
    cosine = np.cos(angles).astype(np.float32)
    sine = np.sin(angles).astype(np.float32)
    cosine = np.concatenate([cosine] * 4, axis=-1)
    sine = np.concatenate([-sine, sine, -sine, sine], axis=-1)
    return cosine, sine


def local_part(wide_count, tokens, condition, cotangent, adaptive, shifts, prenorm, mixer, projection, postnorm,
               expand, offsets, contract, baseline):
    rows, span, width = tokens.shape
    total = 4 * span
    half = width // 2
    pairs = half // PAIR
    ff = expand.shape[1]
    extent = adaptive.shape[0]
    leftover = wide_count // 8
    cosine, sine = rotary_constants(total)
    hbm = pl.BlockSpec(memory_space=pl.ANY)
    vmem = pl.BlockSpec(memory_space=pltpu.VMEM)
    shape = jax.ShapeDtypeStruct
    out_shape = [
        shape(tokens.shape, BF16), shape(tokens.shape, BF16), shape((width // 8, ff), BF16),
        shape((ff // 8, width), BF16), shape((width // 8, width), BF16), shape((width // 8, 3 * width), BF16),
        shape((2 * pairs * 4, span, total), BF16),
    ]
    out_specs = [hbm] * len(out_shape)
    names = INPUTS + GRADS
    if leftover == 1:
        names += FINALS
        out_shape += [
            shape(condition.shape, F32), shape((extent // 8, 6 * width), F32), shape((6 * width // 8,), F32),
            shape((width // 8,), F32), shape((width // 8,), F32), shape((ff // 8,), F32), shape((width // 8,), F32),
        ]
        out_specs += [vmem] * len(FINALS)
    else:
        names += PARTIALS
        out_shape += [shape((2, 16, 16, half), F32), shape((2, 16, 8, half), F32)]
        out_specs += [hbm] * len(PARTIALS)
    buffers = kernel_buffers(span, width, extent, ff)
    names += tuple(buffers)
    outs = pl.pallas_call(
        functools.partial(layer_kernel, leftover, names),
        out_shape=tuple(out_shape),
        in_specs=[hbm] * 7 + [vmem] * 8,
        out_specs=tuple(out_specs),
        scratch_shapes=list(buffers.values()),
        compiler_params=pltpu.CompilerParams(
            collective_id=0, has_side_effects=True, vmem_limit_bytes=64 * 1024 * 1024 - 65536
        ),
        name="layer",
    )(
        tokens, cotangent, adaptive, mixer, projection, expand, contract,
        condition, shifts, prenorm, postnorm, offsets, baseline, jnp.asarray(cosine), jnp.asarray(sine),
    )
    layer_output, grad_tokens = outs[0], outs[1]
    grad_expand, grad_contract, grad_projection, grad_mixer = (part.astype(F32) for part in outs[2:6])
    if leftover == 1:
        grad_time, grad_adaptive, grad_shifts, grad_prenorm, grad_postnorm, grad_offsets, grad_baseline = outs[7:]
        return (
            layer_output, grad_tokens, grad_time, grad_adaptive, grad_shifts, grad_prenorm, grad_mixer,
            grad_projection, grad_postnorm, grad_expand, grad_offsets, grad_contract, grad_baseline,
        )

    w = lax.axis_index("wide")

    def among_groups(part):
        size = part.shape[0]
        whole = jnp.zeros((8 * size,) + part.shape[1:], F32)
        whole = lax.dynamic_update_slice_in_dim(whole, part, lax.div(w, leftover) * size, axis=0)
        return lax.psum_scatter(whole, "wide", scatter_dimension=0, tiled=True)

    grad_expand, grad_contract, grad_projection, grad_mixer = (
        among_groups(part) for part in (grad_expand, grad_contract, grad_projection, grad_mixer)
    )
    all_a, all_b = outs[7], outs[8]
    every = jnp.concatenate([all_b, all_a], axis=2)
    every = every.transpose(1, 2, 0, 3).reshape(2, 8, 24, width)
    every = every.transpose(1, 0, 2, 3)
    mine = lax.dynamic_slice_in_dim(every, lax.div(w, leftover), 1, axis=0)[0]
    every = lax.all_gather(mine, "wide", axis=0, tiled=True)
    sections = [0, 1, 8, 9, 10, 11]
    grad_mod = jnp.concatenate([every[:, r] for r in sections], axis=-1)
    silu_all = every[:, 18, :extent]
    highest = lax.Precision.HIGHEST
    own_rows = extent // wide_count
    grad_adaptive = jnp.dot(
        lax.dynamic_slice_in_dim(silu_all, w * own_rows, own_rows, axis=1).T, grad_mod, precision=highest
    )
    sums = jnp.sum(every, axis=0)

    def own(vector):
        size = vector.shape[0] // wide_count
        return lax.dynamic_slice_in_dim(vector, w * size, size)

    here = lax.dynamic_slice_in_dim(grad_mod, w * rows, rows, axis=0)
    _, silu_back = jax.vjp(jax.nn.silu, condition)
    (grad_time,) = silu_back(jnp.dot(here, adaptive.astype(F32).T, precision=highest))
    return (
        layer_output, grad_tokens, grad_time, grad_adaptive, own(jnp.sum(grad_mod, axis=0)), own(sums[2]),
        grad_mixer, grad_projection, own(sums[12]), grad_expand, own(sums[14:18].reshape(-1)), grad_contract,
        own(sums[13]),
    )


def solution(mesh):
    rows = P("wide", "seq", None)
    by_wide = P("wide", None)
    in_specs = (rows, by_wide, rows) + (P(),) * 10
    out_specs = (
        rows, rows, by_wide, by_wide, P("wide"), P("wide"), by_wide, by_wide, P("wide"), by_wide, P("wide"),
        by_wide, P("wide"),
    )
    return jax.shard_map(
        functools.partial(local_part, mesh.shape["wide"]),
        mesh=mesh, in_specs=in_specs, out_specs=out_specs, check_vma=False,
    )
```

```python
import functools
import itertools
import math
import types

import jax
import jax.numpy as jnp
import numpy as np
from jax import lax
from jax.experimental import pallas as pl
from jax.experimental.pallas import tpu as pltpu
from jax.sharding import PartitionSpec as P

F32 = jnp.float32
BF16 = jnp.bfloat16
MESH = pl.DeviceIdType.MESH
HDIM = 64
PAIR = 2 * HDIM
EPSILON = 1e-06
GELU_A = 0.7978845608
GELU_B = 0.044715

ROWS_BY_ROWS = (((1,), (1,)), ((), ()))
COLS_BY_COLS = (((0,), (0,)), ((), ()))


def dot(a, b, dims=None):
    if dims is None:
        return jnp.dot(a, b, preferred_element_type=F32)
    return lax.dot_general(a, b, dims, preferred_element_type=F32)


def normalize(values):
    center = values - jnp.mean(values, axis=-1, keepdims=True)
    scale = lax.rsqrt(jnp.mean(center * center, axis=-1, keepdims=True) + EPSILON)
    return center * scale, scale


def normalize_back(grad, normal, scale):
    first = jnp.mean(grad, axis=-1, keepdims=True)
    second = jnp.mean(grad * normal, axis=-1, keepdims=True)
    return scale * (grad - first - normal * second)


def turn(values):
    lane = lax.broadcasted_iota(jnp.int32, values.shape, 1)
    first = lax.rem(lane, HDIM) < HDIM // 2
    return jnp.where(
        first, pltpu.roll(values, PAIR - HDIM // 2, 1), pltpu.roll(values, HDIM // 2, 1)
    )


def column_sum(values):
    return jnp.sum(values, axis=0, keepdims=True)


def kernel_buffers(span, width, extent, ff):
    total = 4 * span
    half = width // 2
    pairs = half // PAIR
    uf = ff // 2
    ub = uf // 2
    strip = width // 16
    block = ff // 16
    V = pltpu.VMEM
    piece = (2, span, width)
    whole = (total, width)
    two = lambda n: (2,) * n
    wide_strip = (strip, width)
    half_strip = (strip, half)
    tall = (block, half)
    return dict(
        tok=V(piece, BF16), cot=V(piece, BF16), adap=V((extent, 6 * width), BF16),
        mix=V((width, 3 * half), BF16), proj=V((width, width), BF16), exp=V((width, uf), BF16),
        con=V((uf, width), BF16), mod=V((8, width), F32),
        hid_a=V(whole, BF16), qq=V((pairs, total, PAIR), BF16), kk=V((pairs, total, PAIR), BF16),
        vv=V((pairs, total, PAIR), BF16), q_t=V((half, total), BF16),
        lse=V((pairs, total, PAIR), F32),
        att_s=V((pairs, total, PAIR), BF16), att=V(piece, BF16),
        branch=V(piece, BF16), middle=V(piece, F32), hid_f=V(whole, BF16), gnar=V(whole, BF16),
        gbr=V(whole, BF16), act=V((total, ub), BF16), gwid=V((total, ub), BF16),
        nacc=V(whole, F32), hacc=V(whole, F32), nsend=V(piece, BF16),
        hsend=V(piece, BF16), hrecv=V(piece, BF16),
        dom_t=V((PAIR, total), BF16), dsum=V((total, PAIR), F32),
        dv_t=V((PAIR, total), F32), dk_t=V((PAIR, total), F32), dq=V((total, PAIR), F32),
        ge=V((2,) + two(4) + wide_strip, BF16), gc=V(two(4) + tall, BF16), gcs=V(two(2) + tall, BF16),
        gp=V(two(4) + half_strip, BF16), gps=V(two(3) + half_strip, BF16),
        e1=V((2,) + two(3) + wide_strip, BF16), e2=V((2,) + two(2) + wide_strip, BF16),
        e3=V((2,) + two(1) + wide_strip, BF16), e4=V((2,) + wide_strip, BF16),
        c1=V(two(3) + tall, BF16), c2=V(two(2) + tall, BF16), c3=V(two(1) + tall, BF16), c4=V(tall, BF16),
        p1=V(two(3) + half_strip, BF16), p2=V(two(2) + half_strip, BF16), p3=V(two(1) + half_strip, BF16),
        p4=V(half_strip, BF16),
        m1=V((pairs, 8 * strip, half), BF16), m2=V((pairs, 4 * strip, half), BF16),
        m3=V((pairs, 2 * strip, half), BF16), m4=V((pairs,) + half_strip, BF16),
        ag_e=V(two(3) + wide_strip, BF16), ag_c=V(two(2) + tall, BF16),
        ag_m=V(two(2) + (pairs + 1,) + half_strip, BF16),
        va=V((2, 16, half), F32), vb=V((2, 8, half), F32), va_r=V((16, half), F32), vb_r=V((8, half), F32),
        all_a=V((2, 16, 16, half), F32), all_b=V((2, 16, 8, half), F32), st=V((extent, 16), F32),
        back=V((extent, 8), F32), total=V((1, 6 * width), F32),
        cosine=V((total, PAIR), F32), sine=V((total, PAIR), F32), cond=V((2, extent), F32),
        shifts=V((6 * width,), F32), prenorm=V((width,), F32), postnorm=V((width,), F32),
        offsets=V((ff,), F32), baseline=V((width,), F32),
        lsem=pltpu.SemaphoreType.DMA((64,)),
        ssem=pltpu.SemaphoreType.DMA((100,)), rsem=pltpu.SemaphoreType.DMA((100,)),
    )


ORDERS = {
    "E0": ("y", "x", "z", "q"),
    "E1": ("z", "x", "y", "q"),
    "P": ("z", "y", "x", "q"),
    "M0": ("x", "z", "y", "q"),
    "M1": ("z", "x", "y", "q"),
    "M2": ("x", "z", "y", "q"),
    "C": (("x", "y"), ("y", "x")),
    "out": "b13",
}
SCHEDULE = (
    ("f2", ("C0s",)),
    ("n1", ("C1s",)),
    ("gp", ("E0.0",)),
    ("b00", ("Ps",)),
    ("b01", ("gaC",)),
    ("b02", ("C0.0", "E1.0")),
    ("b10", ("E0.1", "P.0")),
    ("b11", ("ga0", "C1.0")),
    ("b13", ("E0.2",)),
    ("b20", ("C0.1", "P.1", "M0.0")),
    ("b21", ("ga1", "E1.1", "E0.3", "M1.0")),
    ("b22", ("P.2",)),
    ("b23", ("M0.1", "C1.1")),
    ("l0", ("E1.2",)),
    ("l1", ("P.3", "M0.2", "M1.1")),
    ("tail", (
        "ga2", "gbC", "M2.0", "C.2", "M0.3", "E1.3", "M1.2", "gb0",
        "gb1", "M2.1", "ga3", "M1.3", "gaF", "gb2", "C.3", "agE",
        "M2.2", "gb3", "agEc", "agP", "M2.3", "gbF", "agPc", "agC",
        "agM", "agMc", "agCc",
    )),
)

INPUTS = (
    "tok_h", "cot_h", "adap_h", "mix_h", "proj_h", "exp_h", "con_h",
    "cond_h", "shifts_h", "prenorm_h", "postnorm_h", "offsets_h", "baseline_h", "cosine_h", "sine_h",
)
GRADS = ("out_h", "gtok_h", "oe_h", "oc_h", "op_h", "om_h")
FINALS = ("time_o", "adaptive_o", "shifts_o", "prenorm_o", "postnorm_o", "offsets_o", "baseline_o")
PARTIALS = ("all_a_h", "all_b_h")


def layer_kernel(leftover, names, *refs):
    R = types.SimpleNamespace(**dict(zip(names, refs)))
    R.nrecv = R.att
    span = R.tok.shape[1]
    width = R.tok.shape[2]
    total = R.hid_a.shape[0]
    half = width // 2
    pairs = half // PAIR
    blocks = total // span
    ub = R.exp.shape[1] // 2
    strip = width // 16
    block = ub // 4
    w = lax.axis_index("wide")
    s = lax.axis_index("seq")
    y = lax.div(s, 2)
    c = lax.rem(s, 2)
    hi = lax.div(w, leftover)
    b0 = lax.rem(hi, 2)
    b1 = lax.rem(lax.div(hi, 2), 2)
    b2 = lax.div(hi, 4)
    core_dev = (w, y * 2 + 1 - c)
    y_dev = (w, (1 - y) * 2 + c)
    dev0 = (w + leftover * (1 - 2 * b0), s)
    dev1 = (w + 2 * leftover * (1 - 2 * b1), s)
    dev2 = (w + 4 * leftover * (1 - 2 * b2), s)
    remote_count = itertools.count()
    local_count = itertools.count()
    sent = []

    def rows_of(p):
        return pl.ds(pl.multiple_of(p * span, span), span)

    def remote(src, dst, k, dev):
        return pltpu.make_async_remote_copy(
            src_ref=src, dst_ref=dst, send_sem=R.ssem.at[k], recv_sem=R.rsem.at[k],
            device_id=dev, device_id_type=MESH,
        )

    class Link:
        def __init__(self, item):
            self.item, self.open = item, False
            sent.append(self)

        def start(self):
            self.item.start()
            self.open = True

        def wait_recv(self):
            self.item.wait_recv()

        def wait_send(self):
            self.item.wait_send()
            self.open = False

    def link(src, dst, dev):
        return Link(remote(src, dst, next(remote_count), dev))

    def local(src, dst):
        return pltpu.make_async_copy(src, dst, R.lsem.at[next(local_count)])

    own_place = [rows_of(2 * j + c) for j in range(2)]
    other_place = [rows_of(2 * j + 1 - c) for j in range(2)]

    barrier = pltpu.get_barrier_semaphore()
    for dev in (core_dev, y_dev, dev0, dev1, dev2):
        pl.semaphore_signal(barrier, inc=1, device_id=dev, device_id_type=MESH)

    adap_load = local(R.adap_h, R.adap)
    tok_load = local(R.tok_h.at[y], R.tok.at[y])
    cot_load = local(R.cot_h.at[y], R.cot.at[y])
    first_loads = [
        local(getattr(R, name + "_h"), getattr(R, name))
        for name in ("cond", "shifts", "prenorm", "cosine", "sine", "postnorm", "offsets", "baseline")
    ]
    mix_loads = []
    for j in range(pairs):
        for b in range(3):
            mix_loads.append(local(
                R.mix_h.at[:, pl.ds(pl.multiple_of(b * width + c * half + j * PAIR, PAIR), PAIR)],
                R.mix.at[:, pl.ds((j * 3 + b) * PAIR, PAIR)],
            ))
    proj_load = local(R.proj_h, R.proj)
    exp_load = local(R.exp_h.at[:, pl.ds(pl.multiple_of(c * 2 * ub, PAIR), 2 * ub)], R.exp)
    con_load = local(R.con_h.at[pl.ds(pl.multiple_of(c * 2 * ub, PAIR), 2 * ub), :], R.con)
    for item in [adap_load, tok_load] + first_loads + mix_loads:
        item.start()

    tok_swap = link(R.tok_h.at[1 - y], R.tok.at[y], y_dev)
    cot_swap = link(R.cot_h.at[1 - y], R.cot.at[y], y_dev)
    hid_a_push = []
    for j in (y, 1 - y):
        place = rows_of(2 * j + c)
        hid_a_push.append(link(R.hid_a.at[place, :], R.hid_a.at[place, :], core_dev))
    gnar_base = next(remote_count)
    next(remote_count)
    gnar_push = [Link(remote(R.gnar.at[p, :], R.gnar.at[p, :], gnar_base + j, core_dev)) for j, p in enumerate(own_place)]
    hid_f_base = next(remote_count)
    next(remote_count)
    hid_f_push = [Link(remote(R.hid_f.at[p, :], R.hid_f.at[p, :], hid_f_base + j, core_dev)) for j, p in enumerate(own_place)]
    att_base = next(remote_count)
    for _ in range(2 * pairs - 1):
        next(remote_count)
    hsum_base = next(remote_count)
    next(remote_count)
    nsum_base = next(remote_count)
    next(remote_count)
    hsum_push = [Link(remote(R.hsend.at[j], R.hrecv.at[j], hsum_base + j, core_dev)) for j in range(2)]
    nsum_push = [Link(remote(R.nsend.at[j], R.nrecv.at[j], nsum_base + j, core_dev)) for j in range(2)]
    gbr_push = [link(R.gbr.at[p, :], R.gbr.at[p, :], core_dev) for p in own_place]
    asum_push = [link(R.hsend.at[j], R.hrecv.at[j], core_dev) for j in range(2)]
    def stage(n, j):
        return R.gwid.at[pl.ds(pl.multiple_of((2 * n + j) * span, span), span), :]

    out_push = link(stage(0, 1 - y), R.out_h.at[y], y_dev)
    gtok_push = link(stage(1, 1 - y), R.gtok_h.at[y], y_dev)

    class Halving:
        def __init__(self, acc, steps):
            self.acc = acc
            self.steps = []
            place = ()
            for bit, dev, recv in steps:
                self.steps.append((link(acc.at[place + (1 - bit,)], recv, dev), place + (bit,), recv))
                place = place + (bit,)

        def send(self, t):
            self.steps[t][0].start()

        def land(self, t, into=None):
            _, place, recv = self.steps[t]
            value = self.acc.at[place][...] + recv[...]
            if into is None:
                self.acc.at[place][...] = value
            else:
                into[...] = value

    class Strips:
        def __init__(self, ref, lanes):
            self.ref, self.lanes = ref, lanes

        @property
        def at(self):
            return self

        def __getitem__(self, bits):
            start = 0
            for n, bit in enumerate(bits):
                start = start + bit * (8 >> n)
            rows = (16 >> len(bits)) * strip
            return self.ref.at[pl.ds(pl.multiple_of(start * strip, strip), rows), self.lanes]

    step_of = dict(x=(b0, dev0), y=(y, y_dev), z=(b1, dev1), q=(b2, dev2))

    def steps_of(order, recvs):
        return [step_of[key] + (recv,) for key, recv in zip(order, recvs)]

    sums = {
        "E0": Halving(R.ge.at[0], steps_of(ORDERS["E0"], [r.at[0] for r in (R.e1, R.e2, R.e3, R.e4)])),
        "E1": Halving(R.ge.at[1], steps_of(ORDERS["E1"], [r.at[1] for r in (R.e1, R.e2, R.e3, R.e4)])),
        "P": Halving(R.gp, steps_of(ORDERS["P"], (R.p1, R.p2, R.p3, R.p4))),
    }
    for j in range(pairs):
        sums[f"M{j}"] = Halving(
            Strips(R.exp, pl.ds(j * half, half)),
            steps_of(ORDERS[f"M{j}"], [r.at[j] for r in (R.m1, R.m2, R.m3, R.m4)]),
        )
    links, lands = {}, {}
    finals = {
        "E0": R.ag_e.at[c, y, 0], "E1": R.ag_e.at[c, y, 1], "P": R.ag_m.at[c, y, 0],
        **{f"M{j}": R.ag_m.at[c, y, 1 + j] for j in range(pairs)},
    }
    for name, item in sums.items():
        for t in range(4):
            links[f"{name}.{t}"] = item.steps[t][0]
            lands[f"{name}.{t}"] = functools.partial(item.land, t, finals[name] if t == 3 else None)

    everything = slice(None)

    def place_c(i, **bits):
        return (bits.get("x", everything), bits.get("y", everything), i)

    def land_c(link_name, place, recv):
        def run():
            R.gc[place] = R.gc[place] + recv[...]

        lands[link_name] = run

    def link_c(name, send_place, keep_place, recv, dev):
        links[name] = link(R.gc.at[send_place], recv, dev)
        land_c(name, keep_place, recv)

    own_bit = dict(x=b0, y=y)
    plan_c = ORDERS["C"]
    for i in range(2):
        links[f"C{i}s"] = link(R.gcs, R.gc.at[:, :, i, c], core_dev)
        lands[f"C{i}s"] = lambda: None
        one, two = plan_c[i]
        link_c(
            f"C{i}.0", place_c(i, **{one: 1 - own_bit[one]}), place_c(i, **{one: own_bit[one]}),
            R.c1.at[i], step_of[one][1],
        )
        if len(plan_c) == 2:
            link_c(
                f"C{i}.1", place_c(i, **{one: own_bit[one], two: 1 - own_bit[two]}), place_c(i, **own_bit),
                R.c2.at[i], step_of[two][1],
            )
    if len(plan_c) == 2:
        link_c("C.2", place_c(1 - b1, **own_bit), place_c(b1, **own_bit), R.c3, dev1)
    else:
        link_c(
            "C.1", place_c(1 - b1, **{one: own_bit[one]}), place_c(b1, **{one: own_bit[one]}), R.c2, dev1
        )
        link_c(
            "C.2", place_c(b1, **{one: own_bit[one], two: 1 - own_bit[two]}), place_c(b1, **own_bit),
            R.c3, step_of[two][1],
        )
    links["C.3"] = link(R.gc.at[b0, y, b1, 1 - b2], R.c4, dev2)

    def land_c3():
        R.ag_c[c, y] = R.gc[b0, y, b1, b2] + R.c4[...]

    lands["C.3"] = land_c3
    links["Ps"] = link(R.gps, R.gp.at[:, :, :, c], core_dev)
    most, last = pl.ds(0, pairs), pl.ds(pairs, 1)
    for name, mine, both in (
        ("agE", R.ag_e.at[c, y], R.ag_e.at[c]),
        ("agC", R.ag_c.at[c, y], R.ag_c.at[c]),
        ("agP", R.ag_m.at[c, y, most], R.ag_m.at[c, :, most]),
        ("agM", R.ag_m.at[c, y, last], R.ag_m.at[c, :, last]),
    ):
        links[name] = link(mine, mine, y_dev)
        links[name + "c"] = link(both, both, core_dev)

    chip = b0 * 8 + b2 * 4 + b1 * 2 + y

    def land_total(part, recv, every):
        def run():
            every[c, chip] = part[c] + recv[...]

        return run

    for name, part, recv, every in (("ga", R.va, R.va_r, R.all_a), ("gb", R.vb, R.vb_r, R.all_b)):
        links[name + "C"] = link(part.at[1 - c], recv, core_dev)
        lands[name + "C"] = land_total(part, recv, every)
        for t, dev in enumerate((y_dev, dev1, dev2, dev0)):
            size = 2**t
            ref = every.at[c, pl.ds(lax.div(chip, size) * size, size)]
            links[f"{name}{t}"] = link(ref, ref, dev)
        links[name + "F"] = link(every.at[c], every.at[c], core_dev)

    sequence = [name for _, landed in SCHEDULE for name in landed]
    follow = {"C0s": "C0.0", "C1s": "C1.0", "Ps": "P.0", "C.2": "C.3", "C.3": "agC"}
    for name in ("agE", "agC", "agP", "agM"):
        follow[name] = name + "c"
    for name in ("ga", "gb"):
        for one, two in zip("C0123", "0123F"):
            follow[name + one] = name + two
    for name in sums:
        for t in range(3):
            follow[f"{name}.{t}"] = f"{name}.{t + 1}"
    if len(plan_c) == 2:
        follow.update({"C0.0": "C0.1", "C1.0": "C1.1"})
        joined = [(("C0.1", "C1.1"), "C.2")]
    else:
        follow["C.1"] = "C.2"
        joined = [(("C0.0", "C1.0"), "C.1")]
    joined += [(("E0.3", "E1.3"), "agE"), (("P.3", "M0.3", "M1.3"), "agP"), (("M2.3",), "agM")]
    for names_in, name in joined:
        follow[max(names_in, key=sequence.index)] = name

    def serve(name):
        links[name].wait_recv()
        if name in lands:
            lands[name]()
        if name in follow:
            links[follow[name]].start()

    def service(point):
        for name in dict(SCHEDULE).get(point, ()):
            if name == "out":
                continue
            serve(name)

    def add_row(ref, r, value):
        for n in range(2):
            ref[n, pl.ds(r, 1), :] += value[:, n * half : (n + 1) * half]

    pl.semaphore_wait(barrier, 5)
    tok_swap.start()
    for item in (cot_load, proj_load, exp_load, con_load):
        item.start()
    R.va[...] = jnp.zeros_like(R.va)
    R.vb[...] = jnp.zeros_like(R.vb)

    adap_load.wait()
    for item in first_loads:
        item.wait()
    crow = jnp.where(y == 0, R.cond[0:1, :], R.cond[1:2, :])
    crow = crow * (1.0 / (1.0 + jnp.exp(-crow)))
    extent = crow.shape[1]
    R.va[0, 10:11, :extent] = crow * (1 - c).astype(F32)
    eye = lax.broadcasted_iota(jnp.int32, (extent, extent), 0) == lax.broadcasted_iota(
        jnp.int32, (extent, extent), 1
    )
    ccol = jnp.sum(jnp.where(eye, jnp.broadcast_to(crow, (extent, extent)), 0.0), axis=1, keepdims=True)
    shifts = R.shifts[...].reshape(1, 6 * width)
    for n in range(6):
        part = pl.ds(n * width, width)
        R.mod[n : n + 1, :] = column_sum(R.adap[:, part].astype(F32) * ccol) + shifts[:, n * width : (n + 1) * width]
    pregain = R.prenorm[...].reshape(1, width)
    postgain = R.postnorm[...].reshape(1, width)

    def first_norm(j, t):
        normal, _ = normalize(R.tok[j].astype(F32))
        value = normal * (pregain * (1.0 + R.mod[1:2, :])) + R.mod[0:1, :]
        R.hid_a[rows_of(2 * j + c), :] = value.astype(BF16)
        hid_a_push[t].start()

    def project(p):
        place = rows_of(p)
        mixed = dot(R.hid_a[place, :], R.mix[...])
        cos_here = R.cosine[place, :]
        sin_here = R.sine[place, :]
        for j in range(pairs):
            base = j * 3 * PAIR
            query = mixed[:, base : base + PAIR]
            query = (query * cos_here + turn(query) * sin_here).astype(BF16) * jnp.asarray(
                HDIM ** (-0.5), BF16
            )
            R.qq[j, place, :] = query
            key = mixed[:, base + PAIR : base + 2 * PAIR]
            R.kk[j, place, :] = (key * cos_here + turn(key) * sin_here).astype(BF16)
            R.vv[j, place, :] = mixed[:, base + 2 * PAIR : base + 3 * PAIR].astype(BF16)

    tok_load.wait()
    first_norm(y, 0)
    for item in mix_loads:
        item.wait()
    project(2 * y + c)
    tok_swap.wait_recv()
    first_norm(1 - y, 1)
    hid_a_push[0].wait_recv()
    project(2 * y + 1 - c)
    project(2 * (1 - y) + c)
    hid_a_push[1].wait_recv()
    project(2 * (1 - y) + 1 - c)
    for j in range(pairs):
        R.q_t[j * PAIR : (j + 1) * PAIR, :] = R.qq[j].T

    cot_swap.start()
    def att_push(j, jj):
        lanes = pl.ds(pl.multiple_of(c * half + j * PAIR, PAIR), PAIR)
        return remote(
            R.att_s.at[j, other_place[jj], :], R.att.at[jj, :, lanes], att_base + 2 * j + jj, core_dev
        )

    lane_pair = lax.broadcasted_iota(jnp.int32, (span, PAIR), 1)
    lane_long = lax.broadcasted_iota(jnp.int32, (total, PAIR), 1)

    def in_head(lane, hh):
        return lane < HDIM if hh == 0 else lane >= HDIM

    def attend(j, carry):
        def score_of(hh, qb):
            query = R.qq[j, qb * span : (qb + 1) * span, :]
            query = jnp.where(in_head(lane_pair, hh), query, jnp.zeros_like(query))
            return dot(query, R.kk[j], ROWS_BY_ROWS)

        values = []
        for hh in range(2):
            there = R.vv[j]
            values.append(jnp.where(in_head(lane_long, hh), there, jnp.ones_like(there)))
        steps = [(hh, qb) for hh in range(2) for qb in range(blocks)]
        score = score_of(*steps[0])
        for index, (hh, qb) in enumerate(steps):
            following = score_of(*steps[index + 1]) if index + 1 < len(steps) else None
            place = slice(qb * span, (qb + 1) * span)
            top = jnp.max(score, axis=1, keepdims=True)
            low = jnp.exp(score - top).astype(BF16)
            grown = dot(low, values[hh])
            totals = pltpu.roll(grown, HDIM, 1)
            grown = (grown / totals).astype(BF16)
            weight = top + jnp.log(totals)
            if hh == 0:
                R.att_s[j, place, :] = grown
                R.lse[j, place, :] = weight
            else:
                R.att_s[j, place, :] = jnp.where(lane_pair < HDIM, R.att_s[j, place, :], grown)
                R.lse[j, place, :] = jnp.where(lane_pair < HDIM, R.lse[j, place, :], weight)
            score = following
        lanes = pl.ds(pl.multiple_of(c * half + j * PAIR, PAIR), PAIR)
        for jj in range(2):
            att_push(j, jj).start()
            R.att[jj, :, lanes] = R.att_s[j, own_place[jj], :]
        return carry

    lax.fori_loop(0, pairs, attend, 0)
    cot_load.wait()
    cot_swap.wait_recv()
    for j in range(2):
        low = (R.cot[j].astype(F32) * R.mod[5:6, :]).astype(BF16)
        R.gnar[own_place[j], :] = low
        add_row(R.va, 5, column_sum(low.astype(F32)))
        gnar_push[j].start()

    for j in range(pairs):
        for jj in range(2):
            att_push(j, jj).wait_recv()

    proj_load.wait()
    for j in range(2):
        grown = dot(R.att[j], R.proj[...])
        R.branch[j] = grown.astype(BF16)
        value = R.tok[j].astype(F32) + R.mod[2:3, :] * grown
        R.middle[j] = value
        normal, _ = normalize(value)
        R.hid_f[own_place[j], :] = (normal * (postgain * (1.0 + R.mod[4:5, :])) + R.mod[3:4, :]).astype(BF16)
        hid_f_push[j].start()

    def bits_of(n, order):
        bits = dict(q=n // 8, z=n // 4 % 2, x=n // 2 % 2, y=n % 2)
        return tuple(bits[key] for key in order)

    exp_load.wait()
    con_load.wait()
    offsets = R.offsets[...].reshape(1, 4 * ub)
    offsets = jnp.where(c == 0, offsets[:, : 2 * ub], offsets[:, 2 * ub :])
    for i in range(2):
        units = pl.ds(i * ub, ub)

        def feed(t, carry, i=i, units=units):
            late = lax.div(t, 2)
            j = lax.rem(t, 2)
            place = rows_of(2 * j + lax.rem(c + late + i, 2))
            if i == 0:
                @pl.when(late == 1)
                def _():
                    remote(R.hid_f.at[place, :], R.hid_f.at[place, :], hid_f_base + j, core_dev).wait_recv()
                    remote(R.gnar.at[place, :], R.gnar.at[place, :], gnar_base + j, core_dev).wait_recv()
            else:
                for k in range(1, 4):
                    if f"f{k - 1}" in dict(SCHEDULE):
                        @pl.when(t == k)
                        def _(k=k):
                            service(f"f{k - 1}")
            v = dot(R.hid_f[place, :], R.exp[:, units]) + offsets[:, i * ub : (i + 1) * ub]
            square = v * v
            th = jnp.tanh(v * (GELU_A + (GELU_A * GELU_B) * square))
            up = 0.5 + 0.5 * th
            low = (v * up).astype(BF16)
            R.act[place, :] = low
            slope = up + (v * (0.5 - 0.5 * th * th)) * (GELU_A + (3.0 * GELU_A * GELU_B) * square)
            grad = (dot(R.gnar[place, :], R.con[units, :], ROWS_BY_ROWS) * slope).astype(BF16)
            R.gwid[place, :] = grad
            add_row(R.va, 6 + 2 * c + i, column_sum(grad.astype(F32)))
            n_part = dot(low, R.con[units, :])
            h_part = dot(grad, R.exp[:, units], ROWS_BY_ROWS)
            if i == 0:
                R.nacc[place, :] = n_part
                R.hacc[place, :] = h_part
            else:
                R.nacc[place, :] += n_part
                R.hacc[place, :] += h_part

                @pl.when(late == 0)
                def _():
                    R.hsend[j] = R.hacc[place, :].astype(BF16)
                    remote(R.hsend.at[j], R.hrecv.at[j], hsum_base + j, core_dev).start()
                    R.nsend[j] = R.nacc[place, :].astype(BF16)
                    remote(R.nsend.at[j], R.nrecv.at[j], nsum_base + j, core_dev).start()
            return carry

        lax.fori_loop(0, 4, feed, 0)
        if i == 1:
            for item in hsum_push + nsum_push:
                item.open = True
        value = dot(R.hid_f[...], R.gwid[...], COLS_BY_COLS).astype(BF16)
        for n in range(16):
            R.ge[(i,) + bits_of(n, ORDERS[f"E{i}"])] = value[n * strip : (n + 1) * strip]
        links[f"E{i}.0"].start()
        service(f"E{i}")
        value = dot(R.act[...], R.gnar[...], COLS_BY_COLS).astype(BF16)
        left, right = value[:, :half], value[:, half:]
        mine = jnp.where(c == 0, left, right)
        theirs = jnp.where(c == 0, right, left)
        if i == 1:
            service("f3")
            links["C0s"].wait_send()
        for n in range(4):
            a0, ay = n // 2, n % 2
            R.gcs[a0, ay] = theirs[n * block : (n + 1) * block]
            R.gc[a0, ay, i, c] = mine[n * block : (n + 1) * block]
        links[f"C{i}s"].start()
        service(f"C{i}")

    base_row = R.baseline[...].reshape(1, width)
    for j in range(2):
        place = own_place[j]
        hsum_push[j].wait_recv()
        got = R.hacc[place, :] + R.hrecv[j].astype(F32)
        normal, scale = normalize(R.middle[j])
        add_row(R.va, 1, column_sum(got))
        both = column_sum(got * normal)
        add_row(R.va, 2, both * postgain)
        add_row(R.va, 4, both * (1.0 + R.mod[4:5, :]))
        g = R.cot[j].astype(F32)
        nsum_push[j].wait_recv()
        narrowed = R.nacc[place, :] + R.nrecv[j].astype(F32) + base_row
        R.gwid[j * span : (j + 1) * span, :] = (R.middle[j] + R.mod[5:6, :] * narrowed).astype(BF16)
        add_row(R.va, 3, column_sum(g * narrowed))
        value = g + normalize_back(got * (postgain * (1.0 + R.mod[4:5, :])), normal, scale)
        R.middle[j] = value
        add_row(R.va, 0, column_sum(value * R.branch[j].astype(F32)))
        R.gbr[place, :] = (R.mod[2:3, :] * value).astype(BF16)
        gbr_push[j].start()
        if j == 0:
            service("n0")

    out_local = local(stage(0, y), R.out_h.at[y])
    out_local.start()
    links["gaC"].start()
    out_at = ORDERS["out"]
    if out_at == "n1":
        out_push.start()
    service("n1")
    for j in range(2):
        gbr_push[j].wait_recv()

    value = jnp.concatenate(
        [dot(R.att_s[j], R.gbr[...], COLS_BY_COLS).astype(BF16) for j in range(pairs)], axis=0
    )
    left, right = value[:, :half], value[:, half:]
    mine = jnp.where(c == 0, left, right)
    theirs = jnp.where(c == 0, right, left)
    for n in range(8):
        place = bits_of(n, ORDERS["P"][:3])
        R.gps[place] = theirs[n * strip : (n + 1) * strip]
        R.gp[place + (c,)] = mine[n * strip : (n + 1) * strip]
    links["Ps"].start()
    own_proj = R.proj[pl.ds(pl.multiple_of(c * half, PAIR), half), :]
    grown = dot(R.gbr[...], own_proj, ROWS_BY_ROWS).astype(BF16)
    for j in range(pairs):
        R.act[:, half + j * PAIR : half + (j + 1) * PAIR] = grown[:, j * PAIR : (j + 1) * PAIR]

    if out_at == "gp":
        out_push.start()
    service("gp")


    def service_pair(j, point):
        for k in range(pairs):
            key = f"b{k}{point}"
            if key == out_at or key in dict(SCHEDULE):
                @pl.when(j == k)
                def _(key=key):
                    if key == out_at:
                        out_push.start()
                    service(key)

    def attend_back(j, carry):
        grown = R.act[:, pl.ds(pl.multiple_of(half + j * PAIR, PAIR), PAIR)].astype(F32)
        product = grown * R.att_s[j].astype(F32)
        inner = [
            jnp.sum(jnp.where(in_head(lane_long, hh), product, 0.0), axis=1, keepdims=True) for hh in range(2)
        ]
        R.dsum[...] = jnp.where(in_head(lane_long, 0), inner[0], inner[1])
        R.dom_t[...] = grown.astype(BF16).T

        lanes = pl.ds(pl.multiple_of(half + j * PAIR, PAIR), PAIR)

        def one_head(value, hh):
            return jnp.where(in_head(lane_pair, hh), value, jnp.zeros_like(value))

        def products(hh, qb):
            rows = slice(qb * span, (qb + 1) * span)
            grad = dot(one_head(R.act[rows, lanes], hh), R.vv[j], ROWS_BY_ROWS)
            return grad, dot(one_head(R.qq[j, rows, :], hh), R.kk[j], ROWS_BY_ROWS)

        steps = [(hh, qb) for hh in range(2) for qb in range(blocks)]
        current = products(*steps[0])
        for index, (hh, qb) in enumerate(steps):
            following = products(*steps[index + 1]) if index + 1 < len(steps) else None
            grad, score = current
            place = slice(qb * span, (qb + 1) * span)
            rows = slice(hh * HDIM, (hh + 1) * HDIM)
            first = hh * HDIM
            weight = jnp.exp(score - R.lse[j, place, first : first + 1])
            low = weight.astype(BF16)
            grad = (weight * (grad - R.dsum[place, first : first + 1])).astype(BF16)
            q_part = dot(grad, R.kk[j])
            v_part = dot(R.dom_t[rows, place], low)
            k_part = dot(R.q_t[pl.ds(pl.multiple_of(j * PAIR + hh * HDIM, HDIM), HDIM), place], grad)
            if hh == 0:
                R.dq[place, :] = q_part
            else:
                R.dq[place, :] = jnp.where(lane_pair < HDIM, R.dq[place, :], q_part)
            if qb == 0:
                R.dv_t[rows, :] = v_part
                R.dk_t[rows, :] = k_part
            else:
                R.dv_t[rows, :] += v_part
                R.dk_t[rows, :] += k_part
            if qb == blocks - 1:
                service_pair(j, hh)
            current = following
        gq = R.dq[...] * HDIM ** (-0.5)
        gk = R.dk_t[...].T
        gmx = R.act.at[:, pl.ds(0, 3 * PAIR)]
        gmx[:, :PAIR] = (gq * R.cosine[...] - turn(gq) * R.sine[...]).astype(BF16)
        gmx[:, PAIR : 2 * PAIR] = (gk * R.cosine[...] - turn(gk) * R.sine[...]).astype(BF16)
        gmx[:, 2 * PAIR :] = R.dv_t[...].astype(BF16).T
        value = dot(R.hid_a[...], gmx[...], COLS_BY_COLS).astype(BF16)
        for k in range(pairs):
            @pl.when(j == k)
            def _(k=k):
                for n in range(16):
                    index = 0
                    for bit in bits_of(n, ORDERS[f"M{k}"]):
                        index = 2 * index + bit
                    R.exp[index * strip : (index + 1) * strip, k * half : (k + 1) * half] = value[
                        n * strip : (n + 1) * strip
                    ]
                links[f"M{k}.0"].start()
        service_pair(j, 2)
        lanes = pl.ds(pl.multiple_of(j * 3 * PAIR, PAIR), 3 * PAIR)

        def back(p, inner):
            place = rows_of(p)
            part = dot(gmx[place, :], R.mix[:, lanes], ROWS_BY_ROWS)

            @pl.when(j == 0)
            def _():
                R.hacc[place, :] = part

            @pl.when(j > 0)
            def _():
                R.hacc[place, :] += part

            return inner

        lax.fori_loop(0, blocks, back, 0)
        service_pair(j, 3)
        return carry

    lax.fori_loop(0, pairs, attend_back, 0)
    for j in range(2):
        hsum_push[j].wait_send()
        R.hsend[j] = R.hacc[other_place[j], :].astype(BF16)
        asum_push[j].start()

    gtok_local = local(stage(1, y), R.gtok_h.at[y])
    for j, item in ((1 - y, gtok_push), (y, gtok_local)):
        got = R.hacc[rows_of(2 * j + c), :] + 0.0
        if item is gtok_push:
            asum_push[0].wait_recv()
            asum_push[1].wait_recv()
        got = got + R.hrecv[j].astype(F32)
        normal, scale = normalize(R.tok[j].astype(F32))
        add_row(R.vb, 0, column_sum(got))
        both = column_sum(got * normal)
        add_row(R.vb, 1, both * pregain)
        add_row(R.vb, 2, both * (1.0 + R.mod[1:2, :]))
        stage(1, j)[...] = (
            R.middle[j] + normalize_back(got * (pregain * (1.0 + R.mod[1:2, :])), normal, scale)
        ).astype(BF16)
        item.start()
        if item is gtok_push:
            if out_at == "l0":
                out_push.start()
            service("l0")
    links["gbC"].start()
    service("l1")
    service("l2")

    stores = []

    def store(src, dst):
        item = local(src, dst)
        item.start()
        stores.append(item)

    def store_e():
        for n in range(8):
            cc, yy, i = n // 4, n // 2 % 2, n % 2
            store(
                R.ag_e.at[cc, yy, i],
                R.oe_h.at[pl.ds(yy * strip, strip), pl.ds((2 * cc + i) * width, width)],
            )

    def store_c():
        for n in range(4):
            cc, yy = n // 2, n % 2
            store(R.ag_c.at[cc, yy], R.oc_h.at[pl.ds(yy * block, block), pl.ds(cc * half, half)])

    def place_m(j):
        for n in range(4):
            cc, yy = n // 2, n % 2
            value = R.ag_m[cc, yy, 1 + j]
            for b in range(3):
                lane = cc * half + j * PAIR
                row = (2 * b + yy) * strip
                R.hid_f[row : row + strip, lane : lane + PAIR] = value[:, b * PAIR : (b + 1) * PAIR]

    def store_p():
        for n in range(4):
            cc, yy = n // 2, n % 2
            store(R.ag_m.at[cc, yy, 0], R.op_h.at[pl.ds(yy * strip, strip), pl.ds(cc * half, half)])
        for item in hid_f_push:
            item.open = True
            item.wait_send()
        for j in range(pairs - 1):
            place_m(j)

    def store_m():
        place_m(pairs - 1)
        for b in range(3):
            store(R.hid_f.at[pl.ds(2 * b * strip, 2 * strip), :], R.om_h.at[:, pl.ds(b * width, width)])

    results = {"agEc": store_e, "agCc": store_c, "agPc": store_p, "agMc": store_m}
    if leftover == 1:
        early, later = finish_vectors(R, hi, chip - y, width, half, extent)
    else:
        early = [lambda: store(R.all_a, R.all_a_h)]
        later = [lambda: store(R.all_b, R.all_b_h)]
    pieces = []
    tail = dict(SCHEDULE)["tail"]
    if "gaF" not in tail:
        pieces.extend(early)
    for name in tail:
        serve(name)
        if name in results:
            results[name]()
        if name == "gaF":
            pieces.extend(early)
        if name == "gbF":
            pieces.extend(later)
        if pieces:
            pieces.pop(0)()
    for piece in pieces:
        piece()
    for item in stores:
        item.wait()
    out_local.wait()
    out_push.wait_recv()
    gtok_local.wait()
    gtok_push.wait_recv()
    for j in range(pairs):
        for jj in range(2):
            att_push(j, jj).wait_send()
    for item in sent:
        if item.open:
            item.wait_send()


def finish_vectors(R, hi, chip, width, half, extent):
    own = extent // 8
    highest = lax.Precision.HIGHEST
    sections = ((R.all_b, 0), (R.all_b, 1), (R.all_a, 0), (R.all_a, 1), (R.all_a, 2), (R.all_a, 3))

    def transpose():
        R.st[...] = R.all_a[0, :, 10, :extent].T
        R.back[...] = jnp.zeros_like(R.back)

    def section(n, h):
        ref, r = sections[n]
        grads = ref[h, :, r, :]
        lanes = pl.ds(n * width + h * half, half)
        silu_own = R.st[pl.ds(pl.multiple_of(hi * own, own), own), :]
        R.adaptive_o[:, lanes] = jnp.dot(silu_own, grads, precision=highest, preferred_element_type=F32)
        R.total[:, lanes] = column_sum(grads)
        table = R.adap[:, lanes].astype(F32)
        for yy in range(2):
            mine = ref[h, pl.ds(chip + yy, 1), r, :]
            R.back[:, yy : yy + 1] += jnp.sum(table * mine, axis=1, keepdims=True)

    def share(vector, out):
        size = vector.shape[1] // 8
        value = jnp.zeros((1, size), F32)
        for k in range(8):
            value = jnp.where(hi == k, vector[:, k * size : (k + 1) * size], value)
        out[...] = value.reshape(size)

    def total_of(ref, r):
        return jnp.concatenate([column_sum(ref[h, :, r, :]) for h in range(2)], axis=1)

    def vectors():
        share(total_of(R.all_a, 4), R.postnorm_o)
        share(jnp.concatenate([total_of(R.all_a, 6 + n) for n in range(4)], axis=1), R.offsets_o)
        share(total_of(R.all_a, 5), R.baseline_o)

    def last():
        share(total_of(R.all_b, 2), R.prenorm_o)
        share(R.total[...], R.shifts_o)
        eye = lax.broadcasted_iota(jnp.int32, (extent, extent), 0) == lax.broadcasted_iota(
            jnp.int32, (extent, extent), 1
        )
        for yy in range(2):
            back = jnp.broadcast_to(R.back[:, yy : yy + 1], (extent, extent))
            row = column_sum(jnp.where(eye, back, 0.0))
            cond = R.cond[yy : yy + 1, :]
            gate = 1.0 / (1.0 + jnp.exp(-cond))
            R.time_o[yy : yy + 1, :] = row * (gate * (1.0 + cond * (1.0 - gate)))

    early = [transpose] + [functools.partial(section, n, h) for n in range(2, 6) for h in range(2)] + [vectors]
    later = [functools.partial(section, n, h) for n in range(2) for h in range(2)] + [last]
    return early, later


def finish_kernel(count, *refs):
    sums, others, refs = refs[:4], refs[4 : 4 + count], refs[4 + count :]
    sum_outs, other_outs, refs = refs[:4], refs[4 : 4 + count], refs[4 + count :]
    low, high, sem = refs[:4], refs[4:8], refs[8]
    loads = [pltpu.make_async_copy(a, b, sem.at[n]) for n, (a, b) in enumerate(zip(sums, low))]
    copies = [pltpu.make_async_copy(a, b, sem.at[8 + n]) for n, (a, b) in enumerate(zip(others, other_outs))]
    stores = [pltpu.make_async_copy(a, b, sem.at[4 + n]) for n, (a, b) in enumerate(zip(high, sum_outs))]
    for item in loads + copies:
        item.start()
    for n in range(4):
        loads[n].wait()
        high[n][...] = low[n][...].astype(F32)
        stores[n].start()
    for item in stores + copies:
        item.wait()


def finish(sums, others):
    hbm = pl.BlockSpec(memory_space=pl.ANY)
    shape = jax.ShapeDtypeStruct
    return pl.pallas_call(
        functools.partial(finish_kernel, len(others)),
        out_shape=tuple(shape(v.shape, F32) for v in sums) + tuple(shape(v.shape, v.dtype) for v in others),
        in_specs=[hbm] * (4 + len(others)),
        out_specs=(hbm,) * (4 + len(others)),
        scratch_shapes=[pltpu.VMEM(v.shape, BF16) for v in sums] + [pltpu.VMEM(v.shape, F32) for v in sums]
        + [pltpu.SemaphoreType.DMA((8 + len(others),))],
        compiler_params=pltpu.CompilerParams(vmem_limit_bytes=60 * 1024 * 1024),
        name="finish",
    )(*sums, *others)


def rotary_constants(length):
    half_dim = HDIM // 2
    frequency = np.exp(np.arange(half_dim, dtype=np.float32) * np.float32(-2.0 * math.log(10000.0) / HDIM))
    angles = np.arange(length, dtype=np.float32)[:, None] * frequency[None, :].astype(np.float32)
    angles = angles.astype(np.float64)
    cosine = np.cos(angles).astype(np.float32)
    sine = np.sin(angles).astype(np.float32)
    cosine = np.concatenate([cosine] * 4, axis=-1)
    sine = np.concatenate([-sine, sine, -sine, sine], axis=-1)
    return cosine, sine


def local_part(wide_count, tokens, condition, cotangent, adaptive, shifts, prenorm, mixer, projection, postnorm,
               expand, offsets, contract, baseline):
    rows, span, width = tokens.shape
    total = 4 * span
    half = width // 2
    pairs = half // PAIR
    ff = expand.shape[1]
    extent = adaptive.shape[0]
    leftover = wide_count // 8
    cosine, sine = rotary_constants(total)
    hbm = pl.BlockSpec(memory_space=pl.ANY)
    vmem = pl.BlockSpec(memory_space=pltpu.VMEM)
    shape = jax.ShapeDtypeStruct
    out_shape = [
        shape(tokens.shape, BF16), shape(tokens.shape, BF16), shape((width // 8, ff), BF16),
        shape((ff // 8, width), BF16), shape((width // 8, width), BF16), shape((width // 8, 3 * width), BF16),
    ]
    out_specs = [hbm] * len(out_shape)
    names = INPUTS + GRADS
    if leftover == 1:
        names += FINALS
        out_shape += [
            shape(condition.shape, F32), shape((extent // 8, 6 * width), F32), shape((6 * width // 8,), F32),
            shape((width // 8,), F32), shape((width // 8,), F32), shape((ff // 8,), F32), shape((width // 8,), F32),
        ]
        out_specs += [vmem] * len(FINALS)
    else:
        names += PARTIALS
        out_shape += [shape((2, 16, 16, half), F32), shape((2, 16, 8, half), F32)]
        out_specs += [hbm] * len(PARTIALS)
    buffers = kernel_buffers(span, width, extent, ff)
    names += tuple(buffers)
    outs = pl.pallas_call(
        functools.partial(layer_kernel, leftover, names),
        out_shape=tuple(out_shape),
        in_specs=[hbm] * 15,
        out_specs=tuple(out_specs),
        scratch_shapes=list(buffers.values()),
        compiler_params=pltpu.CompilerParams(
            collective_id=0, has_side_effects=True, vmem_limit_bytes=64 * 1024 * 1024 - 65536
        ),
        name="layer",
    )(
        tokens, cotangent, adaptive, mixer, projection, expand, contract,
        condition, shifts, prenorm, postnorm, offsets, baseline, jnp.asarray(cosine), jnp.asarray(sine),
    )
    layer_output, grad_tokens = outs[0], outs[1]
    if leftover == 1:
        done = finish(outs[2:6], outs[:2] + outs[6:])
        grad_expand, grad_contract, grad_projection, grad_mixer = done[:4]
        layer_output, grad_tokens = done[4:6]
        grad_time, grad_adaptive, grad_shifts, grad_prenorm, grad_postnorm, grad_offsets, grad_baseline = done[6:]
        return (
            layer_output, grad_tokens, grad_time, grad_adaptive, grad_shifts, grad_prenorm, grad_mixer,
            grad_projection, grad_postnorm, grad_expand, grad_offsets, grad_contract, grad_baseline,
        )

    grad_expand, grad_contract, grad_projection, grad_mixer = (part.astype(F32) for part in outs[2:6])

    w = lax.axis_index("wide")

    def among_groups(part):
        size = part.shape[0]
        whole = jnp.zeros((8 * size,) + part.shape[1:], F32)
        whole = lax.dynamic_update_slice_in_dim(whole, part, lax.div(w, leftover) * size, axis=0)
        return lax.psum_scatter(whole, "wide", scatter_dimension=0, tiled=True)

    grad_expand, grad_contract, grad_projection, grad_mixer = (
        among_groups(part) for part in (grad_expand, grad_contract, grad_projection, grad_mixer)
    )
    all_a, all_b = outs[6], outs[7]
    every = jnp.concatenate([all_b, all_a], axis=2)
    every = every.reshape(2, 2, 2, 2, 2, 24, half).transpose(2, 3, 1, 4, 5, 0, 6).reshape(8, 2, 24, width)
    mine = lax.dynamic_slice_in_dim(every, lax.div(w, leftover), 1, axis=0)[0]
    every = lax.all_gather(mine, "wide", axis=0, tiled=True)
    sections = [0, 1, 8, 9, 10, 11]
    grad_mod = jnp.concatenate([every[:, r] for r in sections], axis=-1)
    silu_all = every[:, 18, :extent]
    highest = lax.Precision.HIGHEST
    own_rows = extent // wide_count
    grad_adaptive = jnp.dot(
        lax.dynamic_slice_in_dim(silu_all, w * own_rows, own_rows, axis=1).T, grad_mod, precision=highest
    )
    sums = jnp.sum(every, axis=0)

    def own(vector):
        size = vector.shape[0] // wide_count
        return lax.dynamic_slice_in_dim(vector, w * size, size)

    here = lax.dynamic_slice_in_dim(grad_mod, w * rows, rows, axis=0)
    _, silu_back = jax.vjp(jax.nn.silu, condition)
    (grad_time,) = silu_back(jnp.dot(here, adaptive.astype(F32).T, precision=highest))
    return (
        layer_output, grad_tokens, grad_time, grad_adaptive, own(jnp.sum(grad_mod, axis=0)), own(sums[2]),
        grad_mixer, grad_projection, own(sums[12]), grad_expand, own(sums[14:18].reshape(-1)), grad_contract,
        own(sums[13]),
    )


def solution(mesh):
    rows = P("wide", "seq", None)
    by_wide = P("wide", None)
    in_specs = (rows, by_wide, rows) + (P(),) * 10
    out_specs = (
        rows, rows, by_wide, by_wide, P("wide"), P("wide"), by_wide, by_wide, P("wide"), by_wide, P("wide"),
        by_wide, P("wide"),
    )
    return jax.shard_map(
        functools.partial(local_part, mesh.shape["wide"]),
        mesh=mesh, in_specs=in_specs, out_specs=out_specs, check_vma=False,
    )
```

```python
import functools
import itertools
import math
import types

import jax
import jax.numpy as jnp
import numpy as np
from jax import lax
from jax.experimental import pallas as pl
from jax.experimental.pallas import tpu as pltpu
from jax.sharding import PartitionSpec as P

F32 = jnp.float32
BF16 = jnp.bfloat16
MESH = pl.DeviceIdType.MESH
HDIM = 64
PAIR = 2 * HDIM
EPSILON = 1e-06
GELU_A = 0.7978845608
GELU_B = 0.044715

ROWS_BY_ROWS = (((1,), (1,)), ((), ()))
COLS_BY_COLS = (((0,), (0,)), ((), ()))


def dot(a, b, dims=None):
    if dims is None:
        return jnp.dot(a, b, preferred_element_type=F32)
    return lax.dot_general(a, b, dims, preferred_element_type=F32)


def normalize(values):
    center = values - jnp.mean(values, axis=-1, keepdims=True)
    scale = lax.rsqrt(jnp.mean(center * center, axis=-1, keepdims=True) + EPSILON)
    return center * scale, scale


def normalize_back(grad, normal, scale):
    first = jnp.mean(grad, axis=-1, keepdims=True)
    second = jnp.mean(grad * normal, axis=-1, keepdims=True)
    return scale * (grad - first - normal * second)


def turn(values):
    lane = lax.broadcasted_iota(jnp.int32, values.shape, 1)
    first = lax.rem(lane, HDIM) < HDIM // 2
    return jnp.where(
        first, pltpu.roll(values, PAIR - HDIM // 2, 1), pltpu.roll(values, HDIM // 2, 1)
    )


def column_sum(values):
    return jnp.sum(values, axis=0, keepdims=True)


def kernel_buffers(span, width, extent, ff):
    total = 4 * span
    half = width // 2
    pairs = half // PAIR
    uf = ff // 2
    ub = uf // 2
    strip = width // 16
    block = ff // 16
    V = pltpu.VMEM
    piece = (2, span, width)
    whole = (total, width)
    two = lambda n: (2,) * n
    wide_strip = (strip, width)
    half_strip = (strip, half)
    tall = (block, half)
    return dict(
        tok=V(piece, BF16), cot=V(piece, BF16), adap=V((extent, 6 * width), BF16),
        mix=V((width, 3 * half), BF16), proj=V((width, width), BF16), exp=V((width, uf), BF16),
        con=V((uf, width), BF16), mod=V((8, width), F32),
        hid_a=V(whole, BF16), qq=V((pairs, total, PAIR), BF16), kk=V((pairs, total, PAIR), BF16),
        vv=V((pairs, total, PAIR), BF16), q_t=V((half, total), BF16),
        lse=V((pairs, total, PAIR), F32),
        att_s=V((pairs, total, PAIR), BF16), att=V(piece, BF16),
        branch=V(piece, BF16), middle=V(piece, F32), hid_f=V(whole, BF16), gnar=V(whole, BF16),
        gbr=V(whole, BF16), act=V((total, ub), BF16), gwid=V((total, ub), BF16),
        nacc=V(whole, F32), hacc=V(whole, F32), nsend=V(piece, BF16),
        hsend=V(piece, BF16), hrecv=V(piece, BF16),
        dom_t=V((PAIR, total), BF16), dsum=V((total, PAIR), F32),
        dv_t=V((PAIR, total), F32), dk_t=V((PAIR, total), F32), dq=V((total, PAIR), F32),
        ge=V((2,) + two(4) + wide_strip, BF16), gc=V(two(4) + tall, BF16), gcs=V(two(2) + tall, BF16),
        gp=V(two(4) + half_strip, BF16), gps=V(two(3) + half_strip, BF16),
        e1=V((2,) + two(3) + wide_strip, BF16), e2=V((2,) + two(2) + wide_strip, BF16),
        e3=V((2,) + two(1) + wide_strip, BF16), e4=V((2,) + wide_strip, BF16),
        c1=V(two(3) + tall, BF16), c2=V(two(2) + tall, BF16), c3=V(two(1) + tall, BF16), c4=V(tall, BF16),
        p1=V(two(3) + half_strip, BF16), p2=V(two(2) + half_strip, BF16), p3=V(two(1) + half_strip, BF16),
        p4=V(half_strip, BF16),
        m1=V((pairs, 8 * strip, half), BF16), m2=V((pairs, 4 * strip, half), BF16),
        m3=V((pairs, 2 * strip, half), BF16), m4=V((pairs,) + half_strip, BF16),
        ag_e=V(two(3) + wide_strip, BF16), ag_c=V(two(2) + tall, BF16),
        ag_m=V(two(2) + (pairs + 1,) + half_strip, BF16),
        va=V((2, 16, half), F32), vb=V((2, 8, half), F32), va_r=V((16, half), F32), vb_r=V((8, half), F32),
        all_a=V((2, 16, 16, half), F32), all_b=V((2, 16, 8, half), F32), st=V((extent, 16), F32),
        back=V((extent, 8), F32), total=V((1, 6 * width), F32),
        cosine=V((total, PAIR), F32), sine=V((total, PAIR), F32), cond=V((2, extent), F32),
        shifts=V((6 * width,), F32), prenorm=V((width,), F32), postnorm=V((width,), F32),
        offsets=V((ff,), F32), baseline=V((width,), F32),
        lsem=pltpu.SemaphoreType.DMA((64,)),
        ssem=pltpu.SemaphoreType.DMA((100,)), rsem=pltpu.SemaphoreType.DMA((100,)),
    )


ORDERS = {
    "E0": ("y", "x", "z", "q"),
    "E1": ("z", "x", "y", "q"),
    "P": ("z", "y", "x", "q"),
    "M0": ("x", "z", "y", "q"),
    "M1": ("z", "x", "y", "q"),
    "M2": ("x", "z", "y", "q"),
    "C": (("x", "y"), ("y", "x")),
    "out": "b13",
}
SCHEDULE = (
    ("f2", ("C0s",)),
    ("n1", ("C1s",)),
    ("gp", ("E0.0",)),
    ("b00", ("Ps",)),
    ("b01", ("gaC",)),
    ("b02", ("C0.0", "E1.0")),
    ("b10", ("E0.1", "P.0")),
    ("b11", ("ga0", "C1.0")),
    ("b13", ("E0.2",)),
    ("b20", ("C0.1", "P.1", "M0.0")),
    ("b21", ("ga1", "E1.1", "E0.3", "M1.0")),
    ("b22", ("P.2",)),
    ("b23", ("M0.1", "C1.1")),
    ("l0", ("E1.2",)),
    ("l1", ("P.3", "M0.2", "M1.1")),
    ("tail", (
        "ga2", "gbC", "M2.0", "C.2", "M0.3", "E1.3", "M1.2", "gb0",
        "gb1", "M2.1", "ga3", "M1.3", "gaF", "gb2", "C.3", "agE",
        "M2.2", "gb3", "agEc", "agP", "M2.3", "gbF", "agPc", "agC",
        "agM", "agMc", "agCc",
    )),
)

INPUTS = (
    "tok_h", "cot_h", "adap_h", "mix_h", "proj_h", "exp_h", "con_h",
    "cond_h", "shifts_h", "prenorm_h", "postnorm_h", "offsets_h", "baseline_h", "cosine_h", "sine_h",
)
GRADS = ("out_h", "gtok_h", "oe_h", "oc_h", "op_h", "om_h")
FINALS = ("time_o", "adaptive_o", "shifts_o", "prenorm_o", "postnorm_o", "offsets_o", "baseline_o")
PARTIALS = ("all_a_h", "all_b_h")


def layer_kernel(leftover, names, *refs):
    R = types.SimpleNamespace(**dict(zip(names, refs)))
    R.nrecv = R.att
    span = R.tok.shape[1]
    width = R.tok.shape[2]
    total = R.hid_a.shape[0]
    half = width // 2
    pairs = half // PAIR
    blocks = total // span
    ub = R.exp.shape[1] // 2
    strip = width // 16
    block = ub // 4
    w = lax.axis_index("wide")
    s = lax.axis_index("seq")
    y = lax.div(s, 2)
    c = lax.rem(s, 2)
    hi = lax.div(w, leftover)
    b0 = lax.rem(hi, 2)
    b1 = lax.rem(lax.div(hi, 2), 2)
    b2 = lax.div(hi, 4)
    core_dev = (w, y * 2 + 1 - c)
    y_dev = (w, (1 - y) * 2 + c)
    dev0 = (w + leftover * (1 - 2 * b0), s)
    dev1 = (w + 2 * leftover * (1 - 2 * b1), s)
    dev2 = (w + 4 * leftover * (1 - 2 * b2), s)
    remote_count = itertools.count()
    local_count = itertools.count()
    sent = []

    def rows_of(p):
        return pl.ds(pl.multiple_of(p * span, span), span)

    def remote(src, dst, k, dev):
        return pltpu.make_async_remote_copy(
            src_ref=src, dst_ref=dst, send_sem=R.ssem.at[k], recv_sem=R.rsem.at[k],
            device_id=dev, device_id_type=MESH,
        )

    class Link:
        def __init__(self, item):
            self.item, self.open = item, False
            sent.append(self)

        def start(self):
            self.item.start()
            self.open = True

        def wait_recv(self):
            self.item.wait_recv()

        def wait_send(self):
            self.item.wait_send()
            self.open = False

    def link(src, dst, dev):
        return Link(remote(src, dst, next(remote_count), dev))

    def local(src, dst):
        return pltpu.make_async_copy(src, dst, R.lsem.at[next(local_count)])

    own_place = [rows_of(2 * j + c) for j in range(2)]
    other_place = [rows_of(2 * j + 1 - c) for j in range(2)]

    barrier = pltpu.get_barrier_semaphore()
    for dev in (core_dev, y_dev, dev0, dev1, dev2):
        pl.semaphore_signal(barrier, inc=1, device_id=dev, device_id_type=MESH)

    adap_load = local(R.adap_h, R.adap)
    tok_load = local(R.tok_h.at[y], R.tok.at[y])
    cot_load = local(R.cot_h.at[y], R.cot.at[y])
    first_loads = [
        local(getattr(R, name + "_h"), getattr(R, name))
        for name in ("cond", "shifts", "prenorm", "cosine", "sine", "postnorm", "offsets", "baseline")
    ]
    mix_loads = []
    for j in range(pairs):
        for b in range(3):
            mix_loads.append(local(
                R.mix_h.at[:, pl.ds(pl.multiple_of(b * width + c * half + j * PAIR, PAIR), PAIR)],
                R.mix.at[:, pl.ds((j * 3 + b) * PAIR, PAIR)],
            ))
    proj_load = local(R.proj_h, R.proj)
    exp_load = local(R.exp_h.at[:, pl.ds(pl.multiple_of(c * 2 * ub, PAIR), 2 * ub)], R.exp)
    con_load = local(R.con_h.at[pl.ds(pl.multiple_of(c * 2 * ub, PAIR), 2 * ub), :], R.con)
    for item in [adap_load, tok_load] + first_loads + mix_loads:
        item.start()

    tok_swap = link(R.tok_h.at[1 - y], R.tok.at[y], y_dev)
    cot_swap = link(R.cot_h.at[1 - y], R.cot.at[y], y_dev)
    hid_a_push = []
    for j in (y, 1 - y):
        place = rows_of(2 * j + c)
        hid_a_push.append(link(R.hid_a.at[place, :], R.hid_a.at[place, :], core_dev))
    gnar_base = next(remote_count)
    next(remote_count)
    gnar_push = [Link(remote(R.gnar.at[p, :], R.gnar.at[p, :], gnar_base + j, core_dev)) for j, p in enumerate(own_place)]
    hid_f_base = next(remote_count)
    next(remote_count)
    hid_f_push = [Link(remote(R.hid_f.at[p, :], R.hid_f.at[p, :], hid_f_base + j, core_dev)) for j, p in enumerate(own_place)]
    att_base = next(remote_count)
    for _ in range(2 * pairs - 1):
        next(remote_count)
    hsum_base = next(remote_count)
    next(remote_count)
    nsum_base = next(remote_count)
    next(remote_count)
    hsum_push = [Link(remote(R.hsend.at[j], R.hrecv.at[j], hsum_base + j, core_dev)) for j in range(2)]
    nsum_push = [Link(remote(R.nsend.at[j], R.nrecv.at[j], nsum_base + j, core_dev)) for j in range(2)]
    gbr_push = [link(R.gbr.at[p, :], R.gbr.at[p, :], core_dev) for p in own_place]
    asum_push = [link(R.hsend.at[j], R.hrecv.at[j], core_dev) for j in range(2)]
    def stage(n, j):
        return R.gwid.at[pl.ds(pl.multiple_of((2 * n + j) * span, span), span), :]

    out_push = link(stage(0, 1 - y), R.out_h.at[y], y_dev)
    gtok_push = link(stage(1, 1 - y), R.gtok_h.at[y], y_dev)

    class Halving:
        def __init__(self, acc, steps):
            self.acc = acc
            self.steps = []
            place = ()
            for bit, dev, recv in steps:
                self.steps.append((link(acc.at[place + (1 - bit,)], recv, dev), place + (bit,), recv))
                place = place + (bit,)

        def send(self, t):
            self.steps[t][0].start()

        def land(self, t, into=None):
            _, place, recv = self.steps[t]
            value = self.acc.at[place][...] + recv[...]
            if into is None:
                self.acc.at[place][...] = value
            else:
                into[...] = value

    class Strips:
        def __init__(self, ref, lanes):
            self.ref, self.lanes = ref, lanes

        @property
        def at(self):
            return self

        def __getitem__(self, bits):
            start = 0
            for n, bit in enumerate(bits):
                start = start + bit * (8 >> n)
            rows = (16 >> len(bits)) * strip
            return self.ref.at[pl.ds(pl.multiple_of(start * strip, strip), rows), self.lanes]

    step_of = dict(x=(b0, dev0), y=(y, y_dev), z=(b1, dev1), q=(b2, dev2))

    def steps_of(order, recvs):
        return [step_of[key] + (recv,) for key, recv in zip(order, recvs)]

    sums = {
        "E0": Halving(R.ge.at[0], steps_of(ORDERS["E0"], [r.at[0] for r in (R.e1, R.e2, R.e3, R.e4)])),
        "E1": Halving(R.ge.at[1], steps_of(ORDERS["E1"], [r.at[1] for r in (R.e1, R.e2, R.e3, R.e4)])),
        "P": Halving(R.gp, steps_of(ORDERS["P"], (R.p1, R.p2, R.p3, R.p4))),
    }
    for j in range(pairs):
        sums[f"M{j}"] = Halving(
            Strips(R.exp, pl.ds(j * half, half)),
            steps_of(ORDERS[f"M{j}"], [r.at[j] for r in (R.m1, R.m2, R.m3, R.m4)]),
        )
    links, lands = {}, {}
    finals = {
        "E0": R.ag_e.at[c, y, 0], "E1": R.ag_e.at[c, y, 1], "P": R.ag_m.at[c, y, 0],
        **{f"M{j}": R.ag_m.at[c, y, 1 + j] for j in range(pairs)},
    }
    for name, item in sums.items():
        for t in range(4):
            links[f"{name}.{t}"] = item.steps[t][0]
            lands[f"{name}.{t}"] = functools.partial(item.land, t, finals[name] if t == 3 else None)

    everything = slice(None)

    def place_c(i, **bits):
        return (bits.get("x", everything), bits.get("y", everything), i)

    def land_c(link_name, place, recv):
        def run():
            R.gc[place] = R.gc[place] + recv[...]

        lands[link_name] = run

    def link_c(name, send_place, keep_place, recv, dev):
        links[name] = link(R.gc.at[send_place], recv, dev)
        land_c(name, keep_place, recv)

    own_bit = dict(x=b0, y=y)
    plan_c = ORDERS["C"]
    for i in range(2):
        links[f"C{i}s"] = link(R.gcs, R.gc.at[:, :, i, c], core_dev)
        lands[f"C{i}s"] = lambda: None
        one, two = plan_c[i]
        link_c(
            f"C{i}.0", place_c(i, **{one: 1 - own_bit[one]}), place_c(i, **{one: own_bit[one]}),
            R.c1.at[i], step_of[one][1],
        )
        if len(plan_c) == 2:
            link_c(
                f"C{i}.1", place_c(i, **{one: own_bit[one], two: 1 - own_bit[two]}), place_c(i, **own_bit),
                R.c2.at[i], step_of[two][1],
            )
    if len(plan_c) == 2:
        link_c("C.2", place_c(1 - b1, **own_bit), place_c(b1, **own_bit), R.c3, dev1)
    else:
        link_c(
            "C.1", place_c(1 - b1, **{one: own_bit[one]}), place_c(b1, **{one: own_bit[one]}), R.c2, dev1
        )
        link_c(
            "C.2", place_c(b1, **{one: own_bit[one], two: 1 - own_bit[two]}), place_c(b1, **own_bit),
            R.c3, step_of[two][1],
        )
    links["C.3"] = link(R.gc.at[b0, y, b1, 1 - b2], R.c4, dev2)

    def land_c3():
        R.ag_c[c, y] = R.gc[b0, y, b1, b2] + R.c4[...]

    lands["C.3"] = land_c3
    links["Ps"] = link(R.gps, R.gp.at[:, :, :, c], core_dev)
    most, last = pl.ds(0, pairs), pl.ds(pairs, 1)
    for name, mine, both in (
        ("agE", R.ag_e.at[c, y], R.ag_e.at[c]),
        ("agC", R.ag_c.at[c, y], R.ag_c.at[c]),
        ("agP", R.ag_m.at[c, y, most], R.ag_m.at[c, :, most]),
        ("agM", R.ag_m.at[c, y, last], R.ag_m.at[c, :, last]),
    ):
        links[name] = link(mine, mine, y_dev)
        links[name + "c"] = link(both, both, core_dev)

    chip = b0 * 8 + b2 * 4 + b1 * 2 + y

    def land_total(part, recv, every):
        def run():
            every[c, chip] = part[c] + recv[...]

        return run

    for name, part, recv, every in (("ga", R.va, R.va_r, R.all_a), ("gb", R.vb, R.vb_r, R.all_b)):
        links[name + "C"] = link(part.at[1 - c], recv, core_dev)
        lands[name + "C"] = land_total(part, recv, every)
        for t, dev in enumerate((y_dev, dev1, dev2, dev0)):
            size = 2**t
            ref = every.at[c, pl.ds(lax.div(chip, size) * size, size)]
            links[f"{name}{t}"] = link(ref, ref, dev)
        links[name + "F"] = link(every.at[c], every.at[c], core_dev)

    sequence = [name for _, landed in SCHEDULE for name in landed]
    follow = {"C0s": "C0.0", "C1s": "C1.0", "Ps": "P.0", "C.2": "C.3", "C.3": "agC"}
    for name in ("agE", "agC", "agP", "agM"):
        follow[name] = name + "c"
    for name in ("ga", "gb"):
        for one, two in zip("C0123", "0123F"):
            follow[name + one] = name + two
    for name in sums:
        for t in range(3):
            follow[f"{name}.{t}"] = f"{name}.{t + 1}"
    if len(plan_c) == 2:
        follow.update({"C0.0": "C0.1", "C1.0": "C1.1"})
        joined = [(("C0.1", "C1.1"), "C.2")]
    else:
        follow["C.1"] = "C.2"
        joined = [(("C0.0", "C1.0"), "C.1")]
    joined += [(("E0.3", "E1.3"), "agE"), (("P.3", "M0.3", "M1.3"), "agP"), (("M2.3",), "agM")]
    for names_in, name in joined:
        follow[max(names_in, key=sequence.index)] = name

    def serve(name):
        links[name].wait_recv()
        if name in lands:
            lands[name]()
        if name in follow:
            links[follow[name]].start()

    def service(point):
        for name in dict(SCHEDULE).get(point, ()):
            if name == "out":
                continue
            serve(name)

    def add_row(ref, r, value):
        for n in range(2):
            ref[n, pl.ds(r, 1), :] += value[:, n * half : (n + 1) * half]

    pl.semaphore_wait(barrier, 5)
    tok_swap.start()
    for item in (cot_load, proj_load, exp_load, con_load):
        item.start()
    R.va[...] = jnp.zeros_like(R.va)
    R.vb[...] = jnp.zeros_like(R.vb)

    adap_load.wait()
    for item in first_loads:
        item.wait()
    crow = jnp.where(y == 0, R.cond[0:1, :], R.cond[1:2, :])
    crow = crow * (1.0 / (1.0 + jnp.exp(-crow)))
    extent = crow.shape[1]
    R.va[0, 10:11, :extent] = crow * (1 - c).astype(F32)
    eye = lax.broadcasted_iota(jnp.int32, (extent, extent), 0) == lax.broadcasted_iota(
        jnp.int32, (extent, extent), 1
    )
    ccol = jnp.sum(jnp.where(eye, jnp.broadcast_to(crow, (extent, extent)), 0.0), axis=1, keepdims=True)
    shifts = R.shifts[...].reshape(1, 6 * width)
    for n in range(6):
        part = pl.ds(n * width, width)
        R.mod[n : n + 1, :] = column_sum(R.adap[:, part].astype(F32) * ccol) + shifts[:, n * width : (n + 1) * width]
    pregain = R.prenorm[...].reshape(1, width)
    postgain = R.postnorm[...].reshape(1, width)

    def first_norm(j, t):
        normal, _ = normalize(R.tok[j].astype(F32))
        value = normal * (pregain * (1.0 + R.mod[1:2, :])) + R.mod[0:1, :]
        R.hid_a[rows_of(2 * j + c), :] = value.astype(BF16)
        hid_a_push[t].start()

    def project(p):
        place = rows_of(p)
        mixed = dot(R.hid_a[place, :], R.mix[...])
        cos_here = R.cosine[place, :]
        sin_here = R.sine[place, :]
        for j in range(pairs):
            base = j * 3 * PAIR
            query = mixed[:, base : base + PAIR]
            query = (query * cos_here + turn(query) * sin_here).astype(BF16) * jnp.asarray(
                HDIM ** (-0.5), BF16
            )
            R.qq[j, place, :] = query
            key = mixed[:, base + PAIR : base + 2 * PAIR]
            R.kk[j, place, :] = (key * cos_here + turn(key) * sin_here).astype(BF16)
            R.vv[j, place, :] = mixed[:, base + 2 * PAIR : base + 3 * PAIR].astype(BF16)

    tok_load.wait()
    first_norm(y, 0)
    for item in mix_loads:
        item.wait()
    project(2 * y + c)
    tok_swap.wait_recv()
    first_norm(1 - y, 1)
    hid_a_push[0].wait_recv()
    project(2 * y + 1 - c)
    project(2 * (1 - y) + c)
    hid_a_push[1].wait_recv()
    project(2 * (1 - y) + 1 - c)
    for j in range(pairs):
        R.q_t[j * PAIR : (j + 1) * PAIR, :] = R.qq[j].T

    cot_swap.start()
    def att_push(j, jj):
        lanes = pl.ds(pl.multiple_of(c * half + j * PAIR, PAIR), PAIR)
        return remote(
            R.att_s.at[j, other_place[jj], :], R.att.at[jj, :, lanes], att_base + 2 * j + jj, core_dev
        )

    lane_pair = lax.broadcasted_iota(jnp.int32, (span, PAIR), 1)
    lane_long = lax.broadcasted_iota(jnp.int32, (total, PAIR), 1)

    def in_head(lane, hh):
        return lane < HDIM if hh == 0 else lane >= HDIM

    def attend(j, carry):
        def score_of(hh, qb):
            query = R.qq[j, qb * span : (qb + 1) * span, :]
            query = jnp.where(in_head(lane_pair, hh), query, jnp.zeros_like(query))
            return dot(query, R.kk[j], ROWS_BY_ROWS)

        values = []
        for hh in range(2):
            there = R.vv[j]
            values.append(jnp.where(in_head(lane_long, hh), there, jnp.ones_like(there)))
        steps = [(hh, qb) for hh in range(2) for qb in range(blocks)]
        score = score_of(*steps[0])
        for index, (hh, qb) in enumerate(steps):
            following = score_of(*steps[index + 1]) if index + 1 < len(steps) else None
            place = slice(qb * span, (qb + 1) * span)
            top = jnp.max(score, axis=1, keepdims=True)
            low = jnp.exp(score - top).astype(BF16)
            grown = dot(low, values[hh])
            totals = pltpu.roll(grown, HDIM, 1)
            grown = (grown / totals).astype(BF16)
            weight = top + jnp.log(totals)
            if hh == 0:
                R.att_s[j, place, :] = grown
                R.lse[j, place, :] = weight
            else:
                R.att_s[j, place, :] = jnp.where(lane_pair < HDIM, R.att_s[j, place, :], grown)
                R.lse[j, place, :] = jnp.where(lane_pair < HDIM, R.lse[j, place, :], weight)
            score = following
        lanes = pl.ds(pl.multiple_of(c * half + j * PAIR, PAIR), PAIR)
        for jj in range(2):
            att_push(j, jj).start()
            R.att[jj, :, lanes] = R.att_s[j, own_place[jj], :]
        return carry

    lax.fori_loop(0, pairs, attend, 0)
    cot_load.wait()
    cot_swap.wait_recv()
    for j in range(2):
        low = (R.cot[j].astype(F32) * R.mod[5:6, :]).astype(BF16)
        R.gnar[own_place[j], :] = low
        add_row(R.va, 5, column_sum(low.astype(F32)))
        gnar_push[j].start()

    for j in range(pairs):
        for jj in range(2):
            att_push(j, jj).wait_recv()

    proj_load.wait()
    for j in range(2):
        grown = dot(R.att[j], R.proj[...])
        R.branch[j] = grown.astype(BF16)
        value = R.tok[j].astype(F32) + R.mod[2:3, :] * grown
        R.middle[j] = value
        normal, _ = normalize(value)
        R.hid_f[own_place[j], :] = (normal * (postgain * (1.0 + R.mod[4:5, :])) + R.mod[3:4, :]).astype(BF16)
        hid_f_push[j].start()

    def bits_of(n, order):
        bits = dict(q=n // 8, z=n // 4 % 2, x=n // 2 % 2, y=n % 2)
        return tuple(bits[key] for key in order)

    exp_load.wait()
    con_load.wait()
    offsets = R.offsets[...].reshape(1, 4 * ub)
    offsets = jnp.where(c == 0, offsets[:, : 2 * ub], offsets[:, 2 * ub :])
    for i in range(2):
        units = pl.ds(i * ub, ub)

        def feed(t, carry, i=i, units=units):
            late = lax.div(t, 2)
            j = lax.rem(t, 2)
            place = rows_of(2 * j + lax.rem(c + late + i, 2))
            if i == 0:
                @pl.when(late == 1)
                def _():
                    remote(R.hid_f.at[place, :], R.hid_f.at[place, :], hid_f_base + j, core_dev).wait_recv()
                    remote(R.gnar.at[place, :], R.gnar.at[place, :], gnar_base + j, core_dev).wait_recv()
            else:
                for k in range(1, 4):
                    if f"f{k - 1}" in dict(SCHEDULE):
                        @pl.when(t == k)
                        def _(k=k):
                            service(f"f{k - 1}")
            v = dot(R.hid_f[place, :], R.exp[:, units]) + offsets[:, i * ub : (i + 1) * ub]
            square = v * v
            th = jnp.tanh(v * (GELU_A + (GELU_A * GELU_B) * square))
            up = 0.5 + 0.5 * th
            low = (v * up).astype(BF16)
            R.act[place, :] = low
            slope = up + (v * (0.5 - 0.5 * th * th)) * (GELU_A + (3.0 * GELU_A * GELU_B) * square)
            grad = (dot(R.gnar[place, :], R.con[units, :], ROWS_BY_ROWS) * slope).astype(BF16)
            R.gwid[place, :] = grad
            add_row(R.va, 6 + 2 * c + i, column_sum(grad.astype(F32)))
            n_part = dot(low, R.con[units, :])
            h_part = dot(grad, R.exp[:, units], ROWS_BY_ROWS)
            if i == 0:
                R.nacc[place, :] = n_part
                R.hacc[place, :] = h_part
            else:
                R.nacc[place, :] += n_part
                R.hacc[place, :] += h_part

                @pl.when(late == 0)
                def _():
                    R.hsend[j] = R.hacc[place, :].astype(BF16)
                    remote(R.hsend.at[j], R.hrecv.at[j], hsum_base + j, core_dev).start()
                    R.nsend[j] = R.nacc[place, :].astype(BF16)
                    remote(R.nsend.at[j], R.nrecv.at[j], nsum_base + j, core_dev).start()
            return carry

        lax.fori_loop(0, 4, feed, 0)
        if i == 1:
            for item in hsum_push + nsum_push:
                item.open = True
        value = dot(R.hid_f[...], R.gwid[...], COLS_BY_COLS).astype(BF16)
        for n in range(16):
            R.ge[(i,) + bits_of(n, ORDERS[f"E{i}"])] = value[n * strip : (n + 1) * strip]
        links[f"E{i}.0"].start()
        service(f"E{i}")
        value = dot(R.act[...], R.gnar[...], COLS_BY_COLS).astype(BF16)
        left, right = value[:, :half], value[:, half:]
        mine = jnp.where(c == 0, left, right)
        theirs = jnp.where(c == 0, right, left)
        if i == 1:
            service("f3")
            links["C0s"].wait_send()
        for n in range(4):
            a0, ay = n // 2, n % 2
            R.gcs[a0, ay] = theirs[n * block : (n + 1) * block]
            R.gc[a0, ay, i, c] = mine[n * block : (n + 1) * block]
        links[f"C{i}s"].start()
        service(f"C{i}")

    base_row = R.baseline[...].reshape(1, width)
    for j in range(2):
        place = own_place[j]
        hsum_push[j].wait_recv()
        got = R.hacc[place, :] + R.hrecv[j].astype(F32)
        normal, scale = normalize(R.middle[j])
        add_row(R.va, 1, column_sum(got))
        both = column_sum(got * normal)
        add_row(R.va, 2, both * postgain)
        add_row(R.va, 4, both * (1.0 + R.mod[4:5, :]))
        g = R.cot[j].astype(F32)
        nsum_push[j].wait_recv()
        narrowed = R.nacc[place, :] + R.nrecv[j].astype(F32) + base_row
        R.gwid[j * span : (j + 1) * span, :] = (R.middle[j] + R.mod[5:6, :] * narrowed).astype(BF16)
        add_row(R.va, 3, column_sum(g * narrowed))
        value = g + normalize_back(got * (postgain * (1.0 + R.mod[4:5, :])), normal, scale)
        R.middle[j] = value
        add_row(R.va, 0, column_sum(value * R.branch[j].astype(F32)))
        R.gbr[place, :] = (R.mod[2:3, :] * value).astype(BF16)
        gbr_push[j].start()
        if j == 0:
            service("n0")

    out_local = local(stage(0, y), R.out_h.at[y])
    out_local.start()
    links["gaC"].start()
    out_at = ORDERS["out"]
    if out_at == "n1":
        out_push.start()
    service("n1")
    for j in range(2):
        gbr_push[j].wait_recv()

    value = jnp.concatenate(
        [dot(R.att_s[j], R.gbr[...], COLS_BY_COLS).astype(BF16) for j in range(pairs)], axis=0
    )
    left, right = value[:, :half], value[:, half:]
    mine = jnp.where(c == 0, left, right)
    theirs = jnp.where(c == 0, right, left)
    for n in range(8):
        place = bits_of(n, ORDERS["P"][:3])
        R.gps[place] = theirs[n * strip : (n + 1) * strip]
        R.gp[place + (c,)] = mine[n * strip : (n + 1) * strip]
    links["Ps"].start()
    own_proj = R.proj[pl.ds(pl.multiple_of(c * half, PAIR), half), :]
    grown = dot(R.gbr[...], own_proj, ROWS_BY_ROWS).astype(BF16)
    for j in range(pairs):
        R.act[:, half + j * PAIR : half + (j + 1) * PAIR] = grown[:, j * PAIR : (j + 1) * PAIR]

    if out_at == "gp":
        out_push.start()
    service("gp")


    def service_pair(j, point):
        for k in range(pairs):
            key = f"b{k}{point}"
            if key == out_at or key in dict(SCHEDULE):
                @pl.when(j == k)
                def _(key=key):
                    if key == out_at:
                        out_push.start()
                    service(key)

    def attend_back(j, carry):
        grown = R.act[:, pl.ds(pl.multiple_of(half + j * PAIR, PAIR), PAIR)].astype(F32)
        product = grown * R.att_s[j].astype(F32)
        inner = [
            jnp.sum(jnp.where(in_head(lane_long, hh), product, 0.0), axis=1, keepdims=True) for hh in range(2)
        ]
        R.dsum[...] = jnp.where(in_head(lane_long, 0), inner[0], inner[1])
        R.dom_t[...] = grown.astype(BF16).T

        lanes = pl.ds(pl.multiple_of(half + j * PAIR, PAIR), PAIR)

        def one_head(value, hh):
            return jnp.where(in_head(lane_pair, hh), value, jnp.zeros_like(value))

        def products(hh, qb):
            rows = slice(qb * span, (qb + 1) * span)
            grad = dot(one_head(R.act[rows, lanes], hh), R.vv[j], ROWS_BY_ROWS)
            return grad, dot(one_head(R.qq[j, rows, :], hh), R.kk[j], ROWS_BY_ROWS)

        steps = [(hh, qb) for hh in range(2) for qb in range(blocks)]
        current = products(*steps[0])
        for index, (hh, qb) in enumerate(steps):
            following = products(*steps[index + 1]) if index + 1 < len(steps) else None
            grad, score = current
            place = slice(qb * span, (qb + 1) * span)
            rows = slice(hh * HDIM, (hh + 1) * HDIM)
            first = hh * HDIM
            weight = jnp.exp(score - R.lse[j, place, first : first + 1])
            low = weight.astype(BF16)
            grad = (weight * (grad - R.dsum[place, first : first + 1])).astype(BF16)
            q_part = dot(grad, R.kk[j])
            v_part = dot(R.dom_t[rows, place], low)
            k_part = dot(R.q_t[pl.ds(pl.multiple_of(j * PAIR + hh * HDIM, HDIM), HDIM), place], grad)
            if hh == 0:
                R.dq[place, :] = q_part
            else:
                R.dq[place, :] = jnp.where(lane_pair < HDIM, R.dq[place, :], q_part)
            if qb == 0:
                R.dv_t[rows, :] = v_part
                R.dk_t[rows, :] = k_part
            else:
                R.dv_t[rows, :] += v_part
                R.dk_t[rows, :] += k_part
            if qb == blocks - 1:
                service_pair(j, hh)
            current = following
        gq = R.dq[...] * HDIM ** (-0.5)
        gk = R.dk_t[...].T
        gmx = R.act.at[:, pl.ds(0, 3 * PAIR)]
        gmx[:, :PAIR] = (gq * R.cosine[...] - turn(gq) * R.sine[...]).astype(BF16)
        gmx[:, PAIR : 2 * PAIR] = (gk * R.cosine[...] - turn(gk) * R.sine[...]).astype(BF16)
        gmx[:, 2 * PAIR :] = R.dv_t[...].astype(BF16).T
        value = dot(R.hid_a[...], gmx[...], COLS_BY_COLS).astype(BF16)
        for k in range(pairs):
            @pl.when(j == k)
            def _(k=k):
                for n in range(16):
                    index = 0
                    for bit in bits_of(n, ORDERS[f"M{k}"]):
                        index = 2 * index + bit
                    R.exp[index * strip : (index + 1) * strip, k * half : (k + 1) * half] = value[
                        n * strip : (n + 1) * strip
                    ]
                links[f"M{k}.0"].start()
        service_pair(j, 2)
        lanes = pl.ds(pl.multiple_of(j * 3 * PAIR, PAIR), 3 * PAIR)

        def back(p, inner):
            place = rows_of(p)
            part = dot(gmx[place, :], R.mix[:, lanes], ROWS_BY_ROWS)

            @pl.when(j == 0)
            def _():
                R.hacc[place, :] = part

            @pl.when(j > 0)
            def _():
                R.hacc[place, :] += part

            return inner

        lax.fori_loop(0, blocks, back, 0)
        service_pair(j, 3)
        return carry

    lax.fori_loop(0, pairs, attend_back, 0)
    for j in range(2):
        hsum_push[j].wait_send()
        R.hsend[j] = R.hacc[other_place[j], :].astype(BF16)
        asum_push[j].start()

    gtok_local = local(stage(1, y), R.gtok_h.at[y])
    for j, item in ((1 - y, gtok_push), (y, gtok_local)):
        got = R.hacc[rows_of(2 * j + c), :] + 0.0
        if item is gtok_push:
            asum_push[0].wait_recv()
            asum_push[1].wait_recv()
        got = got + R.hrecv[j].astype(F32)
        normal, scale = normalize(R.tok[j].astype(F32))
        add_row(R.vb, 0, column_sum(got))
        both = column_sum(got * normal)
        add_row(R.vb, 1, both * pregain)
        add_row(R.vb, 2, both * (1.0 + R.mod[1:2, :]))
        stage(1, j)[...] = (
            R.middle[j] + normalize_back(got * (pregain * (1.0 + R.mod[1:2, :])), normal, scale)
        ).astype(BF16)
        item.start()
        if item is gtok_push:
            if out_at == "l0":
                out_push.start()
            service("l0")
    links["gbC"].start()
    service("l1")
    service("l2")

    stores = []

    def store(src, dst):
        item = local(src, dst)
        item.start()
        stores.append(item)

    def store_e():
        for n in range(8):
            cc, yy, i = n // 4, n // 2 % 2, n % 2
            store(
                R.ag_e.at[cc, yy, i],
                R.oe_h.at[pl.ds(yy * strip, strip), pl.ds((2 * cc + i) * width, width)],
            )

    def store_c():
        for n in range(4):
            cc, yy = n // 2, n % 2
            store(R.ag_c.at[cc, yy], R.oc_h.at[pl.ds(yy * block, block), pl.ds(cc * half, half)])

    def place_m(j):
        for n in range(4):
            cc, yy = n // 2, n % 2
            value = R.ag_m[cc, yy, 1 + j]
            for b in range(3):
                lane = cc * half + j * PAIR
                row = (2 * b + yy) * strip
                R.hid_f[row : row + strip, lane : lane + PAIR] = value[:, b * PAIR : (b + 1) * PAIR]

    def store_p():
        for n in range(4):
            cc, yy = n // 2, n % 2
            store(R.ag_m.at[cc, yy, 0], R.op_h.at[pl.ds(yy * strip, strip), pl.ds(cc * half, half)])
        for item in hid_f_push:
            item.open = True
            item.wait_send()
        for j in range(pairs - 1):
            place_m(j)

    def store_m():
        place_m(pairs - 1)
        for b in range(3):
            store(R.hid_f.at[pl.ds(2 * b * strip, 2 * strip), :], R.om_h.at[:, pl.ds(b * width, width)])

    results = {"agEc": store_e, "agCc": store_c, "agPc": store_p, "agMc": store_m}
    if leftover == 1:
        early, later = finish_vectors(R, hi, chip - y, width, half, extent)
    else:
        early = [lambda: store(R.all_a, R.all_a_h)]
        later = [lambda: store(R.all_b, R.all_b_h)]
    pieces = []
    tail = dict(SCHEDULE)["tail"]
    if "gaF" not in tail:
        pieces.extend(early)
    for name in tail:
        serve(name)
        if name in results:
            results[name]()
        if name == "gaF":
            pieces.extend(early)
        if name == "gbF":
            pieces.extend(later)
        if pieces:
            pieces.pop(0)()
    for piece in pieces:
        piece()
    for item in stores:
        item.wait()
    out_local.wait()
    out_push.wait_recv()
    gtok_local.wait()
    gtok_push.wait_recv()
    for j in range(pairs):
        for jj in range(2):
            att_push(j, jj).wait_send()
    for item in sent:
        if item.open:
            item.wait_send()


def finish_vectors(R, hi, chip, width, half, extent):
    own = extent // 8
    highest = lax.Precision.HIGHEST
    sections = ((R.all_b, 0), (R.all_b, 1), (R.all_a, 0), (R.all_a, 1), (R.all_a, 2), (R.all_a, 3))

    def transpose():
        R.st[...] = R.all_a[0, :, 10, :extent].T
        R.back[...] = jnp.zeros_like(R.back)

    def section(n, h):
        ref, r = sections[n]
        grads = ref[h, :, r, :]
        lanes = pl.ds(n * width + h * half, half)
        silu_own = R.st[pl.ds(pl.multiple_of(hi * own, own), own), :]
        R.adaptive_o[:, lanes] = jnp.dot(silu_own, grads, precision=highest, preferred_element_type=F32)
        R.total[:, lanes] = column_sum(grads)
        table = R.adap[:, lanes].astype(F32)
        for yy in range(2):
            mine = ref[h, pl.ds(chip + yy, 1), r, :]
            R.back[:, yy : yy + 1] += jnp.sum(table * mine, axis=1, keepdims=True)

    def share(vector, out):
        size = vector.shape[1] // 8
        value = jnp.zeros((1, size), F32)
        for k in range(8):
            value = jnp.where(hi == k, vector[:, k * size : (k + 1) * size], value)
        out[...] = value.reshape(size)

    def total_of(ref, r):
        return jnp.concatenate([column_sum(ref[h, :, r, :]) for h in range(2)], axis=1)

    def vectors():
        share(total_of(R.all_a, 4), R.postnorm_o)
        share(jnp.concatenate([total_of(R.all_a, 6 + n) for n in range(4)], axis=1), R.offsets_o)
        share(total_of(R.all_a, 5), R.baseline_o)

    def last():
        share(total_of(R.all_b, 2), R.prenorm_o)
        share(R.total[...], R.shifts_o)
        eye = lax.broadcasted_iota(jnp.int32, (extent, extent), 0) == lax.broadcasted_iota(
            jnp.int32, (extent, extent), 1
        )
        for yy in range(2):
            back = jnp.broadcast_to(R.back[:, yy : yy + 1], (extent, extent))
            row = column_sum(jnp.where(eye, back, 0.0))
            cond = R.cond[yy : yy + 1, :]
            gate = 1.0 / (1.0 + jnp.exp(-cond))
            R.time_o[yy : yy + 1, :] = row * (gate * (1.0 + cond * (1.0 - gate)))

    early = [transpose] + [functools.partial(section, n, h) for n in range(2, 6) for h in range(2)] + [vectors]
    later = [functools.partial(section, n, h) for n in range(2) for h in range(2)] + [last]
    return early, later


def finish_kernel(count, *refs):
    total = 4 + count
    given, results, held, high, sem = (
        refs[:total], refs[total : 2 * total], refs[2 * total : 3 * total], refs[3 * total : 3 * total + 4], refs[-1]
    )
    loads = [pltpu.make_async_copy(a, b, sem.at[n]) for n, (a, b) in enumerate(zip(given, held))]
    written = tuple(high) + tuple(held[4:])
    stores = [pltpu.make_async_copy(a, b, sem.at[total + n]) for n, (a, b) in enumerate(zip(written, results))]
    for item in loads:
        item.start()
    for n in range(total):
        loads[n].wait()
        if n < 4:
            high[n][...] = held[n][...].astype(F32)
        stores[n].start()
    for item in stores:
        item.wait()


def finish(sums, others):
    hbm = pl.BlockSpec(memory_space=pl.ANY)
    shape = jax.ShapeDtypeStruct
    return pl.pallas_call(
        functools.partial(finish_kernel, len(others)),
        out_shape=tuple(shape(v.shape, F32) for v in sums) + tuple(shape(v.shape, v.dtype) for v in others),
        in_specs=[hbm] * (4 + len(others)),
        out_specs=(hbm,) * (4 + len(others)),
        scratch_shapes=[pltpu.VMEM(v.shape, v.dtype) for v in (*sums, *others)]
        + [pltpu.VMEM(v.shape, F32) for v in sums] + [pltpu.SemaphoreType.DMA((8 + 2 * len(others),))],
        compiler_params=pltpu.CompilerParams(vmem_limit_bytes=60 * 1024 * 1024),
        name="finish",
    )(*sums, *others)


def rotary_constants(length):
    half_dim = HDIM // 2
    frequency = np.exp(np.arange(half_dim, dtype=np.float32) * np.float32(-2.0 * math.log(10000.0) / HDIM))
    angles = np.arange(length, dtype=np.float32)[:, None] * frequency[None, :].astype(np.float32)
    angles = angles.astype(np.float64)
    cosine = np.cos(angles).astype(np.float32)
    sine = np.sin(angles).astype(np.float32)
    cosine = np.concatenate([cosine] * 4, axis=-1)
    sine = np.concatenate([-sine, sine, -sine, sine], axis=-1)
    return cosine, sine


def local_part(wide_count, tokens, condition, cotangent, adaptive, shifts, prenorm, mixer, projection, postnorm,
               expand, offsets, contract, baseline):
    rows, span, width = tokens.shape
    total = 4 * span
    half = width // 2
    pairs = half // PAIR
    ff = expand.shape[1]
    extent = adaptive.shape[0]
    leftover = wide_count // 8
    cosine, sine = rotary_constants(total)
    hbm = pl.BlockSpec(memory_space=pl.ANY)
    vmem = pl.BlockSpec(memory_space=pltpu.VMEM)
    shape = jax.ShapeDtypeStruct
    out_shape = [
        shape(tokens.shape, BF16), shape(tokens.shape, BF16), shape((width // 8, ff), BF16),
        shape((ff // 8, width), BF16), shape((width // 8, width), BF16), shape((width // 8, 3 * width), BF16),
    ]
    out_specs = [hbm] * len(out_shape)
    names = INPUTS + GRADS
    if leftover == 1:
        names += FINALS
        out_shape += [
            shape(condition.shape, F32), shape((extent // 8, 6 * width), F32), shape((6 * width // 8,), F32),
            shape((width // 8,), F32), shape((width // 8,), F32), shape((ff // 8,), F32), shape((width // 8,), F32),
        ]
        out_specs += [vmem] * len(FINALS)
    else:
        names += PARTIALS
        out_shape += [shape((2, 16, 16, half), F32), shape((2, 16, 8, half), F32)]
        out_specs += [hbm] * len(PARTIALS)
    buffers = kernel_buffers(span, width, extent, ff)
    names += tuple(buffers)
    outs = pl.pallas_call(
        functools.partial(layer_kernel, leftover, names),
        out_shape=tuple(out_shape),
        in_specs=[hbm] * 15,
        out_specs=tuple(out_specs),
        scratch_shapes=list(buffers.values()),
        compiler_params=pltpu.CompilerParams(
            collective_id=0, has_side_effects=True, vmem_limit_bytes=64 * 1024 * 1024 - 65536
        ),
        name="layer",
    )(
        tokens, cotangent, adaptive, mixer, projection, expand, contract,
        condition, shifts, prenorm, postnorm, offsets, baseline, jnp.asarray(cosine), jnp.asarray(sine),
    )
    layer_output, grad_tokens = outs[0], outs[1]
    if leftover == 1:
        done = finish(outs[2:6], outs[:2] + outs[6:])
        grad_expand, grad_contract, grad_projection, grad_mixer = done[:4]
        layer_output, grad_tokens = done[4:6]
        grad_time, grad_adaptive, grad_shifts, grad_prenorm, grad_postnorm, grad_offsets, grad_baseline = done[6:]
        return (
            layer_output, grad_tokens, grad_time, grad_adaptive, grad_shifts, grad_prenorm, grad_mixer,
            grad_projection, grad_postnorm, grad_expand, grad_offsets, grad_contract, grad_baseline,
        )

    grad_expand, grad_contract, grad_projection, grad_mixer = (part.astype(F32) for part in outs[2:6])

    w = lax.axis_index("wide")

    def among_groups(part):
        size = part.shape[0]
        whole = jnp.zeros((8 * size,) + part.shape[1:], F32)
        whole = lax.dynamic_update_slice_in_dim(whole, part, lax.div(w, leftover) * size, axis=0)
        return lax.psum_scatter(whole, "wide", scatter_dimension=0, tiled=True)

    grad_expand, grad_contract, grad_projection, grad_mixer = (
        among_groups(part) for part in (grad_expand, grad_contract, grad_projection, grad_mixer)
    )
    all_a, all_b = outs[6], outs[7]
    every = jnp.concatenate([all_b, all_a], axis=2)
    every = every.reshape(2, 2, 2, 2, 2, 24, half).transpose(2, 3, 1, 4, 5, 0, 6).reshape(8, 2, 24, width)
    mine = lax.dynamic_slice_in_dim(every, lax.div(w, leftover), 1, axis=0)[0]
    every = lax.all_gather(mine, "wide", axis=0, tiled=True)
    sections = [0, 1, 8, 9, 10, 11]
    grad_mod = jnp.concatenate([every[:, r] for r in sections], axis=-1)
    silu_all = every[:, 18, :extent]
    highest = lax.Precision.HIGHEST
    own_rows = extent // wide_count
    grad_adaptive = jnp.dot(
        lax.dynamic_slice_in_dim(silu_all, w * own_rows, own_rows, axis=1).T, grad_mod, precision=highest
    )
    sums = jnp.sum(every, axis=0)

    def own(vector):
        size = vector.shape[0] // wide_count
        return lax.dynamic_slice_in_dim(vector, w * size, size)

    here = lax.dynamic_slice_in_dim(grad_mod, w * rows, rows, axis=0)
    _, silu_back = jax.vjp(jax.nn.silu, condition)
    (grad_time,) = silu_back(jnp.dot(here, adaptive.astype(F32).T, precision=highest))
    return (
        layer_output, grad_tokens, grad_time, grad_adaptive, own(jnp.sum(grad_mod, axis=0)), own(sums[2]),
        grad_mixer, grad_projection, own(sums[12]), grad_expand, own(sums[14:18].reshape(-1)), grad_contract,
        own(sums[13]),
    )


def solution(mesh):
    rows = P("wide", "seq", None)
    by_wide = P("wide", None)
    in_specs = (rows, by_wide, rows) + (P(),) * 10
    out_specs = (
        rows, rows, by_wide, by_wide, P("wide"), P("wide"), by_wide, by_wide, P("wide"), by_wide, P("wide"),
        by_wide, P("wide"),
    )
    return jax.shard_map(
        functools.partial(local_part, mesh.shape["wide"]),
        mesh=mesh, in_specs=in_specs, out_specs=out_specs, check_vma=False,
    )
```

```python
import functools
import itertools
import math
import types

import jax
import jax.numpy as jnp
import numpy as np
from jax import lax
from jax.experimental import pallas as pl
from jax.experimental.pallas import tpu as pltpu
from jax.sharding import PartitionSpec as P

F32 = jnp.float32
BF16 = jnp.bfloat16
MESH = pl.DeviceIdType.MESH
HDIM = 64
PAIR = 2 * HDIM
EPSILON = 1e-06
GELU_A = 0.7978845608
GELU_B = 0.044715

ROWS_BY_ROWS = (((1,), (1,)), ((), ()))
COLS_BY_COLS = (((0,), (0,)), ((), ()))


def dot(a, b, dims=None):
    if dims is None:
        return jnp.dot(a, b, preferred_element_type=F32)
    return lax.dot_general(a, b, dims, preferred_element_type=F32)


def normalize(values):
    center = values - jnp.mean(values, axis=-1, keepdims=True)
    scale = lax.rsqrt(jnp.mean(center * center, axis=-1, keepdims=True) + EPSILON)
    return center * scale, scale


def normalize_back(grad, normal, scale):
    first = jnp.mean(grad, axis=-1, keepdims=True)
    second = jnp.mean(grad * normal, axis=-1, keepdims=True)
    return scale * (grad - first - normal * second)


def turn(values):
    lane = lax.broadcasted_iota(jnp.int32, values.shape, 1)
    first = lax.rem(lane, HDIM) < HDIM // 2
    return jnp.where(
        first, pltpu.roll(values, PAIR - HDIM // 2, 1), pltpu.roll(values, HDIM // 2, 1)
    )


def column_sum(values):
    return jnp.sum(values, axis=0, keepdims=True)


def kernel_buffers(span, width, extent, ff):
    total = 4 * span
    half = width // 2
    pairs = half // PAIR
    uf = ff // 2
    ub = uf // 2
    strip = width // 16
    block = ff // 16
    V = pltpu.VMEM
    piece = (2, span, width)
    whole = (total, width)
    two = lambda n: (2,) * n
    wide_strip = (strip, width)
    half_strip = (strip, half)
    tall = (block, half)
    return dict(
        tok=V(piece, BF16), cot=V(piece, BF16), adap=V((extent, 6 * width), BF16),
        mix=V((width, 3 * half), BF16), proj=V((width, width), BF16), exp=V((width, uf), BF16),
        con=V((uf, width), BF16), mod=V((8, width), F32),
        hid_a=V(whole, BF16), qq=V((pairs, total, PAIR), BF16), kk=V((pairs, total, PAIR), BF16),
        vv=V((pairs, total, PAIR), BF16), q_t=V((half, total), BF16),
        lse=V((pairs, total, PAIR), F32),
        att_s=V((pairs, total, PAIR), BF16), att=V(piece, BF16),
        branch=V(piece, BF16), middle=V(piece, F32), hid_f=V(whole, BF16), gnar=V(whole, BF16),
        gbr=V(whole, BF16), act=V((total, ub), BF16), gwid=V((total, ub), BF16),
        nacc=V(whole, F32), hacc=V(whole, F32), nsend=V(piece, BF16),
        hsend=V(piece, BF16), hrecv=V(piece, BF16),
        dom_t=V((PAIR, total), BF16), dsum=V((total, PAIR), F32),
        dv_t=V((PAIR, total), F32), dk_t=V((PAIR, total), F32), dq=V((total, PAIR), F32),
        ge=V((2,) + two(4) + wide_strip, BF16), gc=V(two(4) + tall, BF16), gcs=V(two(2) + tall, BF16),
        gp=V(two(4) + half_strip, BF16), gps=V(two(3) + half_strip, BF16),
        e1=V((2,) + two(3) + wide_strip, BF16), e2=V((2,) + two(2) + wide_strip, BF16),
        e3=V((2,) + two(1) + wide_strip, BF16), e4=V((2,) + wide_strip, BF16),
        c1=V(two(3) + tall, BF16), c2=V(two(2) + tall, BF16), c3=V(two(1) + tall, BF16), c4=V(tall, BF16),
        p1=V(two(3) + half_strip, BF16), p2=V(two(2) + half_strip, BF16), p3=V(two(1) + half_strip, BF16),
        p4=V(half_strip, BF16),
        m1=V((pairs, 8 * strip, half), BF16), m2=V((pairs, 4 * strip, half), BF16),
        m3=V((pairs, 2 * strip, half), BF16), m4=V((pairs,) + half_strip, BF16),
        ag_e=V(two(3) + wide_strip, BF16), ag_c=V(two(2) + tall, BF16),
        ag_m=V(two(2) + (pairs + 1,) + half_strip, BF16),
        va=V((2, 16, half), F32), vb=V((2, 8, half), F32), va_r=V((16, half), F32), vb_r=V((8, half), F32),
        all_a=V((2, 16, 16, half), F32), all_b=V((2, 16, 8, half), F32), st=V((extent, 16), F32),
        back=V((extent, 8), F32), total=V((1, 6 * width), F32),
        cosine=V((total, PAIR), F32), sine=V((total, PAIR), F32), cond=V((2, extent), F32),
        shifts=V((6 * width,), F32), prenorm=V((width,), F32), postnorm=V((width,), F32),
        offsets=V((ff,), F32), baseline=V((width,), F32),
        lsem=pltpu.SemaphoreType.DMA((64,)),
        ssem=pltpu.SemaphoreType.DMA((100,)), rsem=pltpu.SemaphoreType.DMA((100,)),
    )


ORDERS = {
    "E0": ("y", "x", "z", "q"),
    "E1": ("z", "x", "y", "q"),
    "P": ("z", "y", "x", "q"),
    "M0": ("x", "z", "y", "q"),
    "M1": ("z", "x", "y", "q"),
    "M2": ("x", "z", "y", "q"),
    "C": (("x", "y"), ("y", "x")),
    "out": "b13",
}
SCHEDULE = (
    ("f2", ("C0s",)),
    ("n1", ("C1s",)),
    ("gp", ("E0.0",)),
    ("b00", ("Ps",)),
    ("b01", ("gaC",)),
    ("b02", ("C0.0", "E1.0")),
    ("b10", ("E0.1", "P.0")),
    ("b11", ("ga0", "C1.0")),
    ("b13", ("E0.2",)),
    ("b20", ("C0.1", "P.1", "M0.0")),
    ("b21", ("ga1", "E1.1", "E0.3", "M1.0")),
    ("b22", ("P.2",)),
    ("b23", ("M0.1", "C1.1")),
    ("l0", ("E1.2",)),
    ("l1", ("P.3", "M0.2", "M1.1")),
    ("tail", (
        "ga2", "gbC", "M2.0", "C.2", "M0.3", "E1.3", "M1.2", "gb0",
        "gb1", "M2.1", "ga3", "M1.3", "gaF", "gb2", "C.3", "agE",
        "M2.2", "gb3", "agEc", "agP", "M2.3", "gbF", "agPc", "agC",
        "agM", "agMc", "agCc",
    )),
)

INPUTS = (
    "tok_h", "cot_h", "adap_h", "mix_h", "proj_h", "exp_h", "con_h",
    "cond_h", "shifts_h", "prenorm_h", "postnorm_h", "offsets_h", "baseline_h", "cosine_h", "sine_h",
)
GRADS = ("out_h", "gtok_h", "oe_h", "oc_h", "op_h", "om_h")
FINALS = ("time_o", "adaptive_o", "shifts_o", "prenorm_o", "postnorm_o", "offsets_o", "baseline_o")
PARTIALS = ("all_a_h", "all_b_h")


def layer_kernel(leftover, names, *refs):
    R = types.SimpleNamespace(**dict(zip(names, refs)))
    R.nrecv = R.att
    span = R.tok.shape[1]
    width = R.tok.shape[2]
    total = R.hid_a.shape[0]
    half = width // 2
    pairs = half // PAIR
    blocks = total // span
    ub = R.exp.shape[1] // 2
    strip = width // 16
    block = ub // 4
    w = lax.axis_index("wide")
    s = lax.axis_index("seq")
    y = lax.div(s, 2)
    c = lax.rem(s, 2)
    hi = lax.div(w, leftover)
    b0 = lax.rem(hi, 2)
    b1 = lax.rem(lax.div(hi, 2), 2)
    b2 = lax.div(hi, 4)
    core_dev = (w, y * 2 + 1 - c)
    y_dev = (w, (1 - y) * 2 + c)
    dev0 = (w + leftover * (1 - 2 * b0), s)
    dev1 = (w + 2 * leftover * (1 - 2 * b1), s)
    dev2 = (w + 4 * leftover * (1 - 2 * b2), s)
    remote_count = itertools.count()
    local_count = itertools.count()
    sent = []

    def rows_of(p):
        return pl.ds(pl.multiple_of(p * span, span), span)

    def remote(src, dst, k, dev):
        return pltpu.make_async_remote_copy(
            src_ref=src, dst_ref=dst, send_sem=R.ssem.at[k], recv_sem=R.rsem.at[k],
            device_id=dev, device_id_type=MESH,
        )

    class Link:
        def __init__(self, item):
            self.item, self.open = item, False
            sent.append(self)

        def start(self):
            self.item.start()
            self.open = True

        def wait_recv(self):
            self.item.wait_recv()

        def wait_send(self):
            self.item.wait_send()
            self.open = False

    def link(src, dst, dev):
        return Link(remote(src, dst, next(remote_count), dev))

    def local(src, dst):
        return pltpu.make_async_copy(src, dst, R.lsem.at[next(local_count)])

    own_place = [rows_of(2 * j + c) for j in range(2)]
    other_place = [rows_of(2 * j + 1 - c) for j in range(2)]

    barrier = pltpu.get_barrier_semaphore()
    for dev in (core_dev, y_dev, dev0, dev1, dev2):
        pl.semaphore_signal(barrier, inc=1, device_id=dev, device_id_type=MESH)

    adap_load = local(R.adap_h, R.adap)
    tok_load = local(R.tok_h.at[y], R.tok.at[y])
    cot_load = local(R.cot_h.at[y], R.cot.at[y])
    first_loads = [
        local(getattr(R, name + "_h"), getattr(R, name))
        for name in ("cond", "shifts", "prenorm", "cosine", "sine", "postnorm", "offsets", "baseline")
    ]
    mix_loads = []
    for j in range(pairs):
        for b in range(3):
            mix_loads.append(local(
                R.mix_h.at[:, pl.ds(pl.multiple_of(b * width + c * half + j * PAIR, PAIR), PAIR)],
                R.mix.at[:, pl.ds((j * 3 + b) * PAIR, PAIR)],
            ))
    proj_load = local(R.proj_h, R.proj)
    exp_load = local(R.exp_h.at[:, pl.ds(pl.multiple_of(c * 2 * ub, PAIR), 2 * ub)], R.exp)
    con_load = local(R.con_h.at[pl.ds(pl.multiple_of(c * 2 * ub, PAIR), 2 * ub), :], R.con)
    for item in [adap_load, tok_load] + first_loads + mix_loads:
        item.start()

    tok_swap = link(R.tok_h.at[1 - y], R.tok.at[y], y_dev)
    cot_swap = link(R.cot_h.at[1 - y], R.cot.at[y], y_dev)
    hid_a_push = []
    for j in (y, 1 - y):
        place = rows_of(2 * j + c)
        hid_a_push.append(link(R.hid_a.at[place, :], R.hid_a.at[place, :], core_dev))
    gnar_base = next(remote_count)
    next(remote_count)
    gnar_push = [Link(remote(R.gnar.at[p, :], R.gnar.at[p, :], gnar_base + j, core_dev)) for j, p in enumerate(own_place)]
    hid_f_base = next(remote_count)
    next(remote_count)
    hid_f_push = [Link(remote(R.hid_f.at[p, :], R.hid_f.at[p, :], hid_f_base + j, core_dev)) for j, p in enumerate(own_place)]
    att_base = next(remote_count)
    for _ in range(2 * pairs - 1):
        next(remote_count)
    hsum_base = next(remote_count)
    next(remote_count)
    nsum_base = next(remote_count)
    next(remote_count)
    hsum_push = [Link(remote(R.hsend.at[j], R.hrecv.at[j], hsum_base + j, core_dev)) for j in range(2)]
    nsum_push = [Link(remote(R.nsend.at[j], R.nrecv.at[j], nsum_base + j, core_dev)) for j in range(2)]
    gbr_push = [link(R.gbr.at[p, :], R.gbr.at[p, :], core_dev) for p in own_place]
    asum_push = [link(R.hsend.at[j], R.hrecv.at[j], core_dev) for j in range(2)]
    def stage(n, j):
        return R.gwid.at[pl.ds(pl.multiple_of((2 * n + j) * span, span), span), :]

    out_push = link(stage(0, 1 - y), R.out_h.at[y], y_dev)
    gtok_push = link(stage(1, 1 - y), R.gtok_h.at[y], y_dev)

    class Halving:
        def __init__(self, acc, steps):
            self.acc = acc
            self.steps = []
            place = ()
            for bit, dev, recv in steps:
                self.steps.append((link(acc.at[place + (1 - bit,)], recv, dev), place + (bit,), recv))
                place = place + (bit,)

        def send(self, t):
            self.steps[t][0].start()

        def land(self, t, into=None):
            _, place, recv = self.steps[t]
            value = self.acc.at[place][...] + recv[...]
            if into is None:
                self.acc.at[place][...] = value
            else:
                into[...] = value

    class Strips:
        def __init__(self, ref, lanes):
            self.ref, self.lanes = ref, lanes

        @property
        def at(self):
            return self

        def __getitem__(self, bits):
            start = 0
            for n, bit in enumerate(bits):
                start = start + bit * (8 >> n)
            rows = (16 >> len(bits)) * strip
            return self.ref.at[pl.ds(pl.multiple_of(start * strip, strip), rows), self.lanes]

    step_of = dict(x=(b0, dev0), y=(y, y_dev), z=(b1, dev1), q=(b2, dev2))

    def steps_of(order, recvs):
        return [step_of[key] + (recv,) for key, recv in zip(order, recvs)]

    sums = {
        "E0": Halving(R.ge.at[0], steps_of(ORDERS["E0"], [r.at[0] for r in (R.e1, R.e2, R.e3, R.e4)])),
        "E1": Halving(R.ge.at[1], steps_of(ORDERS["E1"], [r.at[1] for r in (R.e1, R.e2, R.e3, R.e4)])),
        "P": Halving(R.gp, steps_of(ORDERS["P"], (R.p1, R.p2, R.p3, R.p4))),
    }
    for j in range(pairs):
        sums[f"M{j}"] = Halving(
            Strips(R.exp, pl.ds(j * half, half)),
            steps_of(ORDERS[f"M{j}"], [r.at[j] for r in (R.m1, R.m2, R.m3, R.m4)]),
        )
    links, lands = {}, {}
    finals = {
        "E0": R.ag_e.at[c, y, 0], "E1": R.ag_e.at[c, y, 1], "P": R.ag_m.at[c, y, 0],
        **{f"M{j}": R.ag_m.at[c, y, 1 + j] for j in range(pairs)},
    }
    for name, item in sums.items():
        for t in range(4):
            links[f"{name}.{t}"] = item.steps[t][0]
            lands[f"{name}.{t}"] = functools.partial(item.land, t, finals[name] if t == 3 else None)

    everything = slice(None)

    def place_c(i, **bits):
        return (bits.get("x", everything), bits.get("y", everything), i)

    def land_c(link_name, place, recv):
        def run():
            R.gc[place] = R.gc[place] + recv[...]

        lands[link_name] = run

    def link_c(name, send_place, keep_place, recv, dev):
        links[name] = link(R.gc.at[send_place], recv, dev)
        land_c(name, keep_place, recv)

    own_bit = dict(x=b0, y=y)
    plan_c = ORDERS["C"]
    for i in range(2):
        links[f"C{i}s"] = link(R.gcs, R.gc.at[:, :, i, c], core_dev)
        lands[f"C{i}s"] = lambda: None
        one, two = plan_c[i]
        link_c(
            f"C{i}.0", place_c(i, **{one: 1 - own_bit[one]}), place_c(i, **{one: own_bit[one]}),
            R.c1.at[i], step_of[one][1],
        )
        if len(plan_c) == 2:
            link_c(
                f"C{i}.1", place_c(i, **{one: own_bit[one], two: 1 - own_bit[two]}), place_c(i, **own_bit),
                R.c2.at[i], step_of[two][1],
            )
    if len(plan_c) == 2:
        link_c("C.2", place_c(1 - b1, **own_bit), place_c(b1, **own_bit), R.c3, dev1)
    else:
        link_c(
            "C.1", place_c(1 - b1, **{one: own_bit[one]}), place_c(b1, **{one: own_bit[one]}), R.c2, dev1
        )
        link_c(
            "C.2", place_c(b1, **{one: own_bit[one], two: 1 - own_bit[two]}), place_c(b1, **own_bit),
            R.c3, step_of[two][1],
        )
    links["C.3"] = link(R.gc.at[b0, y, b1, 1 - b2], R.c4, dev2)

    def land_c3():
        R.ag_c[c, y] = R.gc[b0, y, b1, b2] + R.c4[...]

    lands["C.3"] = land_c3
    links["Ps"] = link(R.gps, R.gp.at[:, :, :, c], core_dev)
    most, last = pl.ds(0, pairs), pl.ds(pairs, 1)
    for name, mine, both in (
        ("agE", R.ag_e.at[c, y], R.ag_e.at[c]),
        ("agC", R.ag_c.at[c, y], R.ag_c.at[c]),
        ("agP", R.ag_m.at[c, y, most], R.ag_m.at[c, :, most]),
        ("agM", R.ag_m.at[c, y, last], R.ag_m.at[c, :, last]),
    ):
        links[name] = link(mine, mine, y_dev)
        links[name + "c"] = link(both, both, core_dev)

    chip = b0 * 8 + b2 * 4 + b1 * 2 + y

    def land_total(part, recv, every):
        def run():
            every[c, chip] = part[c] + recv[...]

        return run

    for name, part, recv, every in (("ga", R.va, R.va_r, R.all_a), ("gb", R.vb, R.vb_r, R.all_b)):
        links[name + "C"] = link(part.at[1 - c], recv, core_dev)
        lands[name + "C"] = land_total(part, recv, every)
        for t, dev in enumerate((y_dev, dev1, dev2, dev0)):
            size = 2**t
            ref = every.at[c, pl.ds(lax.div(chip, size) * size, size)]
            links[f"{name}{t}"] = link(ref, ref, dev)
        links[name + "F"] = link(every.at[c], every.at[c], core_dev)

    sequence = [name for _, landed in SCHEDULE for name in landed]
    follow = {"C0s": "C0.0", "C1s": "C1.0", "Ps": "P.0", "C.2": "C.3", "C.3": "agC"}
    for name in ("agE", "agC", "agP", "agM"):
        follow[name] = name + "c"
    for name in ("ga", "gb"):
        for one, two in zip("C0123", "0123F"):
            follow[name + one] = name + two
    for name in sums:
        for t in range(3):
            follow[f"{name}.{t}"] = f"{name}.{t + 1}"
    if len(plan_c) == 2:
        follow.update({"C0.0": "C0.1", "C1.0": "C1.1"})
        joined = [(("C0.1", "C1.1"), "C.2")]
    else:
        follow["C.1"] = "C.2"
        joined = [(("C0.0", "C1.0"), "C.1")]
    joined += [(("E0.3", "E1.3"), "agE"), (("P.3", "M0.3", "M1.3"), "agP"), (("M2.3",), "agM")]
    for names_in, name in joined:
        follow[max(names_in, key=sequence.index)] = name

    def serve(name):
        links[name].wait_recv()
        if name in lands:
            lands[name]()
        if name in follow:
            links[follow[name]].start()

    def service(point):
        for name in dict(SCHEDULE).get(point, ()):
            if name == "out":
                continue
            serve(name)

    def add_row(ref, r, value):
        for n in range(2):
            ref[n, pl.ds(r, 1), :] += value[:, n * half : (n + 1) * half]

    pl.semaphore_wait(barrier, 5)
    tok_swap.start()
    for item in (cot_load, proj_load, exp_load, con_load):
        item.start()
    R.va[...] = jnp.zeros_like(R.va)
    R.vb[...] = jnp.zeros_like(R.vb)

    adap_load.wait()
    for item in first_loads:
        item.wait()
    crow = jnp.where(y == 0, R.cond[0:1, :], R.cond[1:2, :])
    crow = crow * (1.0 / (1.0 + jnp.exp(-crow)))
    extent = crow.shape[1]
    R.va[0, 10:11, :extent] = crow * (1 - c).astype(F32)
    eye = lax.broadcasted_iota(jnp.int32, (extent, extent), 0) == lax.broadcasted_iota(
        jnp.int32, (extent, extent), 1
    )
    ccol = jnp.sum(jnp.where(eye, jnp.broadcast_to(crow, (extent, extent)), 0.0), axis=1, keepdims=True)
    shifts = R.shifts[...].reshape(1, 6 * width)
    for n in range(6):
        part = pl.ds(n * width, width)
        R.mod[n : n + 1, :] = column_sum(R.adap[:, part].astype(F32) * ccol) + shifts[:, n * width : (n + 1) * width]
    pregain = R.prenorm[...].reshape(1, width)
    postgain = R.postnorm[...].reshape(1, width)

    def first_norm(j, t):
        normal, _ = normalize(R.tok[j].astype(F32))
        value = normal * (pregain * (1.0 + R.mod[1:2, :])) + R.mod[0:1, :]
        R.hid_a[rows_of(2 * j + c), :] = value.astype(BF16)
        hid_a_push[t].start()

    def project(p):
        place = rows_of(p)
        mixed = dot(R.hid_a[place, :], R.mix[...])
        cos_here = R.cosine[place, :]
        sin_here = R.sine[place, :]
        for j in range(pairs):
            base = j * 3 * PAIR
            query = mixed[:, base : base + PAIR]
            query = (query * cos_here + turn(query) * sin_here).astype(BF16) * jnp.asarray(
                HDIM ** (-0.5), BF16
            )
            R.qq[j, place, :] = query
            key = mixed[:, base + PAIR : base + 2 * PAIR]
            R.kk[j, place, :] = (key * cos_here + turn(key) * sin_here).astype(BF16)
            R.vv[j, place, :] = mixed[:, base + 2 * PAIR : base + 3 * PAIR].astype(BF16)

    tok_load.wait()
    first_norm(y, 0)
    for item in mix_loads:
        item.wait()
    project(2 * y + c)
    tok_swap.wait_recv()
    first_norm(1 - y, 1)
    hid_a_push[0].wait_recv()
    project(2 * y + 1 - c)
    project(2 * (1 - y) + c)
    hid_a_push[1].wait_recv()
    project(2 * (1 - y) + 1 - c)
    for j in range(pairs):
        R.q_t[j * PAIR : (j + 1) * PAIR, :] = R.qq[j].T

    cot_swap.start()
    def att_push(j, jj):
        lanes = pl.ds(pl.multiple_of(c * half + j * PAIR, PAIR), PAIR)
        return remote(
            R.att_s.at[j, other_place[jj], :], R.att.at[jj, :, lanes], att_base + 2 * j + jj, core_dev
        )

    lane_pair = lax.broadcasted_iota(jnp.int32, (span, PAIR), 1)
    lane_long = lax.broadcasted_iota(jnp.int32, (total, PAIR), 1)

    def in_head(lane, hh):
        return lane < HDIM if hh == 0 else lane >= HDIM

    def attend(j, carry):
        def score_of(hh, qb):
            query = R.qq[j, qb * span : (qb + 1) * span, :]
            query = jnp.where(in_head(lane_pair, hh), query, jnp.zeros_like(query))
            return dot(query, R.kk[j], ROWS_BY_ROWS)

        values = []
        for hh in range(2):
            there = R.vv[j]
            values.append(jnp.where(in_head(lane_long, hh), there, jnp.ones_like(there)))
        steps = [(hh, qb) for hh in range(2) for qb in range(blocks)]
        score = score_of(*steps[0])
        for index, (hh, qb) in enumerate(steps):
            following = score_of(*steps[index + 1]) if index + 1 < len(steps) else None
            place = slice(qb * span, (qb + 1) * span)
            top = jnp.max(score, axis=1, keepdims=True)
            low = jnp.exp(score - top).astype(BF16)
            grown = dot(low, values[hh])
            totals = pltpu.roll(grown, HDIM, 1)
            grown = (grown / totals).astype(BF16)
            weight = top + jnp.log(totals)
            if hh == 0:
                R.att_s[j, place, :] = grown
                R.lse[j, place, :] = weight
            else:
                R.att_s[j, place, :] = jnp.where(lane_pair < HDIM, R.att_s[j, place, :], grown)
                R.lse[j, place, :] = jnp.where(lane_pair < HDIM, R.lse[j, place, :], weight)
            score = following
        lanes = pl.ds(pl.multiple_of(c * half + j * PAIR, PAIR), PAIR)
        for jj in range(2):
            att_push(j, jj).start()
            R.att[jj, :, lanes] = R.att_s[j, own_place[jj], :]
        return carry

    lax.fori_loop(0, pairs, attend, 0)
    cot_load.wait()
    cot_swap.wait_recv()
    for j in range(2):
        low = (R.cot[j].astype(F32) * R.mod[5:6, :]).astype(BF16)
        R.gnar[own_place[j], :] = low
        add_row(R.va, 5, column_sum(low.astype(F32)))
        gnar_push[j].start()

    for j in range(pairs):
        for jj in range(2):
            att_push(j, jj).wait_recv()

    proj_load.wait()
    for j in range(2):
        grown = dot(R.att[j], R.proj[...])
        R.branch[j] = grown.astype(BF16)
        value = R.tok[j].astype(F32) + R.mod[2:3, :] * grown
        R.middle[j] = value
        normal, _ = normalize(value)
        R.hid_f[own_place[j], :] = (normal * (postgain * (1.0 + R.mod[4:5, :])) + R.mod[3:4, :]).astype(BF16)
        hid_f_push[j].start()

    def bits_of(n, order):
        bits = dict(q=n // 8, z=n // 4 % 2, x=n // 2 % 2, y=n % 2)
        return tuple(bits[key] for key in order)

    exp_load.wait()
    con_load.wait()
    offsets = R.offsets[...].reshape(1, 4 * ub)
    offsets = jnp.where(c == 0, offsets[:, : 2 * ub], offsets[:, 2 * ub :])
    for i in range(2):
        units = pl.ds(i * ub, ub)

        def feed(t, carry, i=i, units=units):
            late = lax.div(t, 2)
            j = lax.rem(t, 2)
            place = rows_of(2 * j + lax.rem(c + late + i, 2))
            if i == 0:
                @pl.when(late == 1)
                def _():
                    remote(R.hid_f.at[place, :], R.hid_f.at[place, :], hid_f_base + j, core_dev).wait_recv()
                    remote(R.gnar.at[place, :], R.gnar.at[place, :], gnar_base + j, core_dev).wait_recv()
            else:
                for k in range(1, 4):
                    if f"f{k - 1}" in dict(SCHEDULE):
                        @pl.when(t == k)
                        def _(k=k):
                            service(f"f{k - 1}")
            v = dot(R.hid_f[place, :], R.exp[:, units]) + offsets[:, i * ub : (i + 1) * ub]
            square = v * v
            th = jnp.tanh(v * (GELU_A + (GELU_A * GELU_B) * square))
            up = 0.5 + 0.5 * th
            low = (v * up).astype(BF16)
            R.act[place, :] = low
            slope = up + (v * (0.5 - 0.5 * th * th)) * (GELU_A + (3.0 * GELU_A * GELU_B) * square)
            grad = (dot(R.gnar[place, :], R.con[units, :], ROWS_BY_ROWS) * slope).astype(BF16)
            R.gwid[place, :] = grad
            add_row(R.va, 6 + 2 * c + i, column_sum(grad.astype(F32)))
            n_part = dot(low, R.con[units, :])
            h_part = dot(grad, R.exp[:, units], ROWS_BY_ROWS)
            if i == 0:
                R.nacc[place, :] = n_part
                R.hacc[place, :] = h_part
            else:
                R.nacc[place, :] += n_part
                R.hacc[place, :] += h_part

                @pl.when(late == 0)
                def _():
                    R.hsend[j] = R.hacc[place, :].astype(BF16)
                    remote(R.hsend.at[j], R.hrecv.at[j], hsum_base + j, core_dev).start()
                    R.nsend[j] = R.nacc[place, :].astype(BF16)
                    remote(R.nsend.at[j], R.nrecv.at[j], nsum_base + j, core_dev).start()
            return carry

        lax.fori_loop(0, 4, feed, 0)
        if i == 1:
            for item in hsum_push + nsum_push:
                item.open = True
        value = dot(R.hid_f[...], R.gwid[...], COLS_BY_COLS).astype(BF16)
        for n in range(16):
            R.ge[(i,) + bits_of(n, ORDERS[f"E{i}"])] = value[n * strip : (n + 1) * strip]
        links[f"E{i}.0"].start()
        service(f"E{i}")
        value = dot(R.act[...], R.gnar[...], COLS_BY_COLS).astype(BF16)
        left, right = value[:, :half], value[:, half:]
        mine = jnp.where(c == 0, left, right)
        theirs = jnp.where(c == 0, right, left)
        if i == 1:
            service("f3")
            links["C0s"].wait_send()
        for n in range(4):
            a0, ay = n // 2, n % 2
            R.gcs[a0, ay] = theirs[n * block : (n + 1) * block]
            R.gc[a0, ay, i, c] = mine[n * block : (n + 1) * block]
        links[f"C{i}s"].start()
        service(f"C{i}")

    base_row = R.baseline[...].reshape(1, width)
    for j in range(2):
        place = own_place[j]
        hsum_push[j].wait_recv()
        got = R.hacc[place, :] + R.hrecv[j].astype(F32)
        normal, scale = normalize(R.middle[j])
        add_row(R.va, 1, column_sum(got))
        both = column_sum(got * normal)
        add_row(R.va, 2, both * postgain)
        add_row(R.va, 4, both * (1.0 + R.mod[4:5, :]))
        g = R.cot[j].astype(F32)
        nsum_push[j].wait_recv()
        narrowed = R.nacc[place, :] + R.nrecv[j].astype(F32) + base_row
        R.gwid[j * span : (j + 1) * span, :] = (R.middle[j] + R.mod[5:6, :] * narrowed).astype(BF16)
        add_row(R.va, 3, column_sum(g * narrowed))
        value = g + normalize_back(got * (postgain * (1.0 + R.mod[4:5, :])), normal, scale)
        R.middle[j] = value
        add_row(R.va, 0, column_sum(value * R.branch[j].astype(F32)))
        R.gbr[place, :] = (R.mod[2:3, :] * value).astype(BF16)
        gbr_push[j].start()
        if j == 0:
            service("n0")

    out_local = local(stage(0, y), R.out_h.at[y])
    out_local.start()
    links["gaC"].start()
    out_at = ORDERS["out"]
    if out_at == "n1":
        out_push.start()
    service("n1")
    for j in range(2):
        gbr_push[j].wait_recv()

    value = jnp.concatenate(
        [dot(R.att_s[j], R.gbr[...], COLS_BY_COLS).astype(BF16) for j in range(pairs)], axis=0
    )
    left, right = value[:, :half], value[:, half:]
    mine = jnp.where(c == 0, left, right)
    theirs = jnp.where(c == 0, right, left)
    for n in range(8):
        place = bits_of(n, ORDERS["P"][:3])
        R.gps[place] = theirs[n * strip : (n + 1) * strip]
        R.gp[place + (c,)] = mine[n * strip : (n + 1) * strip]
    links["Ps"].start()
    own_proj = R.proj[pl.ds(pl.multiple_of(c * half, PAIR), half), :]
    grown = dot(R.gbr[...], own_proj, ROWS_BY_ROWS).astype(BF16)
    for j in range(pairs):
        R.act[:, half + j * PAIR : half + (j + 1) * PAIR] = grown[:, j * PAIR : (j + 1) * PAIR]

    if out_at == "gp":
        out_push.start()
    service("gp")


    def service_pair(j, point):
        for k in range(pairs):
            key = f"b{k}{point}"
            if key == out_at or key in dict(SCHEDULE):
                @pl.when(j == k)
                def _(key=key):
                    if key == out_at:
                        out_push.start()
                    service(key)

    def attend_back(j, carry):
        grown = R.act[:, pl.ds(pl.multiple_of(half + j * PAIR, PAIR), PAIR)].astype(F32)
        product = grown * R.att_s[j].astype(F32)
        inner = [
            jnp.sum(jnp.where(in_head(lane_long, hh), product, 0.0), axis=1, keepdims=True) for hh in range(2)
        ]
        R.dsum[...] = jnp.where(in_head(lane_long, 0), inner[0], inner[1])
        R.dom_t[...] = grown.astype(BF16).T

        lanes = pl.ds(pl.multiple_of(half + j * PAIR, PAIR), PAIR)

        def one_head(value, hh):
            return jnp.where(in_head(lane_pair, hh), value, jnp.zeros_like(value))

        def products(hh, qb):
            rows = slice(qb * span, (qb + 1) * span)
            grad = dot(one_head(R.act[rows, lanes], hh), R.vv[j], ROWS_BY_ROWS)
            return grad, dot(one_head(R.qq[j, rows, :], hh), R.kk[j], ROWS_BY_ROWS)

        steps = [(hh, qb) for hh in range(2) for qb in range(blocks)]
        current = products(*steps[0])
        for index, (hh, qb) in enumerate(steps):
            following = products(*steps[index + 1]) if index + 1 < len(steps) else None
            grad, score = current
            place = slice(qb * span, (qb + 1) * span)
            rows = slice(hh * HDIM, (hh + 1) * HDIM)
            first = hh * HDIM
            weight = jnp.exp(score - R.lse[j, place, first : first + 1])
            low = weight.astype(BF16)
            grad = (weight * (grad - R.dsum[place, first : first + 1])).astype(BF16)
            q_part = dot(grad, R.kk[j])
            v_part = dot(R.dom_t[rows, place], low)
            k_part = dot(R.q_t[pl.ds(pl.multiple_of(j * PAIR + hh * HDIM, HDIM), HDIM), place], grad)
            if hh == 0:
                R.dq[place, :] = q_part
            else:
                R.dq[place, :] = jnp.where(lane_pair < HDIM, R.dq[place, :], q_part)
            if qb == 0:
                R.dv_t[rows, :] = v_part
                R.dk_t[rows, :] = k_part
            else:
                R.dv_t[rows, :] += v_part
                R.dk_t[rows, :] += k_part
            if qb == blocks - 1:
                service_pair(j, hh)
            current = following
        gq = R.dq[...] * HDIM ** (-0.5)
        gk = R.dk_t[...].T
        gmx = R.act.at[:, pl.ds(0, 3 * PAIR)]
        gmx[:, :PAIR] = (gq * R.cosine[...] - turn(gq) * R.sine[...]).astype(BF16)
        gmx[:, PAIR : 2 * PAIR] = (gk * R.cosine[...] - turn(gk) * R.sine[...]).astype(BF16)
        gmx[:, 2 * PAIR :] = R.dv_t[...].astype(BF16).T
        value = dot(R.hid_a[...], gmx[...], COLS_BY_COLS).astype(BF16)
        for k in range(pairs):
            @pl.when(j == k)
            def _(k=k):
                for n in range(16):
                    index = 0
                    for bit in bits_of(n, ORDERS[f"M{k}"]):
                        index = 2 * index + bit
                    R.exp[index * strip : (index + 1) * strip, k * half : (k + 1) * half] = value[
                        n * strip : (n + 1) * strip
                    ]
                links[f"M{k}.0"].start()
        service_pair(j, 2)
        lanes = pl.ds(pl.multiple_of(j * 3 * PAIR, PAIR), 3 * PAIR)

        def back(p, inner):
            place = rows_of(p)
            part = dot(gmx[place, :], R.mix[:, lanes], ROWS_BY_ROWS)

            @pl.when(j == 0)
            def _():
                R.hacc[place, :] = part

            @pl.when(j > 0)
            def _():
                R.hacc[place, :] += part

            return inner

        lax.fori_loop(0, blocks, back, 0)
        service_pair(j, 3)
        return carry

    lax.fori_loop(0, pairs, attend_back, 0)
    for j in range(2):
        hsum_push[j].wait_send()
        R.hsend[j] = R.hacc[other_place[j], :].astype(BF16)
        asum_push[j].start()

    gtok_local = local(stage(1, y), R.gtok_h.at[y])
    for j, item in ((1 - y, gtok_push), (y, gtok_local)):
        got = R.hacc[rows_of(2 * j + c), :] + 0.0
        if item is gtok_push:
            asum_push[0].wait_recv()
            asum_push[1].wait_recv()
        got = got + R.hrecv[j].astype(F32)
        normal, scale = normalize(R.tok[j].astype(F32))
        add_row(R.vb, 0, column_sum(got))
        both = column_sum(got * normal)
        add_row(R.vb, 1, both * pregain)
        add_row(R.vb, 2, both * (1.0 + R.mod[1:2, :]))
        stage(1, j)[...] = (
            R.middle[j] + normalize_back(got * (pregain * (1.0 + R.mod[1:2, :])), normal, scale)
        ).astype(BF16)
        item.start()
        if item is gtok_push:
            if out_at == "l0":
                out_push.start()
            service("l0")
    links["gbC"].start()
    service("l1")
    service("l2")

    stores = []

    def store(src, dst):
        item = local(src, dst)
        item.start()
        stores.append(item)

    def store_e():
        for n in range(8):
            cc, yy, i = n // 4, n // 2 % 2, n % 2
            store(
                R.ag_e.at[cc, yy, i],
                R.oe_h.at[pl.ds(yy * strip, strip), pl.ds((2 * cc + i) * width, width)],
            )

    def store_c():
        for n in range(4):
            cc, yy = n // 2, n % 2
            store(R.ag_c.at[cc, yy], R.oc_h.at[pl.ds(yy * block, block), pl.ds(cc * half, half)])

    def place_m(j):
        for n in range(4):
            cc, yy = n // 2, n % 2
            value = R.ag_m[cc, yy, 1 + j]
            for b in range(3):
                lane = cc * half + j * PAIR
                row = (2 * b + yy) * strip
                R.hid_f[row : row + strip, lane : lane + PAIR] = value[:, b * PAIR : (b + 1) * PAIR]

    def store_p():
        for n in range(4):
            cc, yy = n // 2, n % 2
            store(R.ag_m.at[cc, yy, 0], R.op_h.at[pl.ds(yy * strip, strip), pl.ds(cc * half, half)])
        for item in hid_f_push:
            item.open = True
            item.wait_send()
        for j in range(pairs - 1):
            place_m(j)

    def store_m():
        place_m(pairs - 1)
        for b in range(3):
            store(R.hid_f.at[pl.ds(2 * b * strip, 2 * strip), :], R.om_h.at[:, pl.ds(b * width, width)])

    results = {"agEc": store_e, "agCc": store_c, "agPc": store_p, "agMc": store_m}
    if leftover == 1:
        early, later = finish_vectors(R, hi, chip - y, width, half, extent)
    else:
        early = [lambda: store(R.all_a, R.all_a_h)]
        later = [lambda: store(R.all_b, R.all_b_h)]
    pieces = []
    tail = dict(SCHEDULE)["tail"]
    if "gaF" not in tail:
        pieces.extend(early)
    for name in tail:
        serve(name)
        if name in results:
            results[name]()
        if name == "gaF":
            pieces.extend(early)
        if name == "gbF":
            pieces.extend(later)
        if pieces:
            pieces.pop(0)()
    for piece in pieces:
        piece()
    for item in stores:
        item.wait()
    out_local.wait()
    out_push.wait_recv()
    gtok_local.wait()
    gtok_push.wait_recv()
    for j in range(pairs):
        for jj in range(2):
            att_push(j, jj).wait_send()
    for item in sent:
        if item.open:
            item.wait_send()


def finish_vectors(R, hi, chip, width, half, extent):
    own = extent // 8
    highest = lax.Precision.HIGHEST
    sections = ((R.all_b, 0), (R.all_b, 1), (R.all_a, 0), (R.all_a, 1), (R.all_a, 2), (R.all_a, 3))

    def transpose():
        R.st[...] = R.all_a[0, :, 10, :extent].T
        R.back[...] = jnp.zeros_like(R.back)

    def section(n, h):
        ref, r = sections[n]
        grads = ref[h, :, r, :]
        lanes = pl.ds(n * width + h * half, half)
        silu_own = R.st[pl.ds(pl.multiple_of(hi * own, own), own), :]
        R.adaptive_o[:, lanes] = jnp.dot(silu_own, grads, precision=highest, preferred_element_type=F32)
        R.total[:, lanes] = column_sum(grads)
        table = R.adap[:, lanes].astype(F32)
        for yy in range(2):
            mine = ref[h, pl.ds(chip + yy, 1), r, :]
            R.back[:, yy : yy + 1] += jnp.sum(table * mine, axis=1, keepdims=True)

    def share(vector, out):
        size = vector.shape[1] // 8
        value = jnp.zeros((1, size), F32)
        for k in range(8):
            value = jnp.where(hi == k, vector[:, k * size : (k + 1) * size], value)
        out[...] = value.reshape(size)

    def total_of(ref, r):
        return jnp.concatenate([column_sum(ref[h, :, r, :]) for h in range(2)], axis=1)

    def vectors():
        share(total_of(R.all_a, 4), R.postnorm_o)
        share(jnp.concatenate([total_of(R.all_a, 6 + n) for n in range(4)], axis=1), R.offsets_o)
        share(total_of(R.all_a, 5), R.baseline_o)

    def last():
        share(total_of(R.all_b, 2), R.prenorm_o)
        share(R.total[...], R.shifts_o)
        eye = lax.broadcasted_iota(jnp.int32, (extent, extent), 0) == lax.broadcasted_iota(
            jnp.int32, (extent, extent), 1
        )
        for yy in range(2):
            back = jnp.broadcast_to(R.back[:, yy : yy + 1], (extent, extent))
            row = column_sum(jnp.where(eye, back, 0.0))
            cond = R.cond[yy : yy + 1, :]
            gate = 1.0 / (1.0 + jnp.exp(-cond))
            R.time_o[yy : yy + 1, :] = row * (gate * (1.0 + cond * (1.0 - gate)))

    early = [transpose] + [functools.partial(section, n, h) for n in range(2, 6) for h in range(2)] + [vectors]
    later = [functools.partial(section, n, h) for n in range(2) for h in range(2)] + [last]
    return early, later


def finish_kernel(count, *refs):
    total = 4 + count
    given, results, held, high, sem = (
        refs[:total], refs[total : 2 * total], refs[2 * total : 3 * total], refs[3 * total : 3 * total + 4], refs[-1]
    )
    loads = [pltpu.make_async_copy(a, b, sem.at[n]) for n, (a, b) in enumerate(zip(given, held))]
    written = tuple(high) + tuple(held[4:])
    stores = [pltpu.make_async_copy(a, b, sem.at[total + n]) for n, (a, b) in enumerate(zip(written, results))]
    for n in (0, 4, 1, 5, 3, 2, *range(6, total)):
        loads[n].start()
    for n in (0, 4, 1, 5, 3, 2, *range(6, total)):
        loads[n].wait()
        if n < 4:
            high[n][...] = held[n][...].astype(F32)
        stores[n].start()
    for item in stores:
        item.wait()


def finish(sums, others):
    hbm = pl.BlockSpec(memory_space=pl.ANY)
    shape = jax.ShapeDtypeStruct
    return pl.pallas_call(
        functools.partial(finish_kernel, len(others)),
        out_shape=tuple(shape(v.shape, F32) for v in sums) + tuple(shape(v.shape, v.dtype) for v in others),
        in_specs=[hbm] * (4 + len(others)),
        out_specs=(hbm,) * (4 + len(others)),
        scratch_shapes=[pltpu.VMEM(v.shape, v.dtype) for v in (*sums, *others)]
        + [pltpu.VMEM(v.shape, F32) for v in sums] + [pltpu.SemaphoreType.DMA((8 + 2 * len(others),))],
        compiler_params=pltpu.CompilerParams(vmem_limit_bytes=60 * 1024 * 1024),
        name="finish",
    )(*sums, *others)


def rotary_constants(length):
    half_dim = HDIM // 2
    frequency = np.exp(np.arange(half_dim, dtype=np.float32) * np.float32(-2.0 * math.log(10000.0) / HDIM))
    angles = np.arange(length, dtype=np.float32)[:, None] * frequency[None, :].astype(np.float32)
    angles = angles.astype(np.float64)
    cosine = np.cos(angles).astype(np.float32)
    sine = np.sin(angles).astype(np.float32)
    cosine = np.concatenate([cosine] * 4, axis=-1)
    sine = np.concatenate([-sine, sine, -sine, sine], axis=-1)
    return cosine, sine


def local_part(wide_count, tokens, condition, cotangent, adaptive, shifts, prenorm, mixer, projection, postnorm,
               expand, offsets, contract, baseline):
    rows, span, width = tokens.shape
    total = 4 * span
    half = width // 2
    pairs = half // PAIR
    ff = expand.shape[1]
    extent = adaptive.shape[0]
    leftover = wide_count // 8
    cosine, sine = rotary_constants(total)
    hbm = pl.BlockSpec(memory_space=pl.ANY)
    vmem = pl.BlockSpec(memory_space=pltpu.VMEM)
    shape = jax.ShapeDtypeStruct
    out_shape = [
        shape(tokens.shape, BF16), shape(tokens.shape, BF16), shape((width // 8, ff), BF16),
        shape((ff // 8, width), BF16), shape((width // 8, width), BF16), shape((width // 8, 3 * width), BF16),
    ]
    out_specs = [hbm] * len(out_shape)
    names = INPUTS + GRADS
    if leftover == 1:
        names += FINALS
        out_shape += [
            shape(condition.shape, F32), shape((extent // 8, 6 * width), F32), shape((6 * width // 8,), F32),
            shape((width // 8,), F32), shape((width // 8,), F32), shape((ff // 8,), F32), shape((width // 8,), F32),
        ]
        out_specs += [vmem] * len(FINALS)
    else:
        names += PARTIALS
        out_shape += [shape((2, 16, 16, half), F32), shape((2, 16, 8, half), F32)]
        out_specs += [hbm] * len(PARTIALS)
    buffers = kernel_buffers(span, width, extent, ff)
    names += tuple(buffers)
    outs = pl.pallas_call(
        functools.partial(layer_kernel, leftover, names),
        out_shape=tuple(out_shape),
        in_specs=[hbm] * 15,
        out_specs=tuple(out_specs),
        scratch_shapes=list(buffers.values()),
        compiler_params=pltpu.CompilerParams(
            collective_id=0, has_side_effects=True, vmem_limit_bytes=64 * 1024 * 1024 - 65536
        ),
        name="layer",
    )(
        tokens, cotangent, adaptive, mixer, projection, expand, contract,
        condition, shifts, prenorm, postnorm, offsets, baseline, jnp.asarray(cosine), jnp.asarray(sine),
    )
    layer_output, grad_tokens = outs[0], outs[1]
    if leftover == 1:
        done = finish(outs[2:6], outs[:2] + outs[6:])
        grad_expand, grad_contract, grad_projection, grad_mixer = done[:4]
        layer_output, grad_tokens = done[4:6]
        grad_time, grad_adaptive, grad_shifts, grad_prenorm, grad_postnorm, grad_offsets, grad_baseline = done[6:]
        return (
            layer_output, grad_tokens, grad_time, grad_adaptive, grad_shifts, grad_prenorm, grad_mixer,
            grad_projection, grad_postnorm, grad_expand, grad_offsets, grad_contract, grad_baseline,
        )

    grad_expand, grad_contract, grad_projection, grad_mixer = (part.astype(F32) for part in outs[2:6])

    w = lax.axis_index("wide")

    def among_groups(part):
        size = part.shape[0]
        whole = jnp.zeros((8 * size,) + part.shape[1:], F32)
        whole = lax.dynamic_update_slice_in_dim(whole, part, lax.div(w, leftover) * size, axis=0)
        return lax.psum_scatter(whole, "wide", scatter_dimension=0, tiled=True)

    grad_expand, grad_contract, grad_projection, grad_mixer = (
        among_groups(part) for part in (grad_expand, grad_contract, grad_projection, grad_mixer)
    )
    all_a, all_b = outs[6], outs[7]
    every = jnp.concatenate([all_b, all_a], axis=2)
    every = every.reshape(2, 2, 2, 2, 2, 24, half).transpose(2, 3, 1, 4, 5, 0, 6).reshape(8, 2, 24, width)
    mine = lax.dynamic_slice_in_dim(every, lax.div(w, leftover), 1, axis=0)[0]
    every = lax.all_gather(mine, "wide", axis=0, tiled=True)
    sections = [0, 1, 8, 9, 10, 11]
    grad_mod = jnp.concatenate([every[:, r] for r in sections], axis=-1)
    silu_all = every[:, 18, :extent]
    highest = lax.Precision.HIGHEST
    own_rows = extent // wide_count
    grad_adaptive = jnp.dot(
        lax.dynamic_slice_in_dim(silu_all, w * own_rows, own_rows, axis=1).T, grad_mod, precision=highest
    )
    sums = jnp.sum(every, axis=0)

    def own(vector):
        size = vector.shape[0] // wide_count
        return lax.dynamic_slice_in_dim(vector, w * size, size)

    here = lax.dynamic_slice_in_dim(grad_mod, w * rows, rows, axis=0)
    _, silu_back = jax.vjp(jax.nn.silu, condition)
    (grad_time,) = silu_back(jnp.dot(here, adaptive.astype(F32).T, precision=highest))
    return (
        layer_output, grad_tokens, grad_time, grad_adaptive, own(jnp.sum(grad_mod, axis=0)), own(sums[2]),
        grad_mixer, grad_projection, own(sums[12]), grad_expand, own(sums[14:18].reshape(-1)), grad_contract,
        own(sums[13]),
    )


def solution(mesh):
    rows = P("wide", "seq", None)
    by_wide = P("wide", None)
    in_specs = (rows, by_wide, rows) + (P(),) * 10
    out_specs = (
        rows, rows, by_wide, by_wide, P("wide"), P("wide"), by_wide, by_wide, P("wide"), by_wide, P("wide"),
        by_wide, P("wide"),
    )
    return jax.shard_map(
        functools.partial(local_part, mesh.shape["wide"]),
        mesh=mesh, in_specs=in_specs, out_specs=out_specs, check_vma=False,
    )
```
